32 devices in a mesh: prow: 8 (over y, x, core), pcol: 4 (over z).
Axes of the slice: x: 2, y: 2, z: 4, core: 2. Of those that a mesh axis runs over, the one named last changes fastest.
Arguments:
- packed: bfloat16 [6144, 6144], P('prow', 'pcol'), may hold values from -32 to 32, as said below
- tile_scales: float32 [24, 24], P('prow', 'pcol'), may hold values from 0.5 to 2
Outputs:
- factored: bfloat16 [6144, 6144], P('prow', 'pcol')
The draws below stay inside these ranges and needn't reach their ends.
Inputs may be any that keep to these rules, and one draw needn't show every extreme that they name: `packed`: stored tile entries lie in the range below.
All inputs are finite; a program needn't handle non-finite values.
Results may differ from the reference program's by a relative error of at most 0.0065.
Values may be sent and summed in bfloat16 or wider, within the bound.
No kernel may reach another device: no remote copies, remote signals or barrier semaphores. Data moves between devices by JAX's collectives and lax.ppermute only.
A program may use at most 64 MiB of HBM per device.

```python
import jax
import jax.numpy as jnp
import numpy as np
from jax import lax

NB = 256
TPR = 3
TILES = 24
TPC = 6
N_PROW = 8
N_PCOL = 4


def scale_table(key):
    uniform_draw = jax.random.uniform(jax.random.fold_in(key, 11), (TILES, TILES), jnp.float32)
    return jnp.exp(jnp.log(0.5) + uniform_draw * jnp.log(4.0))


def draw_tile_scales(key, part):
    return scale_table(key)


def leading_block(key):
    block_span = 2 * NB
    edge_bound = 0.8 / (NB - 1)
    diagonal = jax.random.uniform(jax.random.fold_in(key, 12), (block_span,), jnp.float32, 1.0, 1.5)
    inside = jax.random.uniform(jax.random.fold_in(key, 13), (block_span, block_span), jnp.float32, -edge_bound, edge_bound)
    coupling = jax.random.uniform(jax.random.fold_in(key, 14), (block_span, block_span), jnp.float32, -0.2, 0.2)
    row_index = lax.broadcasted_iota(jnp.int32, (block_span, block_span), 0)
    col_index = lax.broadcasted_iota(jnp.int32, (block_span, block_span), 1)
    cross = (row_index >= NB) & (col_index < NB)
    strict = (col_index < row_index) & jnp.logical_not(cross)
    factor = jnp.where(cross, coupling, jnp.where(strict, inside, 0.0)) + jnp.diag(diagonal)
    return jnp.dot(factor, factor.T, precision=lax.Precision.HIGHEST)


def draw_packed(key, part):
    scales = scale_table(key)
    order_size = TILES * NB
    noise_draw = jnp.clip(jax.random.normal(jax.random.fold_in(key, 15), (order_size, order_size), jnp.float32), -6.0, 6.0)
    col_block = lax.broadcasted_iota(jnp.int32, (1, order_size), 1) // NB
    panel_cols = (col_block == 0) | (col_block == TPC)
    entries = noise_draw * jnp.where(panel_cols, 0.2, 1.0)
    leading = leading_block(key)
    first_rows = TPR * NB
    second_cols = TPC * NB
    entries = entries.at[0:NB, 0:NB].set(leading[:NB, :NB] / scales[0, 0])
    entries = entries.at[first_rows:first_rows + NB, 0:NB].set(leading[NB:, :NB] / scales[TPR, 0])
    entries = entries.at[first_rows:first_rows + NB, second_cols:second_cols + NB].set(leading[NB:, NB:] / scales[TPR, TPC])
    entries = entries.at[0:NB, second_cols:second_cols + NB].set(leading[:NB, NB:] / scales[0, TPC])
    return entries.astype(jnp.bfloat16)


def setup_inputs(seed: int = 0) -> dict:
    splits = jax.random.split(jax.random.key(seed), 3)
    packed = draw_packed(jax.random.fold_in(splits[2], 71), 0)
    tile_scales = draw_tile_scales(jax.random.fold_in(splits[2], 71), 0)
    return dict(packed=packed, tile_scales=tile_scales)


def storage_maps():
    blocks = np.arange(TILES)
    row_true = blocks % TPR * N_PROW + blocks // TPR
    col_true = blocks % TPC * N_PCOL + blocks // TPC
    place_of = col_true % N_PROW * TPR + col_true // N_PROW
    return (row_true, col_true, place_of)

def factor_column(column_tiles, panel_index, row_true, pivot_block):
    lower_factor = jnp.linalg.cholesky(column_tiles[pivot_block])
    flat_rows = column_tiles.reshape(-1, NB)
    solved = jax.scipy.linalg.solve_triangular(lower_factor, flat_rows.T, lower=True).T
    solved = solved.reshape(column_tiles.shape)
    below_mask = (row_true > panel_index)[:, None, None]
    pivot_mask = (row_true == panel_index)[:, None, None]
    factors = jnp.where(below_mask, solved, jnp.where(pivot_mask, lower_factor[None], 0.0))
    row_panel = jnp.where(below_mask, solved, 0.0).astype(jnp.bfloat16)
    return (factors, row_panel)

def reference(packed, tile_scales):
    row_true_np, col_true_np, place_np = storage_maps()
    row_true = jnp.asarray(row_true_np.astype(np.int32))
    col_true = jnp.asarray(col_true_np.astype(np.int32))
    place_of = jnp.asarray(place_np.astype(np.int32))

    def column_values(block):
        tiles = packed[:, block * NB:(block + 1) * NB].reshape(TILES, NB, NB).astype(jnp.float32)
        return tiles * tile_scales[:, block][:, None, None]
    first_factors, first_panel = factor_column(column_values(0), 0, row_true, 0)
    second_row = first_panel[TPR].astype(jnp.float32)
    second_values = column_values(TPC) - jnp.einsum('anx,mx->anm', first_panel.astype(jnp.float32), second_row)
    second_factors, second_panel = factor_column(second_values, 1, row_true, TPR)
    first_cols = first_panel[place_of].astype(jnp.float32)
    second_cols = second_panel[place_of].astype(jnp.float32)

    def one_block(block_row):
        rows = lax.dynamic_slice_in_dim(packed, block_row * NB, NB, 0)
        stored = rows.reshape(NB, TILES, NB)
        scales = tile_scales[block_row]
        values = stored.astype(jnp.float32) * scales[None, :, None]
        update_one = jnp.einsum('nx,qmx->nqm', first_panel[block_row].astype(jnp.float32), first_cols)
        update_two = jnp.einsum('nx,qmx->nqm', second_panel[block_row].astype(jnp.float32), second_cols)
        current = values - update_one - update_two
        scaled = current / scales[None, :, None]
        scaled = scaled.at[:, 0, :].set(first_factors[block_row] / scales[0])
        scaled = scaled.at[:, TPC, :].set(second_factors[block_row] / scales[TPC])
        upper_mask = row_true[block_row] < col_true
        result = jnp.where(upper_mask[None, :, None], stored, scaled.astype(jnp.bfloat16))
        return result.reshape(NB, TILES * NB)
    blocks = lax.map(one_block, jnp.arange(TILES, dtype=jnp.int32))
    return blocks.reshape(TILES * NB, TILES * NB)
```

```python
import functools

import jax
import jax.numpy as jnp
from jax import lax
from jax.experimental import pallas as pl
from jax.experimental.pallas import tpu as pltpu
from jax.sharding import PartitionSpec as P

F32 = jnp.float32
BF16 = jnp.bfloat16
HALF = 128
EXTRA = 16


def dot_nt(a, b, precision=None):
    dims = (((1,), (1,)), ((), ()))
    return lax.dot_general(a, b, dims, precision=precision, preferred_element_type=F32)


def dot_nn(a, b, precision=None):
    dims = (((1,), (0,)), ((), ()))
    return lax.dot_general(a, b, dims, precision=precision, preferred_element_type=F32)


HIGHEST = lax.Precision.HIGHEST


def recip(x):
    r = pl.reciprocal(x, approx=True)
    return r * (2.0 - x * r)


def inverse_factor(a):
    n = a.shape[0]
    blocks = n // 8
    full = (8, n)
    rows = [a[8 * i : 8 * i + 8, :] for i in range(blocks)]
    lane = lax.broadcasted_iota(jnp.int32, full, 1)
    sub = lax.broadcasted_iota(jnp.int32, full, 0)
    eye = [jnp.where(lane == sub + 8 * i, 1.0, 0.0).astype(F32) for i in range(blocks)]
    out = []
    for t in range(blocks):
        b = [jnp.broadcast_to(rows[t][j : j + 1, :], full) for j in range(8)]
        g = [jnp.broadcast_to(eye[t][j : j + 1, :], full) for j in range(8)]
        s = {}
        for j in range(8):
            for k in range(j, 8):
                col = 8 * t + k
                s[j, k] = jnp.broadcast_to(b[j][:, col : col + 1], full)
        c = {}
        for i in range(t + 1, blocks):
            for j in range(8):
                col = 8 * t + j
                c[i, j] = jnp.broadcast_to(rows[i][:, col : col + 1], full)
        x = jnp.zeros(full, F32)
        for j in range(8):
            r = recip(s[j, j])
            m = {k: s[j, k] * r for k in range(j + 1, 8)}
            for k in range(j + 1, 8):
                for l in range(k, 8):
                    s[k, l] = s[k, l] - m[k] * s[j, l]
            for k in range(j + 1, 8):
                b[k] = b[k] - m[k] * b[j]
                g[k] = g[k] - m[k] * g[j]
            w = r * b[j]
            h = r * g[j]
            for i in range(t + 1, blocks):
                for k in range(j + 1, 8):
                    c[i, k] = c[i, k] - m[k] * c[i, j]
                rows[i] = rows[i] - c[i, j] * w
                eye[i] = eye[i] - c[i, j] * h
            x = jnp.where(sub == j, lax.rsqrt(s[j, j]) * g[j], x)
        out.append(x)
    return jnp.concatenate(out, axis=0)


def scale_row(ref, row):
    parts = ref[row : row + 16, :].astype(F32)
    return parts[0:1] + parts[1:2] + parts[2:3]


def factor_kernel(p00, p10, p11, x0_ref, x1_ref, panel_ref, diag, low, corner, low_factor, inv):
    n = x0_ref.shape[0]

    def stage(tile):
        diag[...] = tile[:HALF, :HALF]
        low[...] = tile[HALF:, :HALF]
        corner[...] = tile[HALF:, HALF:]

    def finish(out_ref):
        x11 = inv[0]
        x22 = inv[1]
        x21 = dot_nn(dot_nn(x22, low_factor[...], HIGHEST), x11, HIGHEST)
        out_ref[:HALF, :HALF] = x11
        out_ref[:HALF, HALF:] = jnp.zeros((HALF, HALF), F32)
        out_ref[HALF:, :HALF] = -x21
        out_ref[HALF:, HALF:] = x22

    stage(p00[:n, :].astype(F32) * scale_row(p00, n))

    def body(step, carry):
        x = inverse_factor(diag[...])
        inv[step % 2] = x

        @pl.when(step % 2 == 0)
        def _():
            factor = dot_nt(low[...], x, HIGHEST)
            low_factor[...] = factor
            diag[...] = corner[...] - dot_nt(factor, factor, HIGHEST)

        @pl.when(step == 1)
        def _():
            finish(x0_ref)
            solved = dot_nt(p10[:n, :].astype(F32), x0_ref[...], HIGHEST) * scale_row(p10, n)
            panel = solved.astype(BF16)
            panel_ref[...] = panel
            stage(p11[:n, :].astype(F32) * scale_row(p11, n) - dot_nt(panel, panel))

        @pl.when(step == 3)
        def _():
            finish(x1_ref)

        return carry

    lax.fori_loop(0, 4, body, 0)


def factor_pivots(p00, p10, p11):
    n = p00.shape[1]
    square = jax.ShapeDtypeStruct((n, n), F32)
    vmem = pl.BlockSpec(memory_space=pltpu.VMEM)
    return pl.pallas_call(
        factor_kernel,
        out_shape=(square, square, jax.ShapeDtypeStruct((n, n), BF16)),
        in_specs=[vmem] * 3,
        out_specs=(vmem,) * 3,
        scratch_shapes=[
            pltpu.VMEM((HALF, HALF), F32),
            pltpu.VMEM((HALF, HALF), F32),
            pltpu.VMEM((HALF, HALF), F32),
            pltpu.VMEM((HALF, HALF), F32),
            pltpu.VMEM((2, HALF, HALF), F32),
        ],
        compiler_params=pltpu.CompilerParams(vmem_limit_bytes=32 << 20),
        name="factor_pivots",
    )(p00, p10, p11)


def split(x):
    high = x.astype(BF16)
    return high, (x - high.astype(F32)).astype(BF16)


def update_kernel(
    geometry, pos, scales, packed, x0_ref, x1_ref, panel_ref, own, mine, *rest
):
    ratio, nr, nc, tpr, tpc, n, count = geometry
    arrived = rest[:count]
    out, block, rowp, colp, sem = rest[count:]
    step = pl.program_id(0)
    r = pos[0]
    c = pos[1]

    def solve(slot):
        x0h, x0l = split(x0_ref[...])
        x1h, x1l = split(x1_ref[...])
        pieces = []
        for t in range(tpr):
            a0 = block[slot, 0, t * n : (t + 1) * n, :]
            a1 = block[slot, 1, t * n : (t + 1) * n, :]
            tail0 = block[slot, 0, tpr * n :, :].astype(F32)
            tail1 = block[slot, 1, tpr * n :, :].astype(F32)
            s0 = tail0[3 * t : 3 * t + 1] + tail0[3 * t + 1 : 3 * t + 2] + tail0[3 * t + 2 : 3 * t + 3]
            s1 = tail1[3 * t : 3 * t + 1] + tail1[3 * t + 1 : 3 * t + 2] + tail1[3 * t + 2 : 3 * t + 3]
            f0 = (dot_nt(a0, x0h) + dot_nt(a0, x0l)) * s0
            p0 = f0.astype(BF16)
            low = a1.astype(F32) * s1 - dot_nt(p0, panel_ref[...])
            bh, bl = split(low)
            f1 = dot_nt(bh, x1h) + dot_nt(bl, x1h) + dot_nt(bh, x1l)
            pieces.append((f0, f1, p0, f1.astype(BF16)))
        return pieces

    @pl.when(step == 0)
    def _():
        copies = []
        for g in range(ratio):
            source = c + nc * g
            for mask in range(count // 2):
                for other in range(2):
                    ref = arrived[2 * mask + other]
                    hit = (r ^ source) == (2 * mask + other)

                    @pl.when(hit)
                    def _(ref=ref, g=g):
                        pltpu.make_async_copy(ref, block.at[g], sem.at[g]).start()

        pltpu.make_async_copy(mine, block.at[ratio], sem.at[ratio]).start()
        for g in range(ratio + 1):
            pltpu.make_async_copy(mine, block.at[g], sem.at[g]).wait()
        for g in range(ratio):
            for t, (_, _, p0, p1) in enumerate(solve(g)):
                q = t * ratio + g
                colp[q, :, :n] = p0
                colp[q, :, n:] = p1
        for t, (f0, f1, p0, p1) in enumerate(solve(ratio)):
            rowp[t, :, :n] = p0
            rowp[t, :, n:] = p1

    true_row = step * nr + r
    left = rowp[step]
    for q in range(tpc):
        true_col = q * nc + c
        cols = slice(q * n, (q + 1) * n)
        s = scales[step, q]

        @pl.when(true_row < true_col)
        def _(cols=cols):
            out[:, cols] = packed[:, cols]

        @pl.when(jnp.logical_and(true_row >= true_col, true_col >= 2))
        def _(cols=cols, s=s, q=q):
            change = dot_nt(left, colp[q])
            out[:, cols] = (packed[:, cols].astype(F32) - change * (1.0 / s)).astype(BF16)

        if q * nc < 2:

            @pl.when(jnp.logical_and(true_row >= true_col, true_col < 2))
            def _(cols=cols, s=s):
                row = lax.broadcasted_iota(jnp.int32, (n, n), 0)
                col = lax.broadcasted_iota(jnp.int32, (n, n), 1)
                keep = jnp.logical_or(row >= col, true_row != true_col)
                a = packed[:, cols].astype(F32)

                @pl.when(true_col == 0)
                def _():
                    ah = packed[:, cols]
                    xh, xl = split(x0_ref[...])
                    f = dot_nt(ah, xh) + dot_nt(ah, xl)
                    out[:, cols] = jnp.where(keep, f, 0.0).astype(BF16)

                @pl.when(true_col == 1)
                def _():
                    bh, bl = split(a * s - dot_nt(left[:, :n], panel_ref[...]))
                    xh, xl = split(x1_ref[...])
                    f = dot_nt(bh, xh) + dot_nt(bl, xh) + dot_nt(bh, xl)
                    out[:, cols] = jnp.where(keep, f / s, 0.0).astype(BF16)


def update(pos, scales, packed, x0, x1, panel, mine, arrived, nr, nc, tpr, tpc, n):
    ratio = nr // nc
    geometry = (ratio, nr, nc, tpr, tpc, n, len(arrived))
    smem = pl.BlockSpec(memory_space=pltpu.SMEM)
    hbm = pl.BlockSpec(memory_space=pl.ANY)

    def whole(shape):
        return pl.BlockSpec(shape, lambda i: (0,) * len(shape))

    tall = mine.shape[1]
    return pl.pallas_call(
        functools.partial(update_kernel, geometry),
        grid=(tpr,),
        out_shape=jax.ShapeDtypeStruct(packed.shape, BF16),
        in_specs=[
            smem,
            smem,
            pl.BlockSpec((n, tpc * n), lambda i: (i, 0)),
            whole((n, n)),
            whole((n, n)),
            whole((n, n)),
            smem,
            hbm,
        ]
        + [hbm] * len(arrived),
        out_specs=pl.BlockSpec((n, tpc * n), lambda i: (i, 0)),
        scratch_shapes=[
            pltpu.VMEM((ratio + 1, 2, tall, n), BF16),
            pltpu.VMEM((tpr, n, 2 * n), BF16),
            pltpu.VMEM((tpc, n, 2 * n), BF16),
            pltpu.SemaphoreType.DMA((ratio + 1,)),
        ],
        compiler_params=pltpu.CompilerParams(vmem_limit_bytes=48 << 20),
        name="update_tiles",
    )(pos, scales, packed, x0, x1, panel, pos, mine, *arrived)


def exact_parts(scale):
    high = lax.reduce_precision(scale, 8, 7)
    rest = scale - high
    mid = lax.reduce_precision(rest, 8, 7)
    return jnp.stack([high, mid, rest - mid], axis=-1).astype(BF16)


def on_device(nr, nc, packed, tile_scales):
    tpr, tpc = tile_scales.shape
    n = packed.shape[0] // tpr
    r = lax.axis_index("prow")
    c = lax.axis_index("pcol")
    pos = jnp.stack([r, c]).astype(jnp.int32)

    def send(x, pairs):
        table = [(a * nc + b, d * nc + e) for (a, b), (d, e) in pairs]
        return lax.ppermute(x, ("prow", "pcol"), table)

    def choose(options, index):
        value = options[0]
        for k in range(1, len(options)):
            value = jnp.where(index == k, options[k], value)
        return value

    tail = exact_parts(tile_scales[:, 0]).reshape(-1)
    tail = jnp.pad(tail, (0, EXTRA - tail.shape[0]))
    tail = jnp.broadcast_to(tail[:, None], (EXTRA, n))
    pivot = jnp.concatenate([packed[:n, :n], tail], axis=0)
    message = jnp.concatenate([packed[:, :n], tail], axis=0)

    came = [pivot]
    for k in range(1, nc):
        pairs = [((0, 0), (0, k)), ((1, 0), (1, k)), ((1, 1), (1, (1 + k) % nc))]
        came.append(send(pivot, pairs))
    first = choose(came, c)
    second = choose(came, (c - 1) % nc)

    def spread(x, root):
        stride = nr
        while stride > 1:
            radix = 4 if stride >= 4 else 2
            stride //= radix
            got = [x]
            for k in range(1, radix):
                pairs = []
                for base in range(0, nr, radix * stride):
                    for col in range(nc):
                        pairs.append((((base ^ root), col), ((base + k * stride) ^ root, col)))
                got.append(send(x, pairs))
            x = choose(got, ((r ^ root) // stride) % radix)
        return x

    p00 = spread(first, 0)
    both = spread(jnp.stack([first, second]), 1)

    got0 = [message] * nc
    got1 = [message] * nc
    swap = send(message, [((a, b), (a, 1 - b)) for a in range(nr) for b in range(2)])
    got0[1] = swap
    got1[0] = swap
    for k in range(2, nc):
        other = 2 + (k - 1) % (nc - 2)
        pairs = [((a, 0), (a, k)) for a in range(nr)] + [((a, 1), (a, other)) for a in range(nr)]
        far = send(message, pairs)
        got0[k] = far
        got1[other] = far
    mine = jnp.stack([choose(got0, c), choose(got1, c)])

    arrived = []
    for mask in range(0, nr, 2):
        if mask == 0:
            near = mine
        else:
            pairs = []
            for col in range(nc):
                for g in range(nr // nc):
                    pairs.append(((col + nc * g, col), ((col + nc * g) ^ mask, col)))
            near = send(mine, pairs)
        pairs = []
        for col in range(nc):
            for g in range(nr // nc):
                place = (col + nc * g) ^ mask
                pairs.append(((place, col), (place ^ 1, col)))
        arrived += [near, send(near, pairs)]

    x0, x1, panel = factor_pivots(p00, both[0], both[1])
    return update(pos, tile_scales, packed, x0, x1, panel, mine, arrived, nr, nc, tpr, tpc, n)


def solution(mesh):
    nr = mesh.shape["prow"]
    nc = mesh.shape["pcol"]
    return jax.shard_map(
        functools.partial(on_device, nr, nc),
        mesh=mesh,
        in_specs=(P("prow", "pcol"), P("prow", "pcol")),
        out_specs=P("prow", "pcol"),
        check_vma=False,
    )
```

```python
import functools

import jax
import jax.numpy as jnp
import numpy as np
from jax import lax
from jax.experimental import pallas as pl
from jax.experimental.pallas import tpu as pltpu
from jax.sharding import PartitionSpec as P

F32 = jnp.float32
BF16 = jnp.bfloat16
HALF = 128
EXTRA = 16


def dot_nt(a, b, precision=None):
    dims = (((1,), (1,)), ((), ()))
    return lax.dot_general(a, b, dims, precision=precision, preferred_element_type=F32)


def dot_nn(a, b, precision=None):
    dims = (((1,), (0,)), ((), ()))
    return lax.dot_general(a, b, dims, precision=precision, preferred_element_type=F32)


HIGHEST = lax.Precision.HIGHEST


def inverse_factor(a):
    n = a.shape[0]
    blocks = n // 8
    full = (8, n)
    rows = [a[8 * i : 8 * i + 8, :] for i in range(blocks)]
    lane = lax.broadcasted_iota(jnp.int32, full, 1)
    sub = lax.broadcasted_iota(jnp.int32, full, 0)
    out = []
    for t in range(blocks):
        base = 8 * t
        here = jnp.logical_and(lane >= base, lane < base + 8)
        b = [jnp.broadcast_to(rows[t][j : j + 1, :], full) for j in range(8)]
        s = {}
        for j in range(8):
            for k in range(j, 8):
                s[j, k] = jnp.broadcast_to(b[j][:, base + k : base + k + 1], full)
        c = {}
        for i in range(t + 1, blocks):
            for j in range(8):
                c[i, j] = jnp.broadcast_to(rows[i][:, base + j : base + j + 1], full)
            rows[i] = jnp.where(here, 0.0, rows[i])
        b = [jnp.where(here, jnp.where(lane == base + j, 1.0, 0.0), b[j]) for j in range(8)]
        d = [c[t + 1, j] for j in range(8)] if t + 1 < blocks else None
        m = {}
        z = []
        x = jnp.zeros(full, F32)
        for j in range(8):
            r0 = pl.reciprocal(s[j, j], approx=True)
            e = 2.0 - s[j, j] * r0
            r = r0 * e
            for k in range(j + 1, 8):
                m[j, k] = s[j, k] * r
            for k in range(j + 1, 8):
                for l in range(k, 8):
                    if k == j + 1 and l == k:
                        s[k, l] = s[k, l] - ((s[j, k] * s[j, k]) * r0) * e
                    else:
                        s[k, l] = s[k, l] - m[j, k] * s[j, l]
                b[k] = b[k] - m[j, k] * b[j]
            z.append(r * b[j])
            if d is not None:
                for k in range(j + 1, 8):
                    d[k] = d[k] - m[j, k] * d[j]
                rows[t + 1] = rows[t + 1] - d[j] * z[j]
            x = jnp.where(sub == j, lax.rsqrt(s[j, j]) * b[j], x)
        out.append(jnp.where(lane < base + 8, x, 0.0))
        if t + 2 < blocks:
            y = list(z)
            for k in range(7, 0, -1):
                for j in range(k):
                    y[j] = y[j] - m[j, k] * y[k]
            for i in range(t + 2, blocks):
                for j in range(8):
                    rows[i] = rows[i] - c[i, j] * y[j]
    return jnp.concatenate(out, axis=0)


def scale_row(ref, row):
    parts = ref[row : row + 16, :].astype(F32)
    return parts[0:1] + parts[1:2] + parts[2:3]


def factor_tile(tile, out_ref, work, inv):
    work[0] = tile[:HALF, :HALF]
    work[1] = tile[HALF:, :HALF]
    work[2] = tile[HALF:, HALF:]

    def body(step, carry):
        x = inverse_factor(work[0])
        inv[step] = x

        @pl.when(step == 0)
        def _():
            factor = dot_nt(work[1], x, HIGHEST)
            work[1] = factor
            work[0] = work[2] - dot_nt(factor, factor, HIGHEST)

        return carry

    lax.fori_loop(0, 2, body, 0)
    x11 = inv[0]
    x22 = inv[1]
    x21 = dot_nn(x22, dot_nn(work[1], x11, HIGHEST), HIGHEST)
    out_ref[:HALF, :HALF] = x11
    out_ref[:HALF, HALF:] = jnp.zeros((HALF, HALF), F32)
    out_ref[HALF:, :HALF] = -x21
    out_ref[HALF:, HALF:] = x22


def first_kernel(p00, x0_ref, work, inv):
    n = x0_ref.shape[0]
    factor_tile(p00[:n, :].astype(F32) * scale_row(p00, n), x0_ref, work, inv)


def second_kernel(x0, p10, p11, x1_ref, panel_ref, work, inv):
    n = x0.shape[0]
    solved = dot_nt(p10[:n, :].astype(F32), x0[...], HIGHEST) * scale_row(p10, n)
    panel = solved.astype(BF16)
    panel_ref[...] = panel
    tile = p11[:n, :].astype(F32) * scale_row(p11, n) - dot_nt(panel, panel)
    factor_tile(tile, x1_ref, work, inv)


def factor_call(kernel, name, outs, args):
    vmem = pl.BlockSpec(memory_space=pltpu.VMEM)
    return pl.pallas_call(
        kernel,
        out_shape=outs,
        in_specs=[vmem] * len(args),
        out_specs=(vmem,) * len(outs),
        scratch_shapes=[pltpu.VMEM((3, HALF, HALF), F32), pltpu.VMEM((2, HALF, HALF), F32)],
        compiler_params=pltpu.CompilerParams(vmem_limit_bytes=24 << 20),
        cost_estimate=pl.CostEstimate(flops=10_000_000_000, bytes_accessed=1 << 20, transcendentals=0),
        name=name,
    )(*args)


def split(x):
    high = x.astype(BF16)
    return high, (x - high.astype(F32)).astype(BF16)


def update_kernel(geometry, table, pos, scales, packed, x0_ref, x1_ref, panel_ref, here, there, *rest):
    ratio, nr, nc, tpr, tpc, n, count = geometry
    blocks = rest[:count]
    out, block, rowp, colp, sem = rest[count:]
    step = pl.program_id(0)
    r = pos[0]
    c = pos[1]

    def solve(slot):
        x0h, x0l = split(x0_ref[...])
        x1h, x1l = split(x1_ref[...])
        pieces = []
        for t in range(tpr):
            a0 = block[slot, 0, t * n : (t + 1) * n, :]
            a1 = block[slot, 1, t * n : (t + 1) * n, :]
            tail0 = block[slot, 0, tpr * n :, :].astype(F32)
            tail1 = block[slot, 1, tpr * n :, :].astype(F32)
            s0 = tail0[3 * t : 3 * t + 1] + tail0[3 * t + 1 : 3 * t + 2] + tail0[3 * t + 2 : 3 * t + 3]
            s1 = tail1[3 * t : 3 * t + 1] + tail1[3 * t + 1 : 3 * t + 2] + tail1[3 * t + 2 : 3 * t + 3]
            f0 = (dot_nt(a0, x0h) + dot_nt(a0, x0l)) * s0
            p0 = f0.astype(BF16)
            low = a1.astype(F32) * s1 - dot_nt(p0, panel_ref[...])
            bh, bl = split(low)
            f1 = dot_nt(bh, x1h) + dot_nt(bl, x1h) + dot_nt(bh, x1l)
            pieces.append((f0, f1, p0, f1.astype(BF16)))
        return pieces

    @pl.when(step == 0)
    def _():
        same = (r % 2) == (c % 2)

        @pl.when(same)
        def _():
            for g in range(ratio):
                pltpu.make_async_copy(here.at[g], block.at[g], sem.at[g]).start()

        @pl.when(jnp.logical_not(same))
        def _():
            for g in range(ratio):
                pltpu.make_async_copy(there.at[g], block.at[g], sem.at[g]).start()

        for panel in range(2):
            index = table[2 * (r * nc + c) + panel]
            for k in range(count):

                @pl.when(index == k)
                def _(k=k, panel=panel):
                    pltpu.make_async_copy(blocks[k], block.at[ratio, panel], sem.at[ratio + panel]).start()

        for g in range(ratio):
            pltpu.make_async_copy(here.at[g], block.at[g], sem.at[g]).wait()
        for panel in range(2):
            pltpu.make_async_copy(blocks[0], block.at[ratio, panel], sem.at[ratio + panel]).wait()
        for g in range(ratio):
            for t, (_, _, p0, p1) in enumerate(solve(g)):
                q = t * ratio + g
                colp[q, :, :n] = p0
                colp[q, :, n:] = p1
        for t, (f0, f1, p0, p1) in enumerate(solve(ratio)):
            rowp[t, :, :n] = p0
            rowp[t, :, n:] = p1

    true_row = step * nr + r
    left = rowp[step]
    for q in range(tpc):
        true_col = q * nc + c
        cols = slice(q * n, (q + 1) * n)
        s = scales[step, q]

        @pl.when(true_row < true_col)
        def _(cols=cols):
            out[:, cols] = packed[:, cols]

        @pl.when(jnp.logical_and(true_row >= true_col, true_col >= 2))
        def _(cols=cols, s=s, q=q):
            change = dot_nt(left, colp[q])
            out[:, cols] = (packed[:, cols].astype(F32) - change * (1.0 / s)).astype(BF16)

        if q * nc < 2:

            @pl.when(jnp.logical_and(true_row >= true_col, true_col < 2))
            def _(cols=cols, s=s):
                row = lax.broadcasted_iota(jnp.int32, (n, n), 0)
                col = lax.broadcasted_iota(jnp.int32, (n, n), 1)
                keep = jnp.logical_or(row >= col, true_row != true_col)
                a = packed[:, cols].astype(F32)

                @pl.when(true_col == 0)
                def _():
                    ah = packed[:, cols]
                    xh, xl = split(x0_ref[...])
                    f = dot_nt(ah, xh) + dot_nt(ah, xl)
                    out[:, cols] = jnp.where(keep, f, 0.0).astype(BF16)

                @pl.when(true_col == 1)
                def _():
                    bh, bl = split(a * s - dot_nt(left[:, :n], panel_ref[...]))
                    xh, xl = split(x1_ref[...])
                    f = dot_nt(bh, xh) + dot_nt(bl, xh) + dot_nt(bh, xl)
                    out[:, cols] = jnp.where(keep, f / s, 0.0).astype(BF16)


def update(table, pos, scales, packed, x0, x1, panel, here, there, blocks, nr, nc, tpr, tpc, n):
    ratio = nr // nc
    geometry = (ratio, nr, nc, tpr, tpc, n, len(blocks))
    smem = pl.BlockSpec(memory_space=pltpu.SMEM)
    hbm = pl.BlockSpec(memory_space=pl.ANY)

    def whole(shape):
        return pl.BlockSpec(shape, lambda i: (0,) * len(shape))

    tall = blocks[0].shape[0]
    return pl.pallas_call(
        functools.partial(update_kernel, geometry),
        grid=(tpr,),
        out_shape=jax.ShapeDtypeStruct(packed.shape, BF16),
        in_specs=[smem, smem, smem, pl.BlockSpec((n, tpc * n), lambda i: (i, 0))]
        + [whole((n, n))] * 3
        + [hbm] * (2 + len(blocks)),
        out_specs=pl.BlockSpec((n, tpc * n), lambda i: (i, 0)),
        scratch_shapes=[
            pltpu.VMEM((ratio + 1, 2, tall, n), BF16),
            pltpu.VMEM((tpr, n, 2 * n), BF16),
            pltpu.VMEM((tpc, n, 2 * n), BF16),
            pltpu.SemaphoreType.DMA((ratio + 2,)),
        ],
        compiler_params=pltpu.CompilerParams(vmem_limit_bytes=48 << 20),
        cost_estimate=pl.CostEstimate(flops=4_000_000_000, bytes_accessed=8 << 20, transcendentals=0),
        name="update_tiles",
    )(table, pos, scales, packed, x0, x1, panel, here, there, *blocks)


def row_plan(nr, nc):
    if nc == 4:
        by_turn = [
            {0: [(1, 0, 0)], 1: [(0, 1, 0), (1, 2, 0)], 2: [(1, 2, 0)], 3: [(1, 3, 0)]},
            {0: [(0, 1, 0), (1, 2, 0)], 1: [(0, 2, 0), (1, 0, 0)], 2: [(0, 2, 0), (1, 0, 0)], 3: [(0, 3, 0), (1, 0, 0)]},
            {0: [(0, 2, 0), (2, 3, 2)], 1: [(2, 3, 1)], 2: [(0, 1, 0), (2, 3, 1)], 3: [(0, 1, 0), (3, 2, 1)]},
            {0: [(2, 3, 3)], 1: [(2, 3, 2)], 2: [(2, 3, 2)], 3: [(3, 2, 2)]},
        ]
        return [[(r, a, b, k) for r in range(nr) for a, b, k in turn[r % 4]] for turn in by_turn]
    rounds = [[], []]
    for r in range(nr):
        want = r % nc
        rounds[0].append((r, 0, 1, 0) if want == 1 else (r, 1, want, 0))
        if want > 1:
            rounds[1].append((r, 0, want, 0))
    for shift in range(1, nc):
        turn = []
        for r in range(nr):
            for a in range(2):
                b = (a + shift) % nc
                done = any((r, a, b, 0) in old for old in rounds[:2])
                if not done:
                    turn.append((r, a, b, 0))
        rounds.append(turn)
    return rounds


def exact_parts(scale):
    high = lax.reduce_precision(scale, 8, 7)
    rest = scale - high
    mid = lax.reduce_precision(rest, 8, 7)
    return jnp.stack([high, mid, rest - mid], axis=-1).astype(BF16)


def on_device(nr, nc, packed, tile_scales):
    tpr, tpc = tile_scales.shape
    n = packed.shape[0] // tpr
    r = lax.axis_index("prow")
    c = lax.axis_index("pcol")
    pos = jnp.stack([r, c]).astype(jnp.int32)
    place = r * nc + c

    def send(x, pairs):
        table = [(a * nc + b, d * nc + e) for (a, b), (d, e) in pairs]
        return lax.ppermute(x, ("prow", "pcol"), table)

    def choose(options, index):
        value = options[0]
        for k in range(1, len(options)):
            value = jnp.where(index == k, options[k], value)
        return value

    tail = exact_parts(tile_scales[:, 0]).reshape(-1)
    tail = jnp.pad(tail, (0, EXTRA - tail.shape[0]))
    tail = jnp.broadcast_to(tail[:, None], (EXTRA, n))
    pivot = jnp.concatenate([packed[:n, :n], tail], axis=0)
    message = jnp.concatenate([packed[:, :n], tail], axis=0)

    came = [pivot]
    for k in range(1, nc):
        pairs = [((0, 0), (0, k)), ((1, 0), (1, k)), ((1, 1), (1, (1 + k) % nc))]
        came.append(send(pivot, pairs))
    first = choose(came, c)
    second = choose(came, (c - 1) % nc)

    def spread(x, root):
        stride = nr
        while stride > 1:
            radix = 4 if stride >= 4 else 2
            stride //= radix
            got = [x]
            for k in range(1, radix):
                pairs = []
                for base in range(0, nr, radix * stride):
                    for col in range(nc):
                        pairs.append((((base ^ root), col), ((base + k * stride) ^ root, col)))
                got.append(send(x, pairs))
            x = choose(got, ((r ^ root) // stride) % radix)
        return x

    p00 = spread(first, 0)
    both = spread(jnp.stack([first, second]), 1)

    rounds = row_plan(nr, nc)
    blocks = [message]
    holds = {(a, b, b): 0 for a in range(nr) for b in range(2)}
    for turn in rounds:
        used = sorted({k for _, _, _, k in turn})
        operand = blocks[used[0]]
        for k in used[1:]:
            places = [a * nc + b for a, b, _, j in turn if j == k]
            hit = functools.reduce(jnp.logical_or, [place == p for p in places])
            operand = jnp.where(hit, blocks[k], operand)
        table = [((a, b), (a, d)) for a, b, d, _ in turn]
        for a, b, d, k in turn:
            panel = next(p for p in range(2) if holds.get((a, b, p)) == k)
            holds[a, d, panel] = len(blocks)
        blocks.append(send(operand, table))
    where_from = np.array([holds[a, b, p] for a in range(nr) for b in range(nc) for p in range(2)], np.int32)

    ratio = nr // nc
    col0 = jnp.where(c == 0, message, jnp.where(c == 1, blocks[1], blocks[2]))
    col1 = jnp.where(c == 1, message, blocks[1])
    source = jnp.stack([col0, col1])
    near = [source]
    for mask in range(2, nr, 2):
        pairs = [((e + nc * g, e), ((e + nc * g) ^ mask, e)) for e in range(nc) for g in range(ratio)]
        near.append(send(source, pairs))
    here = jnp.stack([choose(near, (r ^ (c + nc * g)) // 2) for g in range(ratio)])
    pairs = [((a, e), (a ^ 1, e)) for a in range(nr) for e in range(nc) if a % 2 == e % 2]
    there = send(here, pairs)

    square = jax.ShapeDtypeStruct((n, n), F32)
    (x0,) = factor_call(first_kernel, "factor_first", (square,), (p00,))
    x1, panel = factor_call(
        second_kernel, "factor_second", (square, jax.ShapeDtypeStruct((n, n), BF16)), (x0, both[0], both[1])
    )
    return update(
        where_from, pos, tile_scales, packed, x0, x1, panel, here, there, blocks, nr, nc, tpr, tpc, n
    )


def solution(mesh):
    nr = mesh.shape["prow"]
    nc = mesh.shape["pcol"]
    return jax.shard_map(
        functools.partial(on_device, nr, nc),
        mesh=mesh,
        in_specs=(P("prow", "pcol"), P("prow", "pcol")),
        out_specs=P("prow", "pcol"),
        check_vma=False,
    )
```

```python
import functools

import jax
import jax.numpy as jnp
import numpy as np
from jax import lax
from jax.experimental import pallas as pl
from jax.experimental.pallas import tpu as pltpu
from jax.sharding import PartitionSpec as P

F32 = jnp.float32
BF16 = jnp.bfloat16
HALF = 128
EXTRA = 16


def dot_nt(a, b, precision=None):
    dims = (((1,), (1,)), ((), ()))
    return lax.dot_general(a, b, dims, precision=precision, preferred_element_type=F32)


def dot_nn(a, b, precision=None):
    dims = (((1,), (0,)), ((), ()))
    return lax.dot_general(a, b, dims, precision=precision, preferred_element_type=F32)


HIGHEST = lax.Precision.HIGHEST


def inverse_factor(a):
    n = a.shape[0]
    blocks = n // 8
    full = (8, n)
    rows = [a[8 * i : 8 * i + 8, :] for i in range(blocks)]
    lane = lax.broadcasted_iota(jnp.int32, full, 1)
    sub = lax.broadcasted_iota(jnp.int32, full, 0)
    out = []
    for t in range(blocks):
        base = 8 * t
        here = jnp.logical_and(lane >= base, lane < base + 8)
        b = [jnp.broadcast_to(rows[t][j : j + 1, :], full) for j in range(8)]
        s = {}
        for j in range(8):
            for k in range(j, 8):
                s[j, k] = jnp.broadcast_to(b[j][:, base + k : base + k + 1], full)
        c = {}
        for i in range(t + 1, blocks):
            for j in range(8):
                c[i, j] = jnp.broadcast_to(rows[i][:, base + j : base + j + 1], full)
            rows[i] = jnp.where(here, 0.0, rows[i])
        b = [jnp.where(here, jnp.where(lane == base + j, 1.0, 0.0), b[j]) for j in range(8)]
        d = [c[t + 1, j] for j in range(8)] if t + 1 < blocks else None
        m = {}
        z = []
        x = jnp.zeros(full, F32)
        for j in range(8):
            r0 = pl.reciprocal(s[j, j], approx=True)
            e = 2.0 - s[j, j] * r0
            r = r0 * e
            for k in range(j + 1, 8):
                m[j, k] = s[j, k] * r
            for k in range(j + 1, 8):
                for l in range(k, 8):
                    if k == j + 1 and l == k:
                        s[k, l] = s[k, l] - ((s[j, k] * s[j, k]) * r0) * e
                    else:
                        s[k, l] = s[k, l] - m[j, k] * s[j, l]
                b[k] = b[k] - m[j, k] * b[j]
            z.append(r * b[j])
            if d is not None:
                for k in range(j + 1, 8):
                    d[k] = d[k] - m[j, k] * d[j]
                rows[t + 1] = rows[t + 1] - d[j] * z[j]
            x = jnp.where(sub == j, lax.rsqrt(s[j, j]) * b[j], x)
        out.append(jnp.where(lane < base + 8, x, 0.0))
        if t + 2 < blocks:
            y = list(z)
            for k in range(7, 0, -1):
                for j in range(k):
                    y[j] = y[j] - m[j, k] * y[k]
            for i in range(t + 2, blocks):
                for j in range(8):
                    rows[i] = rows[i] - c[i, j] * y[j]
    return jnp.concatenate(out, axis=0)


def tile_of(pieces):
    n = pieces.shape[0] * 8
    tile = pieces[:, :, :n].reshape(n, n)
    parts = pieces[0, :, n:].astype(F32)
    scale = parts[0:1, 0:1] + parts[1:2, 0:1] + parts[2:3, 0:1]
    return tile, scale


def factor_tile(tile, out_ref, work, inv):
    work[0] = tile[:HALF, :HALF]
    work[1] = tile[HALF:, :HALF]
    work[2] = tile[HALF:, HALF:]

    def body(step, carry):
        x = inverse_factor(work[0])
        inv[step] = x

        @pl.when(step == 0)
        def _():
            factor = dot_nt(work[1], x, HIGHEST)
            work[1] = factor
            work[0] = work[2] - dot_nt(factor, factor, HIGHEST)

        return carry

    lax.fori_loop(0, 2, body, 0)
    x11 = inv[0]
    x22 = inv[1]
    x21 = dot_nn(x22, dot_nn(work[1], x11, HIGHEST), HIGHEST)
    out_ref[:HALF, :HALF] = x11
    out_ref[:HALF, HALF:] = jnp.zeros((HALF, HALF), F32)
    out_ref[HALF:, :HALF] = -x21
    out_ref[HALF:, HALF:] = x22


def first_kernel(p00, x0_ref, work, inv):
    tile, scale = tile_of(p00[...])
    factor_tile(tile.astype(F32) * scale, x0_ref, work, inv)


def second_kernel(x0, p1, x1_ref, panel_ref, work, inv):
    low, low_scale = tile_of(p1[:, 0])
    corner, corner_scale = tile_of(p1[:, 1])
    solved = dot_nt(low.astype(F32), x0[...], HIGHEST) * low_scale
    panel = solved.astype(BF16)
    panel_ref[...] = panel
    tile = corner.astype(F32) * corner_scale - dot_nt(panel, panel)
    factor_tile(tile, x1_ref, work, inv)


def factor_call(kernel, name, outs, args):
    vmem = pl.BlockSpec(memory_space=pltpu.VMEM)
    return pl.pallas_call(
        kernel,
        out_shape=outs,
        in_specs=[vmem] * len(args),
        out_specs=(vmem,) * len(outs),
        scratch_shapes=[pltpu.VMEM((3, HALF, HALF), F32), pltpu.VMEM((2, HALF, HALF), F32)],
        compiler_params=pltpu.CompilerParams(vmem_limit_bytes=24 << 20),
        cost_estimate=pl.CostEstimate(flops=10_000_000_000, bytes_accessed=1 << 20, transcendentals=0),
        name=name,
    )(*args)


def split(x):
    high = x.astype(BF16)
    return high, (x - high.astype(F32)).astype(BF16)


def update_kernel(
    geometry, table, pos, scales, packed, x0_ref, x1_ref, panel_ref, here, there, mine, relayed, out, block, rowp, colp, sem
):
    ratio, nr, nc, tpr, tpc, n = geometry
    step = pl.program_id(0)
    r = pos[0]
    c = pos[1]

    def solve(slot):
        x0h, x0l = split(x0_ref[...])
        x1h, x1l = split(x1_ref[...])
        pieces = []
        for t in range(tpr):
            a0 = block[slot, 0, t * n : (t + 1) * n, :]
            a1 = block[slot, 1, t * n : (t + 1) * n, :]
            tail0 = block[slot, 0, tpr * n :, :].astype(F32)
            tail1 = block[slot, 1, tpr * n :, :].astype(F32)
            s0 = tail0[3 * t : 3 * t + 1] + tail0[3 * t + 1 : 3 * t + 2] + tail0[3 * t + 2 : 3 * t + 3]
            s1 = tail1[3 * t : 3 * t + 1] + tail1[3 * t + 1 : 3 * t + 2] + tail1[3 * t + 2 : 3 * t + 3]
            f0 = (dot_nt(a0, x0h) + dot_nt(a0, x0l)) * s0
            p0 = f0.astype(BF16)
            low = a1.astype(F32) * s1 - dot_nt(p0, panel_ref[...])
            bh, bl = split(low)
            f1 = dot_nt(bh, x1h) + dot_nt(bl, x1h) + dot_nt(bh, x1l)
            pieces.append((f0, f1, p0, f1.astype(BF16)))
        return pieces

    @pl.when(step == 0)
    def _():
        same = (r % 2) == (c % 2)

        @pl.when(same)
        def _():
            for g in range(ratio):
                pltpu.make_async_copy(here.at[g], block.at[g], sem.at[g]).start()

        @pl.when(jnp.logical_not(same))
        def _():
            for g in range(ratio):
                pltpu.make_async_copy(there.at[g], block.at[g], sem.at[g]).start()

        late = table[r * nc + c] == 1

        @pl.when(late)
        def _():
            pltpu.make_async_copy(relayed, block.at[ratio], sem.at[ratio]).start()

        @pl.when(jnp.logical_not(late))
        def _():
            pltpu.make_async_copy(mine, block.at[ratio], sem.at[ratio]).start()

        for g in range(ratio):
            pltpu.make_async_copy(here.at[g], block.at[g], sem.at[g]).wait()
        pltpu.make_async_copy(mine, block.at[ratio], sem.at[ratio]).wait()
        for g in range(ratio):
            for t, (_, _, p0, p1) in enumerate(solve(g)):
                q = t * ratio + g
                colp[q, :, :n] = p0
                colp[q, :, n:] = p1
        for t, (f0, f1, p0, p1) in enumerate(solve(ratio)):
            rowp[t, :, :n] = p0
            rowp[t, :, n:] = p1

    true_row = step * nr + r
    left = rowp[step]
    for q in range(tpc):
        true_col = q * nc + c
        cols = slice(q * n, (q + 1) * n)
        s = scales[step, q]

        @pl.when(true_row < true_col)
        def _(cols=cols):
            out[:, cols] = packed[:, cols]

        @pl.when(jnp.logical_and(true_row >= true_col, true_col >= 2))
        def _(cols=cols, s=s, q=q):
            change = dot_nt(left, colp[q])
            out[:, cols] = (packed[:, cols].astype(F32) - change * (1.0 / s)).astype(BF16)

        if q * nc < 2:

            @pl.when(jnp.logical_and(true_row >= true_col, true_col < 2))
            def _(cols=cols, s=s):
                row = lax.broadcasted_iota(jnp.int32, (n, n), 0)
                col = lax.broadcasted_iota(jnp.int32, (n, n), 1)
                keep = jnp.logical_or(row >= col, true_row != true_col)
                a = packed[:, cols].astype(F32)

                @pl.when(true_col == 0)
                def _():
                    ah = packed[:, cols]
                    xh, xl = split(x0_ref[...])
                    f = dot_nt(ah, xh) + dot_nt(ah, xl)
                    out[:, cols] = jnp.where(keep, f, 0.0).astype(BF16)

                @pl.when(true_col == 1)
                def _():
                    bh, bl = split(a * s - dot_nt(left[:, :n], panel_ref[...]))
                    xh, xl = split(x1_ref[...])
                    f = dot_nt(bh, xh) + dot_nt(bl, xh) + dot_nt(bh, xl)
                    out[:, cols] = jnp.where(keep, f / s, 0.0).astype(BF16)


def update(table, pos, scales, packed, x0, x1, panel, here, there, mine, relayed, nr, nc, tpr, tpc, n):
    ratio = nr // nc
    geometry = (ratio, nr, nc, tpr, tpc, n)
    smem = pl.BlockSpec(memory_space=pltpu.SMEM)
    hbm = pl.BlockSpec(memory_space=pl.ANY)

    def whole(shape):
        return pl.BlockSpec(shape, lambda i: (0,) * len(shape))

    tall = mine.shape[1]
    return pl.pallas_call(
        functools.partial(update_kernel, geometry),
        grid=(tpr,),
        out_shape=jax.ShapeDtypeStruct(packed.shape, BF16),
        in_specs=[smem, smem, smem, pl.BlockSpec((n, tpc * n), lambda i: (i, 0))]
        + [whole((n, n))] * 3
        + [hbm] * 4,
        out_specs=pl.BlockSpec((n, tpc * n), lambda i: (i, 0)),
        scratch_shapes=[
            pltpu.VMEM((ratio + 1, 2, tall, n), BF16),
            pltpu.VMEM((tpr, n, 2 * n), BF16),
            pltpu.VMEM((tpc, n, 2 * n), BF16),
            pltpu.SemaphoreType.DMA((ratio + 1,)),
        ],
        compiler_params=pltpu.CompilerParams(vmem_limit_bytes=48 << 20),
        cost_estimate=pl.CostEstimate(flops=4_000_000_000, bytes_accessed=8 << 20, transcendentals=0),
        name="update_tiles",
    )(table, pos, scales, packed, x0, x1, panel, here, there, mine, relayed)


def exact_parts(scale):
    high = lax.reduce_precision(scale, 8, 7)
    rest = scale - high
    mid = lax.reduce_precision(rest, 8, 7)
    return jnp.stack([high, mid, rest - mid], axis=-1).astype(BF16)


def on_device(nr, nc, packed, tile_scales):
    tpr, tpc = tile_scales.shape
    n = packed.shape[0] // tpr
    r = lax.axis_index("prow")
    c = lax.axis_index("pcol")
    pos = jnp.stack([r, c]).astype(jnp.int32)

    def send(x, pairs):
        table = [(a * nc + b, d * nc + e) for (a, b), (d, e) in pairs]
        return lax.ppermute(x, ("prow", "pcol"), table)

    def choose(options, index):
        value = options[0]
        for k in range(1, len(options)):
            value = jnp.where(index == k, options[k], value)
        return value

    parts = exact_parts(tile_scales[:, 0])
    beside = jnp.zeros((8, 128), BF16) + jnp.pad(parts[0], (0, 5))[:, None]
    devices = nr * nc
    if n == 8 * devices:
        own = jnp.concatenate([packed[:n, :n].reshape(devices, 8, n), jnp.broadcast_to(beside, (devices, 8, 128))], axis=2)
        spread = lax.all_to_all(own, ("prow", "pcol"), 0, 0)
        p00 = lax.all_to_all(jnp.broadcast_to(spread[0], own.shape), ("prow", "pcol"), 0, 0)
        pair = spread[nc : nc + 2]
        p1 = lax.all_to_all(jnp.broadcast_to(pair, (devices,) + pair.shape), ("prow", "pcol"), 0, 0)
    else:
        own = jnp.concatenate(
            [packed[:n, :n].reshape(n // 8, 8, n), jnp.broadcast_to(beside, (n // 8, 8, 128))], axis=2
        )
        found = []
        for root in ((0, 0), (1, 0), (1, 1)):
            x = jnp.where((r == root[0]) & (c == root[1]), own, 0)
            step = 1
            while step < devices:
                base = root[0] * nc + root[1]
                pairs = [((base + k) % devices, (base + k + step) % devices) for k in range(min(step, devices - step))]
                x = x + lax.ppermute(x, ("prow", "pcol"), pairs)
                step *= 2
            found.append(x)
        p00 = found[0]
        p1 = jnp.stack(found[1:], axis=1)

    tail = jnp.pad(parts.reshape(-1), (0, EXTRA - parts.size))
    tail = jnp.broadcast_to(tail[:, None], (EXTRA, n))
    message = jnp.concatenate([packed[:, :n], tail], axis=0)

    u = r % nc
    if nc == 4:
        first = {0: [(1, 0), (0, 2)], 1: [(0, 1), (1, 2)], 2: [(1, 2), (0, 1)], 3: [(1, 3), (0, 1)]}
        second = {0: [(1, 2), (0, 1)], 1: [(0, 2), (1, 0)], 2: [(0, 2), (1, 0)], 3: [(0, 3), (1, 0)]}
        turns = [[((a, x), (a, y)) for a in range(nr) for x, y in t[a % 4]] for t in (first, second)]
        got = [send(message, turn) for turn in turns]
        swap = (u == 0) == (c >= 2)
        m0 = jnp.where(c == 0, message, jnp.where(swap, got[0], got[1]))
        m0 = jnp.where(c == 1, jnp.where(u == 0, got[1], got[0]), m0)
        m1 = jnp.where(c == 1, message, jnp.where(swap, got[1], got[0]))
        m1 = jnp.where(c == 0, jnp.where(u == 0, got[0], got[1]), m1)
        mine = jnp.stack([m0, m1])
        relayed = send(mine, [((a, 3), (a, 2)) if a % 4 == 3 else ((a, 2), (a, 3)) for a in range(nr)])
        late = [[b == (2 if a % 4 == 3 else 3) for b in range(nc)] for a in range(nr)]
    else:
        m0 = message
        m1 = jnp.zeros_like(message)
        for k in range(1, nc):
            m0 = jnp.where(c == k, send(message, [((a, 0), (a, k)) for a in range(nr)]), m0)
        for k in range(nc):
            if k != 1:
                m1 = jnp.where(c == k, send(message, [((a, 1), (a, k)) for a in range(nr)]), m1)
        mine = jnp.stack([m0, jnp.where(c == 1, message, m1)])
        relayed = mine
        late = [[False] * nc] * nr
    late = np.array(late, np.int32).reshape(-1)

    ratio = nr // nc
    near = [mine]
    for mask in range(2, nr, 2):
        pairs = [((e + nc * g, e), ((e + nc * g) ^ mask, e)) for e in range(nc) for g in range(ratio)]
        near.append(send(mine, pairs))
    here = jnp.stack([choose(near, (r ^ (c + nc * g)) // 2) for g in range(ratio)])
    pairs = [((a, e), (a ^ 1, e)) for a in range(nr) for e in range(nc) if a % 2 == e % 2]
    there = send(here, pairs)

    square = jax.ShapeDtypeStruct((n, n), F32)
    (x0,) = factor_call(first_kernel, "factor_first", (square,), (p00,))
    x1, panel = factor_call(
        second_kernel, "factor_second", (square, jax.ShapeDtypeStruct((n, n), BF16)), (x0, p1)
    )
    return update(
        late, pos, tile_scales, packed, x0, x1, panel, here, there, mine, relayed, nr, nc, tpr, tpc, n
    )


def solution(mesh):
    nr = mesh.shape["prow"]
    nc = mesh.shape["pcol"]
    return jax.shard_map(
        functools.partial(on_device, nr, nc),
        mesh=mesh,
        in_specs=(P("prow", "pcol"), P("prow", "pcol")),
        out_specs=P("prow", "pcol"),
        check_vma=False,
    )
```

```python
import functools

import jax
import jax.numpy as jnp
import numpy as np
from jax import lax
from jax.experimental import pallas as pl
from jax.experimental.pallas import tpu as pltpu
from jax.sharding import PartitionSpec as P

F32 = jnp.float32
BF16 = jnp.bfloat16
HALF = 128
EXTRA = 16


def dot_nt(a, b, precision=None):
    dims = (((1,), (1,)), ((), ()))
    return lax.dot_general(a, b, dims, precision=precision, preferred_element_type=F32)


def dot_nn(a, b, precision=None):
    dims = (((1,), (0,)), ((), ()))
    return lax.dot_general(a, b, dims, precision=precision, preferred_element_type=F32)


HIGHEST = lax.Precision.HIGHEST


def inverse_factor(a):
    n = a.shape[0]
    blocks = n // 8
    full = (8, n)
    rows = [a[8 * i : 8 * i + 8, :] for i in range(blocks)]
    lane = lax.broadcasted_iota(jnp.int32, full, 1)
    sub = lax.broadcasted_iota(jnp.int32, full, 0)
    out = []
    for t in range(blocks):
        base = 8 * t
        here = jnp.logical_and(lane >= base, lane < base + 8)
        b = [jnp.broadcast_to(rows[t][j : j + 1, :], full) for j in range(8)]
        s = {}
        for j in range(8):
            for k in range(j, 8):
                s[j, k] = jnp.broadcast_to(b[j][:, base + k : base + k + 1], full)
        c = {}
        for i in range(t + 1, blocks):
            for j in range(8):
                c[i, j] = jnp.broadcast_to(rows[i][:, base + j : base + j + 1], full)
            rows[i] = jnp.where(here, 0.0, rows[i])
        b = [jnp.where(here, jnp.where(lane == base + j, 1.0, 0.0), b[j]) for j in range(8)]
        d = [c[t + 1, j] for j in range(8)] if t + 1 < blocks else None
        m = {}
        z = []
        x = jnp.zeros(full, F32)
        for j in range(8):
            r0 = pl.reciprocal(s[j, j], approx=True)
            e = 2.0 - s[j, j] * r0
            r = r0 * e
            for k in range(j + 1, 8):
                m[j, k] = s[j, k] * r
            for k in range(j + 1, 8):
                for l in range(k, 8):
                    if k == j + 1 and l == k:
                        s[k, l] = s[k, l] - ((s[j, k] * s[j, k]) * r0) * e
                    else:
                        s[k, l] = s[k, l] - m[j, k] * s[j, l]
                b[k] = b[k] - m[j, k] * b[j]
            z.append(r * b[j])
            if d is not None:
                for k in range(j + 1, 8):
                    d[k] = d[k] - m[j, k] * d[j]
                rows[t + 1] = rows[t + 1] - d[j] * z[j]
            x = jnp.where(sub == j, lax.rsqrt(s[j, j]) * b[j], x)
        out.append(jnp.where(lane < base + 8, x, 0.0))
        if t + 2 < blocks:
            y = list(z)
            for k in range(7, 0, -1):
                for j in range(k):
                    y[j] = y[j] - m[j, k] * y[k]
            for i in range(t + 2, blocks):
                for j in range(8):
                    rows[i] = rows[i] - c[i, j] * y[j]
    return jnp.concatenate(out, axis=0)


def split(x):
    high = x.astype(BF16)
    return high, (x - high.astype(F32)).astype(BF16)


def scale_row(ref, tile, n):
    tail = ref[n:, :].astype(F32)
    return tail[3 * tile : 3 * tile + 1] + tail[3 * tile + 1 : 3 * tile + 2] + tail[3 * tile + 2 : 3 * tile + 3]


def first_half(tile, inv_ref, low_ref, rest_ref):
    x = inverse_factor(tile[:HALF, :HALF])
    factor = dot_nt(tile[HALF:, :HALF], x, HIGHEST)
    inv_ref[...] = x
    low_ref[...] = factor
    rest_ref[...] = tile[HALF:, HALF:] - dot_nt(factor, factor, HIGHEST)


def second_half(inv_ref, low_ref, rest_ref, out_ref):
    x22 = inverse_factor(rest_ref[...])
    x11 = inv_ref[...]
    x21 = -dot_nn(x22, dot_nn(low_ref[...], x11, HIGHEST), HIGHEST)
    for k, x in enumerate((x11, x21, x22)):
        out_ref[k], out_ref[k + 3] = split(x)


def first_kernel(scales, packed, inv_ref, low_ref, rest_ref):
    first_half(packed[...].astype(F32) * scales[0, 0], inv_ref, low_ref, rest_ref)


def second_kernel(x0, pair, x1_ref, panel_ref, inv, low, rest):
    n = 2 * HALF
    cat = join(x0)
    a = pair[0, :n, :]
    solved = dot_nt(jnp.concatenate([a, a], axis=1), cat) * scale_row(pair[0], 0, n)
    panel = solved.astype(BF16)
    panel_ref[...] = panel
    tile = pair[1, :n, :].astype(F32) * scale_row(pair[1], 0, n) - dot_nt(panel, panel)
    first_half(tile, inv, low, rest)
    second_half(inv, low, rest, x1_ref)


def join(x):
    zero = jnp.zeros((HALF, HALF), BF16)
    upper = jnp.concatenate([x[0], zero, x[3], zero], axis=1)
    lower = jnp.concatenate([x[1], x[2], x[4], x[5]], axis=1)
    return jnp.concatenate([upper, lower], axis=0)


VMEM = pl.BlockSpec(memory_space=pltpu.VMEM)
SMEM = pl.BlockSpec(memory_space=pltpu.SMEM)
HBM = pl.BlockSpec(memory_space=pl.ANY)
BLOCK = jax.ShapeDtypeStruct((HALF, HALF), F32)
PARTS = jax.ShapeDtypeStruct((6, HALF, HALF), BF16)


def factor_call(kernel, name, outs, args, specs=None, scratch=(), work=1):
    return pl.pallas_call(
        kernel,
        grid=(1,) if specs else (),
        out_shape=outs,
        in_specs=specs or [VMEM] * len(args),
        out_specs=(VMEM,) * len(outs),
        scratch_shapes=scratch,
        compiler_params=pltpu.CompilerParams(vmem_limit_bytes=24 << 20),
        cost_estimate=pl.CostEstimate(flops=work * 5_000_000_000, bytes_accessed=1 << 20, transcendentals=0),
        name=name,
    )(*args)


def update_kernel(
    geometry, pos, scales, packed, x0_ref, x1_ref, panel_ref, side, far, there, mine, relayed, out, block, rowp, colp, rowl, sem
):
    ratio, nr, nc, tpr, tpc, n = geometry
    step = pl.program_id(0)
    r = pos[0]
    c = pos[1]
    late = pos[2]
    swap = pos[3]
    tall = tpr * n

    def scale_column(slot, panel):
        tail = block[slot, panel, tall:, :].astype(F32)
        rows = []
        for t in range(tpr):
            s = tail[3 * t : 3 * t + 1, :1] + tail[3 * t + 1 : 3 * t + 2, :1] + tail[3 * t + 2 : 3 * t + 3, :1]
            rows.append(jnp.broadcast_to(s, (n, 1)))
        return jnp.concatenate(rows, axis=0)

    def solve(slot, cat0, cat1):
        a0 = block[slot, 0, :tall, :]
        s0 = scale_column(slot, 0)
        s1 = scale_column(slot, 1)
        raw0 = dot_nt(jnp.concatenate([a0, a0], axis=1), cat0)
        p0 = (raw0 * s0).astype(BF16)
        rest = block[slot, 1, :tall, :].astype(F32) * s1 - dot_nt(p0, panel_ref[...])
        high, low = split(rest)
        f1 = dot_nt(jnp.concatenate([high, low, high], axis=1), cat1)
        return raw0, f1, s1, p0, f1.astype(BF16)

    @pl.when(step == 0)
    def _():
        same = (r % 2) == (c % 2)

        @pl.when(same)
        def _():
            pltpu.make_async_copy(side, block.at[0], sem.at[0]).start()
            pltpu.make_async_copy(far, block.at[1], sem.at[1]).start()

        @pl.when(jnp.logical_not(same))
        def _():
            for k in range(2):
                pltpu.make_async_copy(there.at[k], block.at[k], sem.at[k]).start()

        @pl.when(late == 1)
        def _():
            pltpu.make_async_copy(relayed, block.at[2], sem.at[2]).start()

        @pl.when(late == 0)
        def _():
            pltpu.make_async_copy(mine, block.at[2], sem.at[2]).start()

        cat0 = join(x0_ref)
        cat1 = join(x1_ref)
        cat1 = jnp.concatenate([cat1[:, :n], cat1[:, :n], cat1[:, n:]], axis=1)
        for k in range(2):
            pltpu.make_async_copy(mine, block.at[k], sem.at[k]).wait()
            _, _, _, p0, p1 = solve(k, cat0, cat1)
            for t in range(tpr):
                q = t * ratio + (swap ^ k)
                colp[q, :, :n] = p0[t * n : (t + 1) * n]
                colp[q, :, n:] = p1[t * n : (t + 1) * n]
        pltpu.make_async_copy(mine, block.at[2], sem.at[2]).wait()
        raw0, f1, s1, p0, p1 = solve(2, cat0, cat1)
        for t in range(tpr):
            rowp[t, :, :n] = p0[t * n : (t + 1) * n]
            rowp[t, :, n:] = p1[t * n : (t + 1) * n]

        @pl.when(c == 0)
        def _():
            rowl[...] = raw0

        @pl.when(c == 1)
        def _():
            rowl[...] = f1 / s1

    true_row = step * nr + r
    left = rowp[step]
    for q in range(tpc):
        true_col = q * nc + c
        cols = slice(q * n, (q + 1) * n)
        s = scales[step, q]

        @pl.when(true_row < true_col)
        def _(cols=cols):
            out[:, cols] = packed[:, cols]

        @pl.when(jnp.logical_and(true_row >= true_col, true_col >= 2))
        def _(cols=cols, s=s, q=q):
            change = dot_nt(left, colp[q])
            out[:, cols] = (packed[:, cols].astype(F32) - change * (1.0 / s)).astype(BF16)

        if q * nc < 2:

            @pl.when(jnp.logical_and(true_row >= true_col, true_col < 2))
            def _(cols=cols):
                row = lax.broadcasted_iota(jnp.int32, (n, n), 0)
                col = lax.broadcasted_iota(jnp.int32, (n, n), 1)
                keep = jnp.logical_or(row >= col, true_row != true_col)
                f = rowl[pl.ds(pl.multiple_of(step * n, n), n), :]
                out[:, cols] = jnp.where(keep, f, 0.0).astype(BF16)


def update(pos, scales, packed, x0, x1, panel, side, far, there, mine, relayed, nr, nc, tpr, tpc, n):
    ratio = nr // nc
    geometry = (ratio, nr, nc, tpr, tpc, n)

    def whole(shape):
        return pl.BlockSpec(shape, lambda i: (0,) * len(shape))

    tall = mine.shape[1]
    return pl.pallas_call(
        functools.partial(update_kernel, geometry),
        grid=(tpr,),
        out_shape=jax.ShapeDtypeStruct(packed.shape, BF16),
        in_specs=[SMEM, SMEM, pl.BlockSpec((n, tpc * n), lambda i: (i, 0))]
        + [whole(PARTS.shape)] * 2
        + [whole((n, n))]
        + [HBM] * 5,
        out_specs=pl.BlockSpec((n, tpc * n), lambda i: (i, 0)),
        scratch_shapes=[
            pltpu.VMEM((3, 2, tall, n), BF16),
            pltpu.VMEM((tpr, n, 2 * n), BF16),
            pltpu.VMEM((tpc, n, 2 * n), BF16),
            pltpu.VMEM((tpr * n, n), F32),
            pltpu.SemaphoreType.DMA((3,)),
        ],
        compiler_params=pltpu.CompilerParams(vmem_limit_bytes=48 << 20),
        cost_estimate=pl.CostEstimate(flops=4_000_000_000, bytes_accessed=8 << 20, transcendentals=0),
        name="update_tiles",
    )(pos, scales, packed, x0, x1, panel, side, far, there, mine, relayed)


def exact_parts(scale):
    high = lax.reduce_precision(scale, 8, 7)
    rest = scale - high
    mid = lax.reduce_precision(rest, 8, 7)
    return jnp.stack([high, mid, rest - mid], axis=-1).astype(BF16)


def on_device(nr, nc, packed, tile_scales):
    tpr, tpc = tile_scales.shape
    n = packed.shape[0] // tpr
    r = lax.axis_index("prow")
    c = lax.axis_index("pcol")
    def send(x, pairs):
        table = [(a * nc + b, d * nc + e) for (a, b), (d, e) in pairs]
        return lax.ppermute(x, ("prow", "pcol"), table)

    def choose(options, index):
        value = options[0]
        for k in range(1, len(options)):
            value = jnp.where(index == k, options[k], value)
        return value

    def spread(x, root, radices):
        stride = nr
        for radix in radices:
            stride //= radix
            got = [x]
            for k in range(1, radix):
                pairs = [
                    ((base ^ root, col), ((base + k * stride) ^ root, col))
                    for base in range(0, nr, radix * stride)
                    for col in range(nc)
                ]
                got.append(send(x, pairs))
            x = choose(got, ((r ^ root) // stride) % radix)
        return x

    radices = []
    while np.prod(radices, initial=1) < nr:
        radices.append(4 if nr // int(np.prod(radices, initial=1)) >= 4 else 2)
    twos = [2] * (nr.bit_length() - 1)

    corner = pl.BlockSpec((n, n), lambda i: (0, 0))
    halves = factor_call(first_kernel, "factor_start", (BLOCK,) * 3, (tile_scales, packed), [SMEM, corner])
    parts = exact_parts(tile_scales[:, 0])
    tail = jnp.pad(parts.reshape(-1), (0, EXTRA - parts.size))
    tail = jnp.broadcast_to(tail[:, None], (EXTRA, n))
    message = jnp.concatenate([packed[:, :n], tail], axis=0)
    message, *halves = lax.optimization_barrier((message, *halves))
    (x0,) = factor_call(second_half, "factor_finish", (PARTS,), tuple(halves))

    pivot = jnp.concatenate([message[:n], message[tpr * n :]], axis=0)
    if nc == 4:
        got = send(pivot, [((1, 0), (1, 2)), ((1, 1), (1, 3))])
        held = jnp.where(c < 2, pivot, got)
        other = send(held, [((1, k), (1, k ^ 1)) for k in range(nc)])
        pair = jnp.stack([jnp.where(c % 2 == 0, held, other), jnp.where(c % 2 == 0, other, held)])
    else:
        low = pivot
        high = jnp.where(c == 1, pivot, 0)
        for k in range(1, nc):
            low = jnp.where(c == k, send(pivot, [((1, 0), (1, k))]), low)
        for k in range(nc):
            if k != 1:
                high = jnp.where(c == k, send(pivot, [((1, 1), (1, k))]), high)
        pair = jnp.stack([low, high])
    pair = spread(pair, 1, twos)

    x0 = choose([x0] + [send(x0, [((0, 0), (0, k))]) for k in range(1, nc)], c)

    u = r % nc
    if nc == 4:
        first = {0: [(1, 0), (0, 2)], 1: [(0, 1), (1, 2)], 2: [(1, 2), (0, 1)], 3: [(1, 3), (0, 1)]}
        second = {0: [(1, 2), (0, 1)], 1: [(0, 2), (1, 0)], 2: [(0, 2), (1, 0)], 3: [(0, 3), (1, 0)]}
        turns = [[((a, x), (a, y)) for a in range(nr) for x, y in t[a % 4]] for t in (first, second)]
        got = [send(message, turn) for turn in turns]
        *got, _ = lax.optimization_barrier((*got, x0))
        swap = (u == 0) == (c >= 2)
        m0 = jnp.where(c == 0, message, jnp.where(swap, got[0], got[1]))
        m0 = jnp.where(c == 1, jnp.where(u == 0, got[1], got[0]), m0)
        m1 = jnp.where(c == 1, message, jnp.where(swap, got[1], got[0]))
        m1 = jnp.where(c == 0, jnp.where(u == 0, got[0], got[1]), m1)
        mine = jnp.stack([m0, m1])
        relayed = send(mine, [((a, 3), (a, 2)) if a % 4 == 3 else ((a, 2), (a, 3)) for a in range(nr)])
        late = [[b == (2 if a % 4 == 3 else 3) for b in range(nc)] for a in range(nr)]
    else:
        m0 = message
        m1 = jnp.zeros_like(message)
        for k in range(1, nc):
            m0 = jnp.where(c == k, send(message, [((a, 0), (a, k)) for a in range(nr)]), m0)
        for k in range(nc):
            if k != 1:
                m1 = jnp.where(c == k, send(message, [((a, 1), (a, k)) for a in range(nr)]), m1)
        mine = jnp.stack([m0, jnp.where(c == 1, message, m1)])
        relayed = mine
        late = [[False] * nc] * nr
    late = jnp.array(np.array(late, np.int32))[r, c]

    x0 = spread(x0, 0, radices)

    ratio = nr // nc
    if (nr, nc) == (8, 4):
        got = send(mine, [((e + 4 * g, e), ((e + 4 * g) ^ 2, e)) for e in range(nc) for g in range(2)])
        side = jnp.where(u == c, mine, got)
        far = send(side, [((a, e), (a ^ 4, e)) for a in range(nr) for e in range(nc) if a % 2 == e % 2])
        swap = r // 4
    else:
        near = [mine]
        for mask in range(2, nr, 2):
            pairs = [((e + nc * g, e), ((e + nc * g) ^ mask, e)) for e in range(nc) for g in range(ratio)]
            near.append(send(mine, pairs))
        side, far = [choose(near, (r ^ (c + nc * g)) // 2) for g in range(ratio)]
        swap = jnp.zeros_like(r)
    pairs = [((a, e), (a ^ 1, e)) for a in range(nr) for e in range(nc) if a % 2 == e % 2]
    there = send(jnp.stack([side, far]), pairs)

    scratch = [pltpu.VMEM((HALF, HALF), F32)] * 3
    panel = jax.ShapeDtypeStruct((n, n), BF16)
    x1, panel = factor_call(second_kernel, "factor_second", (PARTS, panel), (x0, pair), None, scratch, 2)
    pos = jnp.stack([r, c, late, swap]).astype(jnp.int32)
    return update(pos, tile_scales, packed, x0, x1, panel, side, far, there, mine, relayed, nr, nc, tpr, tpc, n)


def solution(mesh):
    nr = mesh.shape["prow"]
    nc = mesh.shape["pcol"]
    return jax.shard_map(
        functools.partial(on_device, nr, nc),
        mesh=mesh,
        in_specs=(P("prow", "pcol"), P("prow", "pcol")),
        out_specs=P("prow", "pcol"),
        check_vma=False,
    )
```

```python
import functools

import jax
import jax.numpy as jnp
import numpy as np
from jax import lax
from jax.experimental import pallas as pl
from jax.experimental.pallas import tpu as pltpu
from jax.sharding import PartitionSpec as P

F32 = jnp.float32
BF16 = jnp.bfloat16
HALF = 128
EXTRA = 16


def dot_nt(a, b, precision=None):
    dims = (((1,), (1,)), ((), ()))
    return lax.dot_general(a, b, dims, precision=precision, preferred_element_type=F32)


def dot_nn(a, b, precision=None):
    dims = (((1,), (0,)), ((), ()))
    return lax.dot_general(a, b, dims, precision=precision, preferred_element_type=F32)


HIGHEST = lax.Precision.HIGHEST


def inverse_factor(a):
    n = a.shape[0]
    blocks = n // 8
    full = (8, n)
    rows = [a[8 * i : 8 * i + 8, :] for i in range(blocks)]
    lane = lax.broadcasted_iota(jnp.int32, full, 1)
    sub = lax.broadcasted_iota(jnp.int32, full, 0)
    out = []
    for t in range(blocks):
        base = 8 * t
        here = jnp.logical_and(lane >= base, lane < base + 8)
        b = [jnp.broadcast_to(rows[t][j : j + 1, :], full) for j in range(8)]
        s = {}
        for j in range(8):
            for k in range(j, 8):
                s[j, k] = jnp.broadcast_to(b[j][:, base + k : base + k + 1], full)
        c = {}
        for i in range(t + 1, blocks):
            for j in range(8):
                c[i, j] = jnp.broadcast_to(rows[i][:, base + j : base + j + 1], full)
            rows[i] = jnp.where(here, 0.0, rows[i])
        b = [jnp.where(here, jnp.where(lane == base + j, 1.0, 0.0), b[j]) for j in range(8)]
        d = [c[t + 1, j] for j in range(8)] if t + 1 < blocks else None
        m = {}
        z = []
        x = jnp.zeros(full, F32)
        for j in range(8):
            r0 = pl.reciprocal(s[j, j], approx=True)
            e = 2.0 - s[j, j] * r0
            r = r0 * e
            for k in range(j + 1, 8):
                m[j, k] = s[j, k] * r
            for k in range(j + 1, 8):
                for l in range(k, 8):
                    if k == j + 1 and l == k:
                        s[k, l] = s[k, l] - ((s[j, k] * s[j, k]) * r0) * e
                    else:
                        s[k, l] = s[k, l] - m[j, k] * s[j, l]
                b[k] = b[k] - m[j, k] * b[j]
            z.append(r * b[j])
            if d is not None:
                for k in range(j + 1, 8):
                    d[k] = d[k] - m[j, k] * d[j]
                rows[t + 1] = rows[t + 1] - d[j] * z[j]
            x = jnp.where(sub == j, lax.rsqrt(s[j, j]) * b[j], x)
        out.append(jnp.where(lane < base + 8, x, 0.0))
        if t + 2 < blocks:
            y = list(z)
            for k in range(7, 0, -1):
                for j in range(k):
                    y[j] = y[j] - m[j, k] * y[k]
            for i in range(t + 2, blocks):
                for j in range(8):
                    rows[i] = rows[i] - c[i, j] * y[j]
    return jnp.concatenate(out, axis=0)


def split(x):
    high = x.astype(BF16)
    return high, (x - high.astype(F32)).astype(BF16)


def scale_row(ref, tile, n):
    tail = ref[n:, :].astype(F32)
    return tail[3 * tile : 3 * tile + 1] + tail[3 * tile + 1 : 3 * tile + 2] + tail[3 * tile + 2 : 3 * tile + 3]


def first_half(tile, inv_ref, low_ref, rest_ref):
    x = inverse_factor(tile[:HALF, :HALF])
    factor = dot_nt(tile[HALF:, :HALF], x, HIGHEST)
    inv_ref[...] = x
    low_ref[...] = factor
    rest_ref[...] = tile[HALF:, HALF:] - dot_nt(factor, factor, HIGHEST)


def second_half(inv_ref, low_ref, rest_ref, out_ref):
    x22 = inverse_factor(rest_ref[...])
    x11 = inv_ref[...]
    x21 = -dot_nn(x22, dot_nn(low_ref[...], x11, HIGHEST), HIGHEST)
    for k, x in enumerate((x11, x21, x22)):
        out_ref[k], out_ref[k + 3] = split(x)


def scale_tail(scales, n):
    row = lax.broadcasted_iota(jnp.int32, (EXTRA, n), 0)
    total = jnp.zeros((EXTRA, n), F32)
    for t in range(scales.shape[0]):
        rest = jnp.full((EXTRA, n), scales[t, 0], F32)
        for k in range(3):
            part = rest.astype(BF16).astype(F32)
            total = jnp.where(row == 3 * t + k, part, total)
            rest = rest - part
    return total.astype(BF16)


def start_kernel(scales, packed, inv_ref, low_ref, rest_ref, message, pivot, sem):
    n = pivot.shape[1]
    tall = message.shape[0] - EXTRA
    tile_copy = pltpu.make_async_copy(packed.at[0:n, 0:n], pivot.at[0:n], sem.at[0])
    block_copy = pltpu.make_async_copy(packed.at[:, 0:n], message.at[0:tall], sem.at[1])
    tile_copy.start()
    block_copy.start()
    tail = scale_tail(scales, n)
    pivot[n:, :] = tail
    message[tall:, :] = tail
    tile_copy.wait()
    first_half(pivot[:n, :].astype(F32) * scales[0, 0], inv_ref, low_ref, rest_ref)
    block_copy.wait()


def second_kernel(x0, pair, out_ref, inv, low, rest):
    n = 2 * HALF
    out_ref[0:6] = x0[...]
    a = pair[0, :n, :]
    solved = dot_nt(jnp.concatenate([a, a], axis=1), join(x0, 0)) * scale_row(pair[0], 0, n)
    panel = solved.astype(BF16)
    for k in range(4):
        i, j = divmod(k, 2)
        out_ref[12 + k] = panel[i * HALF : (i + 1) * HALF, j * HALF : (j + 1) * HALF]
    tile = pair[1, :n, :].astype(F32) * scale_row(pair[1], 0, n) - dot_nt(panel, panel)
    first_half(tile, inv, low, rest)
    second_half(inv, low, rest, out_ref.at[6:12])


def join(x, base):
    zero = jnp.zeros((HALF, HALF), BF16)
    upper = jnp.concatenate([x[base], zero, x[base + 3], zero], axis=1)
    lower = jnp.concatenate([x[base + 1], x[base + 2], x[base + 4], x[base + 5]], axis=1)
    return jnp.concatenate([upper, lower], axis=0)


VMEM = pl.BlockSpec(memory_space=pltpu.VMEM)
SMEM = pl.BlockSpec(memory_space=pltpu.SMEM)
HBM = pl.BlockSpec(memory_space=pl.ANY)
BLOCK = jax.ShapeDtypeStruct((HALF, HALF), F32)
PARTS = jax.ShapeDtypeStruct((6, HALF, HALF), BF16)
FACTORS = jax.ShapeDtypeStruct((16, HALF, HALF), BF16)


def factor_call(kernel, name, outs, args, specs=None, scratch=(), work=1):
    return pl.pallas_call(
        kernel,
        out_shape=outs,
        in_specs=specs or [VMEM] * len(args),
        out_specs=(VMEM,) * len(outs),
        scratch_shapes=scratch,
        compiler_params=pltpu.CompilerParams(vmem_limit_bytes=56 << 20),
        cost_estimate=pl.CostEstimate(flops=work * 5_000_000_000, bytes_accessed=1 << 20, transcendentals=0),
        name=name,
    )(*args)


def update_kernel(geometry, scales, packed, *rest):
    ratio, nr, nc, tpr, tpc, n = geometry
    factors, factors_other, cols_here, cols_other, mine, relayed = rest[0], rest[1], rest[2:4], rest[4:6], rest[6], rest[7]
    out, block, rowp, colp, rowl, xs, sem = rest[8:]
    step = pl.program_id(0)
    r = lax.axis_index("prow")
    c = lax.axis_index("pcol")
    late = jnp.logical_and(nc == 4, jnp.where(r % 4 == 3, c == 2, c == 3))
    swap = jnp.where((nr, nc) == (8, 4), r // 4, 0)
    tall = tpr * n

    def scale_column(slot, panel):
        tail = block[slot, panel, tall:, :].astype(F32)
        rows = []
        for t in range(tpr):
            s = tail[3 * t : 3 * t + 1, :1] + tail[3 * t + 1 : 3 * t + 2, :1] + tail[3 * t + 2 : 3 * t + 3, :1]
            rows.append(jnp.broadcast_to(s, (n, 1)))
        return jnp.concatenate(rows, axis=0)

    def solve(slot, cat0, cat1, panel):
        a0 = block[slot, 0, :tall, :]
        s0 = scale_column(slot, 0)
        s1 = scale_column(slot, 1)
        raw0 = dot_nt(jnp.concatenate([a0, a0], axis=1), cat0)
        p0 = (raw0 * s0).astype(BF16)
        rest = block[slot, 1, :tall, :].astype(F32) * s1 - dot_nt(p0, panel)
        high, low = split(rest)
        f1 = dot_nt(jnp.concatenate([high, low, high], axis=1), cat1)
        return raw0, f1, s1, p0, f1.astype(BF16)

    @pl.when(step == 0)
    def _():
        def fetch(choice, here, there, target, k):
            @pl.when(choice)
            def _():
                pltpu.make_async_copy(here, target, sem.at[k]).start()

            @pl.when(jnp.logical_not(choice))
            def _():
                pltpu.make_async_copy(there, target, sem.at[k]).start()

        fetch(r % 2 == 0, factors, factors_other, xs, 3)
        for k in range(2):
            fetch((r % 2) == (c % 2), cols_here[k], cols_other[k], block.at[k], k)
        fetch(late, relayed, mine, block.at[2], 2)
        pltpu.make_async_copy(factors, xs, sem.at[3]).wait()
        cat0 = join(xs, 0)
        cat1 = join(xs, 6)
        cat1 = jnp.concatenate([cat1[:, :n], cat1[:, :n], cat1[:, n:]], axis=1)
        panel = jnp.concatenate(
            [jnp.concatenate([xs[12], xs[13]], axis=1), jnp.concatenate([xs[14], xs[15]], axis=1)], axis=0
        )
        for k in range(2):
            pltpu.make_async_copy(mine, block.at[k], sem.at[k]).wait()
            _, _, _, p0, p1 = solve(k, cat0, cat1, panel)
            for t in range(tpr):
                q = t * ratio + (swap ^ k)
                colp[q, :, :n] = p0[t * n : (t + 1) * n]
                colp[q, :, n:] = p1[t * n : (t + 1) * n]
        pltpu.make_async_copy(mine, block.at[2], sem.at[2]).wait()
        raw0, f1, s1, p0, p1 = solve(2, cat0, cat1, panel)
        for t in range(tpr):
            rowp[t, :, :n] = p0[t * n : (t + 1) * n]
            rowp[t, :, n:] = p1[t * n : (t + 1) * n]

        @pl.when(c == 0)
        def _():
            rowl[...] = raw0

        @pl.when(c == 1)
        def _():
            rowl[...] = f1 / s1

    true_row = step * nr + r
    left = rowp[step]
    for q in range(tpc):
        true_col = q * nc + c
        cols = slice(q * n, (q + 1) * n)
        s = scales[step, q]

        @pl.when(true_row < true_col)
        def _(cols=cols):
            out[:, cols] = packed[:, cols]

        @pl.when(jnp.logical_and(true_row >= true_col, true_col >= 2))
        def _(cols=cols, s=s, q=q):
            change = dot_nt(left, colp[q])
            out[:, cols] = (packed[:, cols].astype(F32) - change * (1.0 / s)).astype(BF16)

        if q * nc < 2:

            @pl.when(jnp.logical_and(true_row >= true_col, true_col < 2))
            def _(cols=cols):
                row = lax.broadcasted_iota(jnp.int32, (n, n), 0)
                col = lax.broadcasted_iota(jnp.int32, (n, n), 1)
                keep = jnp.logical_or(row >= col, true_row != true_col)
                f = rowl[pl.ds(pl.multiple_of(step * n, n), n), :]
                out[:, cols] = jnp.where(keep, f, 0.0).astype(BF16)


def update(scales, packed, blocks, nr, nc, tpr, tpc, n):
    geometry = (nr // nc, nr, nc, tpr, tpc, n)
    tall = blocks[-1].shape[1]
    return pl.pallas_call(
        functools.partial(update_kernel, geometry),
        grid=(tpr,),
        out_shape=jax.ShapeDtypeStruct(packed.shape, BF16),
        in_specs=[SMEM, pl.BlockSpec((n, tpc * n), lambda i: (i, 0))] + [HBM] * len(blocks),
        out_specs=pl.BlockSpec((n, tpc * n), lambda i: (i, 0)),
        scratch_shapes=[
            pltpu.VMEM((3, 2, tall, n), BF16),
            pltpu.VMEM((tpr, n, 2 * n), BF16),
            pltpu.VMEM((tpc, n, 2 * n), BF16),
            pltpu.VMEM((tpr * n, n), F32),
            pltpu.VMEM(FACTORS.shape, BF16),
            pltpu.SemaphoreType.DMA((4,)),
        ],
        compiler_params=pltpu.CompilerParams(vmem_limit_bytes=48 << 20),
        cost_estimate=pl.CostEstimate(flops=4_000_000_000, bytes_accessed=8 << 20, transcendentals=0),
        name="update_tiles",
    )(scales, packed, *blocks)


def on_device(nr, nc, packed, tile_scales):
    tpr, tpc = tile_scales.shape
    n = packed.shape[0] // tpr
    r = lax.axis_index("prow")
    c = lax.axis_index("pcol")
    def send(x, pairs):
        table = [(a * nc + b, d * nc + e) for (a, b), (d, e) in pairs]
        return lax.ppermute(x, ("prow", "pcol"), table)

    inv, low, rest, message, pivot = factor_call(
        start_kernel,
        "factor_start",
        (BLOCK,) * 3
        + (jax.ShapeDtypeStruct((tpr * n + EXTRA, n), BF16), jax.ShapeDtypeStruct((n + EXTRA, n), BF16)),
        (tile_scales, packed),
        [SMEM, HBM],
        [pltpu.SemaphoreType.DMA((2,))],
    )
    (x0,) = factor_call(second_half, "factor_finish", (PARTS,), (inv, low, rest), work=10)

    if nc == 4:
        got = send(pivot, [((1, 0), (1, 2)), ((1, 1), (1, 3))])
        held = jnp.where(c < 2, pivot, got)
        other = send(held, [((1, k), (1, k ^ 1)) for k in range(nc)])
        pair = jnp.stack([jnp.where(c % 2 == 0, held, other), jnp.where(c % 2 == 0, other, held)])
    else:
        left = pivot
        right = jnp.where(c == 1, pivot, 0)
        for k in range(1, nc):
            left = jnp.where(c == k, send(pivot, [((1, 0), (1, k))]), left)
        for k in range(nc):
            if k != 1:
                right = jnp.where(c == k, send(pivot, [((1, 1), (1, k))]), right)
        pair = jnp.stack([left, right])

    step = nc // 2
    while step:
        x0 = jnp.where((c // step) % 2 == 1, send(x0, [((0, k), (0, k + step)) for k in range(0, nc, 2 * step)]), x0)
        step //= 2

    u = r % nc
    if nc == 4:
        first = {0: [(1, 0), (0, 2)], 1: [(0, 1), (1, 2)], 2: [(1, 2), (0, 1)], 3: [(1, 3), (0, 1)]}
        second = {0: [(1, 2), (0, 1)], 1: [(0, 2), (1, 0)], 2: [(0, 2), (1, 0)], 3: [(0, 3), (1, 0)]}
        turns = [[((a, x), (a, y)) for a in range(nr) for x, y in t[a % 4]] for t in (first, second)]
        got = [send(message, turn) for turn in turns]
        *got, _ = lax.optimization_barrier((*got, x0))
        swap = (u == 0) == (c >= 2)
        m0 = jnp.where(c == 0, message, jnp.where(swap, got[0], got[1]))
        m0 = jnp.where(c == 1, jnp.where(u == 0, got[1], got[0]), m0)
        m1 = jnp.where(c == 1, message, jnp.where(swap, got[1], got[0]))
        m1 = jnp.where(c == 0, jnp.where(u == 0, got[0], got[1]), m1)
        mine = jnp.stack([m0, m1])
        relayed = send(mine, [((a, 3), (a, 2)) if a % 4 == 3 else ((a, 2), (a, 3)) for a in range(nr)])
    else:
        m0 = message
        m1 = jnp.where(c == 1, message, 0)
        for k in range(1, nc):
            m0 = jnp.where(c == k, send(message, [((a, 0), (a, k)) for a in range(nr)]), m0)
        for k in range(nc):
            if k != 1:
                m1 = jnp.where(c == k, send(message, [((a, 1), (a, k)) for a in range(nr)]), m1)
        mine = jnp.stack([m0, m1])
        relayed = mine

    step = nr // 2
    while step > 1:
        takes = (r // step) % 2 == 1
        pairs = [((a, e), (a + step, e)) for a in range(0, nr, 2 * step) for e in range(nc)]
        x0 = jnp.where(takes, send(x0, pairs), x0)
        pairs = [((a or 1, e), (a + step, e)) for a in range(0, nr, 2 * step) for e in range(nc)]
        pair = jnp.where(takes, send(pair, pairs), pair)
        step //= 2
    pair = jnp.where(r == 0, send(pair, [((1, e), (0, e)) for e in range(nc)]), pair)

    ratio = nr // nc
    if (nr, nc) == (8, 4):
        got = send(mine, [((e + 4 * g, e), ((e + 4 * g) ^ 2, e)) for e in range(nc) for g in range(2)])
        side = jnp.where(u == c, mine, got)
        cols = [side, send(side, [((a, e), (a ^ 4, e)) for a in range(nr) for e in range(nc) if a % 2 == e % 2])]
    else:
        cols = [mine] * ratio
        for mask in range(2, nr, 2):
            pairs = [((e + nc * g, e), ((e + nc * g) ^ mask, e)) for e in range(nc) for g in range(ratio)]
            got = send(mine, pairs)
            cols = [jnp.where((r ^ (c + nc * g)) // 2 == mask // 2, got, cols[g]) for g in range(ratio)]
    pairs = [((a, e), (a ^ 1, e)) for a in range(nr) for e in range(nc) if a % 2 == e % 2]
    cols_other = [send(x, pairs) for x in cols]

    scratch = [pltpu.VMEM((HALF, HALF), F32)] * 3
    (factors,) = factor_call(second_kernel, "factor_second", (FACTORS,), (x0, pair), None, scratch, 10)
    factors_other = send(factors, [((a, e), (a + 1, e)) for a in range(0, nr, 2) for e in range(nc)])
    blocks = (factors, factors_other, *cols, *cols_other, mine, relayed)
    return update(tile_scales, packed, blocks, nr, nc, tpr, tpc, n)


def solution(mesh):
    nr = mesh.shape["prow"]
    nc = mesh.shape["pcol"]
    return jax.shard_map(
        functools.partial(on_device, nr, nc),
        mesh=mesh,
        in_specs=(P("prow", "pcol"), P("prow", "pcol")),
        out_specs=P("prow", "pcol"),
        check_vma=False,
    )
```

```python
import functools

import jax
import jax.numpy as jnp
import numpy as np
from jax import lax
from jax.experimental import pallas as pl
from jax.experimental.pallas import tpu as pltpu
from jax.sharding import PartitionSpec as P

F32 = jnp.float32
BF16 = jnp.bfloat16
HALF = 128
EXTRA = 16


def dot_nt(a, b, precision=None):
    dims = (((1,), (1,)), ((), ()))
    return lax.dot_general(a, b, dims, precision=precision, preferred_element_type=F32)


def dot_nn(a, b, precision=None):
    dims = (((1,), (0,)), ((), ()))
    return lax.dot_general(a, b, dims, precision=precision, preferred_element_type=F32)


HIGHEST = lax.Precision.HIGHEST


def inverse_factor(a):
    n = a.shape[0]
    blocks = n // 8
    full = (8, n)
    rows = [a[8 * i : 8 * i + 8, :] for i in range(blocks)]
    lane = lax.broadcasted_iota(jnp.int32, full, 1)
    sub = lax.broadcasted_iota(jnp.int32, full, 0)

    def column(x, k):
        return jnp.broadcast_to(x[:, k : k + 1], full)

    def row(x, k):
        return jnp.broadcast_to(x[k : k + 1, :], full)

    out = []
    own = [column(rows[0], k) for k in range(8)]
    for t in range(blocks):
        base = 8 * t
        here = jnp.logical_and(lane >= base, lane < base + 8)
        s = {(j, k): row(own[k], j) for j in range(8) for k in range(j, 8)}
        c = {}
        for i in range(t + 1, blocks):
            for j in range(8):
                c[i, j] = column(rows[i], base + j)
        last = t + 1 == blocks
        if not last:
            own = [column(rows[t + 1], base + 8 + k) for k in range(8)]
        for i in range(t + 1, blocks):
            rows[i] = jnp.where(here, 0.0, rows[i])
        b = [jnp.where(here, jnp.where(lane == base + j, 1.0, 0.0), row(rows[t], j)) for j in range(8)]
        d = [] if last else [c[t + 1, j] for j in range(8)]
        m = {}
        z = []
        x = jnp.zeros(full, F32)
        for j in range(8):
            r0 = pl.reciprocal(s[j, j], approx=True)
            e = 2.0 - s[j, j] * r0
            r = r0 * e
            for k in range(j + 1, 8):
                m[j, k] = s[j, k] * r
            for k in range(j + 1, 8):
                for l in range(k, 8):
                    if k == j + 1 and l == k:
                        s[k, l] = s[k, l] - ((s[j, k] * s[j, k]) * r0) * e
                    else:
                        s[k, l] = s[k, l] - m[j, k] * s[j, l]
                b[k] = b[k] - m[j, k] * b[j]
            z.append(r * b[j])
            if not last:
                for k in range(j + 1, 8):
                    d[k] = d[k] - m[j, k] * d[j]
                w = d[j] * r
                own = [own[k] - w * row(d[j], k) for k in range(8)]
                rows[t + 1] = rows[t + 1] - d[j] * z[j]
            x = jnp.where(sub == j, lax.rsqrt(s[j, j]) * b[j], x)
        out.append(jnp.where(lane < base + 8, x, 0.0))
        if t + 2 < blocks:
            y = list(z)
            for k in range(7, 0, -1):
                for j in range(k):
                    y[j] = y[j] - m[j, k] * y[k]
            for i in range(t + 2, blocks):
                for j in range(8):
                    rows[i] = rows[i] - c[i, j] * y[j]
    return jnp.concatenate(out, axis=0)


def split(x):
    high = x.astype(BF16)
    return high, (x - high.astype(F32)).astype(BF16)


def scale_row(ref, tile, n):
    tail = ref[n:, :].astype(F32)
    return tail[3 * tile : 3 * tile + 1] + tail[3 * tile + 1 : 3 * tile + 2] + tail[3 * tile + 2 : 3 * tile + 3]


def first_half(tile, inv_ref, low_ref, rest_ref):
    x = inverse_factor(tile[:HALF, :HALF])
    factor = dot_nt(tile[HALF:, :HALF], x, HIGHEST)
    inv_ref[...] = x
    low_ref[...] = factor
    rest_ref[...] = tile[HALF:, HALF:] - dot_nt(factor, factor, HIGHEST)


def second_half(inv_ref, low_ref, rest_ref, out_ref):
    x22 = inverse_factor(rest_ref[...])
    x11 = inv_ref[...]
    x21 = -dot_nn(x22, dot_nn(low_ref[...], x11, HIGHEST), HIGHEST)
    for k, x in enumerate((x11, x21, x22)):
        out_ref[k], out_ref[k + 3] = split(x)


def scale_tail(scales, n):
    row = lax.broadcasted_iota(jnp.int32, (EXTRA, n), 0)
    total = jnp.zeros((EXTRA, n), F32)
    for t in range(scales.shape[0]):
        rest = jnp.full((EXTRA, n), scales[t, 0], F32)
        for k in range(3):
            part = rest.astype(BF16).astype(F32)
            total = jnp.where(row == 3 * t + k, part, total)
            rest = rest - part
    return total.astype(BF16)


def pack_kernel(scales, packed, message, pivot, sem):
    n = pivot.shape[1]
    tall = message.shape[0] - EXTRA
    tile_copy = pltpu.make_async_copy(packed.at[0:n, 0:n], pivot.at[0:n], sem.at[0])
    block_copy = pltpu.make_async_copy(packed.at[:, 0:n], message.at[0:tall], sem.at[1])
    tile_copy.start()
    block_copy.start()
    tail = scale_tail(scales, n)
    pivot[n:, :] = tail
    message[tall:, :] = tail
    tile_copy.wait()
    block_copy.wait()


def take(tiles, mask, target):
    for k, tile in enumerate(tiles):

        @pl.when(mask == 2 * k)
        def _(tile=tile):
            n = target.shape[0]
            target[...] = tile[:n, :].astype(F32) * scale_row(tile, 0, n)


def first_kernel(*refs):
    tiles, out_ref, tile, inv, low, rest = refs[:-5], *refs[-5:]
    take(tiles, lax.axis_index("prow"), tile)
    first_half(tile, inv, low, rest)
    second_half(inv, low, rest, out_ref)


def second_kernel(x0, *refs):
    tiles, out_ref, left, tile, inv, low, rest = refs[:-6], *refs[-6:]
    n = 2 * HALF
    r = lax.axis_index("prow")
    out_ref[0:6] = x0[...]
    take(tiles, r ^ 2, left)
    take(tiles, r ^ 4, tile)
    high, part = split(left[...])
    cat = join(x0, 0)
    both = jnp.concatenate([cat[:, :n], cat[:, :n], cat[:, n:]], axis=1)
    panel = dot_nt(jnp.concatenate([high, part, high], axis=1), both).astype(BF16)
    for k in range(4):
        i, j = divmod(k, 2)
        out_ref[12 + k] = panel[i * HALF : (i + 1) * HALF, j * HALF : (j + 1) * HALF]
    tile[...] = tile[...] - dot_nt(panel, panel)
    first_half(tile, inv, low, rest)
    second_half(inv, low, rest, out_ref.at[6:12])


def join(x, base):
    zero = jnp.zeros((HALF, HALF), BF16)
    upper = jnp.concatenate([x[base], zero, x[base + 3], zero], axis=1)
    lower = jnp.concatenate([x[base + 1], x[base + 2], x[base + 4], x[base + 5]], axis=1)
    return jnp.concatenate([upper, lower], axis=0)


VMEM = pl.BlockSpec(memory_space=pltpu.VMEM)
SMEM = pl.BlockSpec(memory_space=pltpu.SMEM)
HBM = pl.BlockSpec(memory_space=pl.ANY)
BLOCK = jax.ShapeDtypeStruct((HALF, HALF), F32)
PARTS = jax.ShapeDtypeStruct((6, HALF, HALF), BF16)
FACTORS = jax.ShapeDtypeStruct((16, HALF, HALF), BF16)


def factor_call(kernel, name, outs, args, specs=None, scratch=(), work=1):
    return pl.pallas_call(
        kernel,
        out_shape=outs,
        in_specs=specs or [VMEM] * len(args),
        out_specs=(VMEM,) * len(outs),
        scratch_shapes=scratch,
        compiler_params=pltpu.CompilerParams(vmem_limit_bytes=24 << 20),
        cost_estimate=pl.CostEstimate(flops=work * 5_000_000_000, bytes_accessed=1 << 20, transcendentals=0),
        name=name,
    )(*args)


def update_kernel(geometry, scales, packed, *rest):
    ratio, nr, nc, tpr, tpc, n = geometry
    factors, factors_other, cols_here, cols_other, mine, relayed = rest[0], rest[1], rest[2:4], rest[4:6], rest[6], rest[7]
    out, block, rowp, colp, rowl, xs, sem = rest[8:]
    step = pl.program_id(0)
    r = lax.axis_index("prow")
    c = lax.axis_index("pcol")
    late = jnp.logical_and(nc == 4, jnp.where(r % 4 == 3, c == 2, c == 3))
    tall = tpr * n

    def scale_column(slot, panel):
        tail = block[slot, panel, tall:, :].astype(F32)
        rows = []
        for t in range(tpr):
            s = tail[3 * t : 3 * t + 1, :1] + tail[3 * t + 1 : 3 * t + 2, :1] + tail[3 * t + 2 : 3 * t + 3, :1]
            rows.append(jnp.broadcast_to(s, (n, 1)))
        return jnp.concatenate(rows, axis=0)

    def solve(slot, cat0, cat1, panel):
        a0 = block[slot, 0, :tall, :]
        s0 = scale_column(slot, 0)
        s1 = scale_column(slot, 1)
        raw0 = dot_nn(jnp.concatenate([a0, a0], axis=1), cat0)
        p0 = (raw0 * s0).astype(BF16)
        rest = block[slot, 1, :tall, :].astype(F32) * s1 - dot_nn(p0, panel)
        high, low = split(rest)
        f1 = dot_nn(jnp.concatenate([high, low, high], axis=1), cat1)
        return raw0, f1, s1, p0, f1.astype(BF16)

    @pl.when(step == 0)
    def _():
        def fetch(choice, here, there, target, k):
            @pl.when(choice)
            def _():
                pltpu.make_async_copy(here, target, sem.at[k]).start()

            @pl.when(jnp.logical_not(choice))
            def _():
                pltpu.make_async_copy(there, target, sem.at[k]).start()

        fetch(r % 2 == 0, factors, factors_other, xs, 3)
        for k in range(2):
            fetch((r % 2) == (c % 2), cols_here[k], cols_other[k], block.at[k], k)
        fetch(late, relayed, mine, block.at[2], 2)
        pltpu.make_async_copy(factors, xs, sem.at[3]).wait()
        cat0 = join(xs, 0).T
        cat1 = join(xs, 6).T
        cat1 = jnp.concatenate([cat1[:n], cat1[:n], cat1[n:]], axis=0)
        panel = jnp.concatenate(
            [jnp.concatenate([xs[12], xs[13]], axis=1), jnp.concatenate([xs[14], xs[15]], axis=1)], axis=0
        ).T
        for k in range(2):
            pltpu.make_async_copy(mine, block.at[k], sem.at[k]).wait()
            _, _, _, p0, p1 = solve(k, cat0, cat1, panel)
            for t in range(tpr):
                q = t * ratio + k
                colp[q, :n, :] = p0[t * n : (t + 1) * n].T
                colp[q, n:, :] = p1[t * n : (t + 1) * n].T
        pltpu.make_async_copy(mine, block.at[2], sem.at[2]).wait()
        raw0, f1, s1, p0, p1 = solve(2, cat0, cat1, panel)
        for t in range(tpr):
            rowp[t, :, :n] = p0[t * n : (t + 1) * n]
            rowp[t, :, n:] = p1[t * n : (t + 1) * n]

        @pl.when(c == 0)
        def _():
            rowl[...] = raw0

        @pl.when(c == 1)
        def _():
            rowl[...] = f1 / s1

    true_row = step * nr + r
    left = rowp[step]
    for q in range(tpc):
        true_col = q * nc + c
        cols = slice(q * n, (q + 1) * n)
        s = scales[step, q]

        @pl.when(true_row < true_col)
        def _(cols=cols):
            out[:, cols] = packed[:, cols]

        @pl.when(jnp.logical_and(true_row >= true_col, true_col >= 2))
        def _(cols=cols, s=s, q=q):
            change = dot_nn(left, colp[q])
            out[:, cols] = (packed[:, cols].astype(F32) - change * (1.0 / s)).astype(BF16)

        if q * nc < 2:

            @pl.when(jnp.logical_and(true_row >= true_col, true_col < 2))
            def _(cols=cols):
                row = lax.broadcasted_iota(jnp.int32, (n, n), 0)
                col = lax.broadcasted_iota(jnp.int32, (n, n), 1)
                keep = jnp.logical_or(row >= col, true_row != true_col)
                f = rowl[pl.ds(pl.multiple_of(step * n, n), n), :]
                out[:, cols] = jnp.where(keep, f, 0.0).astype(BF16)


def update(scales, packed, blocks, nr, nc, tpr, tpc, n):
    geometry = (nr // nc, nr, nc, tpr, tpc, n)
    tall = blocks[-1].shape[1]
    return pl.pallas_call(
        functools.partial(update_kernel, geometry),
        grid=(tpr,),
        out_shape=jax.ShapeDtypeStruct(packed.shape, BF16),
        in_specs=[SMEM, pl.BlockSpec((n, tpc * n), lambda i: (i, 0))] + [HBM] * len(blocks),
        out_specs=pl.BlockSpec((n, tpc * n), lambda i: (i, 0)),
        scratch_shapes=[
            pltpu.VMEM((3, 2, tall, n), BF16),
            pltpu.VMEM((tpr, n, 2 * n), BF16),
            pltpu.VMEM((tpc, 2 * n, n), BF16),
            pltpu.VMEM((tpr * n, n), F32),
            pltpu.VMEM(FACTORS.shape, BF16),
            pltpu.SemaphoreType.DMA((4,)),
        ],
        compiler_params=pltpu.CompilerParams(vmem_limit_bytes=48 << 20),
        cost_estimate=pl.CostEstimate(flops=4_000_000_000, bytes_accessed=8 << 20, transcendentals=0),
        name="update_tiles",
    )(scales, packed, *blocks)


def on_device(nr, nc, packed, tile_scales):
    tpr, tpc = tile_scales.shape
    n = packed.shape[0] // tpr
    r = lax.axis_index("prow")
    c = lax.axis_index("pcol")
    def send(x, pairs):
        table = [(a * nc + b, d * nc + e) for (a, b), (d, e) in pairs]
        return lax.ppermute(x, ("prow", "pcol"), table)

    message, pivot = pl.pallas_call(
        pack_kernel,
        out_shape=(jax.ShapeDtypeStruct((tpr * n + EXTRA, n), BF16), jax.ShapeDtypeStruct((n + EXTRA, n), BF16)),
        in_specs=[SMEM, HBM],
        out_specs=(VMEM,) * 2,
        scratch_shapes=[pltpu.SemaphoreType.DMA((2,))],
        compiler_params=pltpu.CompilerParams(vmem_limit_bytes=48 << 20),
        name="pack_panel",
    )(tile_scales, packed)

    came = []
    for k in range(nc):
        pairs = [((1, 0), (2, k)), ((1, 1), (4, (k + 1) % nc))]
        came.append(send(pivot, pairs + [((0, 0), (0, k))] * (k > 0)))
    index = jnp.where(r == 4, (c + nc - 1) % nc, c)
    tile = jnp.where((r == 0) & (c == 0), pivot, came[0])
    for k in range(1, nc):
        tile = jnp.where(index == k, came[k], tile)
    tiles = [tile]
    for mask in range(2, nr, 2):
        tiles.append(send(tile, [((a, e), (a ^ mask, e)) for a in (0, 2, 4) for e in range(nc)]))
    blank = pltpu.VMEM((HALF, HALF), F32)
    whole = pltpu.VMEM((n, n), F32)
    (x0,) = factor_call(first_kernel, "factor_first", (PARTS,), tuple(tiles), None, [whole] + [blank] * 3, 2)

    u = r % nc
    if nc == 4:
        first = {0: [(1, 0), (0, 2)], 1: [(0, 1), (1, 2)], 2: [(1, 2), (0, 1)], 3: [(1, 3), (0, 1)]}
        second = {0: [(1, 2), (0, 1)], 1: [(0, 2), (1, 0)], 2: [(0, 2), (1, 0)], 3: [(0, 3), (1, 0)]}
        turns = [[((a, x), (a, y)) for a in range(nr) for x, y in t[a % 4]] for t in (first, second)]
        got = [send(message, turn) for turn in turns]
        *got, _ = lax.optimization_barrier((*got, x0))
        swap = (u == 0) == (c >= 2)
        m0 = jnp.where(c == 0, message, jnp.where(swap, got[0], got[1]))
        m0 = jnp.where(c == 1, jnp.where(u == 0, got[1], got[0]), m0)
        m1 = jnp.where(c == 1, message, jnp.where(swap, got[1], got[0]))
        m1 = jnp.where(c == 0, jnp.where(u == 0, got[0], got[1]), m1)
        mine = jnp.stack([m0, m1])
        relayed = send(mine, [((a, 3), (a, 2)) if a % 4 == 3 else ((a, 2), (a, 3)) for a in range(nr)])
    else:
        m0 = message
        m1 = jnp.where(c == 1, message, 0)
        for k in range(1, nc):
            m0 = jnp.where(c == k, send(message, [((a, 0), (a, k)) for a in range(nr)]), m0)
        for k in range(nc):
            if k != 1:
                m1 = jnp.where(c == k, send(message, [((a, 1), (a, k)) for a in range(nr)]), m1)
        mine = jnp.stack([m0, m1])
        relayed = mine

    ratio = nr // nc
    near = []
    for mask in range(2, nr, 2):
        pairs = [((e + nc * g, e), ((e + nc * g) ^ mask, e)) for e in range(nc) for g in range(ratio)]
        near.append(send(mine, pairs))
    scratch = [whole] * 2 + [blank] * 3
    (factors,) = factor_call(second_kernel, "factor_second", (FACTORS,), (x0, *tiles), None, scratch, 2)
    factors_other = send(factors, [((a, e), (a + 1, e)) for a in range(0, nr, 2) for e in range(nc)])
    *near, _ = lax.optimization_barrier((*near, factors))
    cols = [mine] * ratio
    for k, got in enumerate(near):
        cols = [jnp.where((r ^ (c + nc * g)) // 2 == k + 1, got, cols[g]) for g in range(ratio)]
    pairs = [((a, e), (a ^ 1, e)) for a in range(nr) for e in range(nc) if a % 2 == e % 2]
    cols_other = [send(x, pairs) for x in cols]
    blocks = (factors, factors_other, *cols, *cols_other, mine, relayed)
    return update(tile_scales, packed, blocks, nr, nc, tpr, tpc, n)


def solution(mesh):
    nr = mesh.shape["prow"]
    nc = mesh.shape["pcol"]
    return jax.shard_map(
        functools.partial(on_device, nr, nc),
        mesh=mesh,
        in_specs=(P("prow", "pcol"), P("prow", "pcol")),
        out_specs=P("prow", "pcol"),
        check_vma=False,
    )
```

```python
import functools

import jax
import jax.numpy as jnp
import numpy as np
from jax import lax
from jax.experimental import pallas as pl
from jax.experimental.pallas import tpu as pltpu
from jax.sharding import PartitionSpec as P

F32 = jnp.float32
BF16 = jnp.bfloat16
HALF = 128
EXTRA = 16


def dot_nt(a, b, precision=None):
    dims = (((1,), (1,)), ((), ()))
    return lax.dot_general(a, b, dims, precision=precision, preferred_element_type=F32)


def dot_nn(a, b, precision=None):
    dims = (((1,), (0,)), ((), ()))
    return lax.dot_general(a, b, dims, precision=precision, preferred_element_type=F32)


HIGHEST = lax.Precision.HIGHEST


def inverse_factor(a):
    n = a.shape[0]
    blocks = n // 8
    full = (8, n)
    rows = [a[8 * i : 8 * i + 8, :] for i in range(blocks)]
    lane = lax.broadcasted_iota(jnp.int32, full, 1)
    sub = lax.broadcasted_iota(jnp.int32, full, 0)

    def column(x, k):
        return jnp.broadcast_to(x[:, k : k + 1], full)

    def row(x, k):
        return jnp.broadcast_to(x[k : k + 1, :], full)

    out = []
    own = [column(rows[0], k) for k in range(8)]
    for t in range(blocks):
        base = 8 * t
        here = jnp.logical_and(lane >= base, lane < base + 8)
        s = {(j, k): row(own[k], j) for j in range(8) for k in range(j, 8)}
        c = {}
        for i in range(t + 1, blocks):
            for j in range(8):
                c[i, j] = column(rows[i], base + j)
        last = t + 1 == blocks
        if not last:
            own = [column(rows[t + 1], base + 8 + k) for k in range(8)]
        for i in range(t + 1, blocks):
            rows[i] = jnp.where(here, 0.0, rows[i])
        b = [jnp.where(here, jnp.where(lane == base + j, 1.0, 0.0), row(rows[t], j)) for j in range(8)]
        d = [] if last else [c[t + 1, j] for j in range(8)]
        m = {}
        z = []
        x = jnp.zeros(full, F32)
        for j in range(8):
            r0 = pl.reciprocal(s[j, j], approx=True)
            e = 2.0 - s[j, j] * r0
            r = r0 * e
            for k in range(j + 1, 8):
                m[j, k] = s[j, k] * r
            for k in range(j + 1, 8):
                for l in range(k, 8):
                    if k == j + 1 and l == k:
                        s[k, l] = s[k, l] - ((s[j, k] * s[j, k]) * r0) * e
                    else:
                        s[k, l] = s[k, l] - m[j, k] * s[j, l]
                b[k] = b[k] - m[j, k] * b[j]
            z.append(r * b[j])
            if not last:
                for k in range(j + 1, 8):
                    d[k] = d[k] - m[j, k] * d[j]
                w = d[j] * r
                own = [own[k] - w * row(d[j], k) for k in range(8)]
                rows[t + 1] = rows[t + 1] - d[j] * z[j]
            x = jnp.where(sub == j, lax.rsqrt(s[j, j]) * b[j], x)
        out.append(jnp.where(lane < base + 8, x, 0.0))
        if t + 2 < blocks:
            y = list(z)
            for k in range(7, 0, -1):
                for j in range(k):
                    y[j] = y[j] - m[j, k] * y[k]
            for i in range(t + 2, blocks):
                for j in range(8):
                    rows[i] = rows[i] - c[i, j] * y[j]
    return jnp.concatenate(out, axis=0)


def split(x):
    high = x.astype(BF16)
    return high, (x - high.astype(F32)).astype(BF16)


def scale_row(ref, tile, n):
    tail = ref[n:, :].astype(F32)
    return tail[3 * tile : 3 * tile + 1] + tail[3 * tile + 1 : 3 * tile + 2] + tail[3 * tile + 2 : 3 * tile + 3]


def first_half(tile, inv_ref, low_ref, rest_ref):
    x = inverse_factor(tile[:HALF, :HALF])
    factor = dot_nt(tile[HALF:, :HALF], x, HIGHEST)
    inv_ref[...] = x
    low_ref[...] = factor
    rest_ref[...] = tile[HALF:, HALF:] - dot_nt(factor, factor, HIGHEST)


def second_half(inv_ref, low_ref, rest_ref, out_ref):
    x22 = inverse_factor(rest_ref[...])
    x11 = inv_ref[...]
    x21 = -dot_nn(x22, dot_nn(low_ref[...], x11, HIGHEST), HIGHEST)
    for k, x in enumerate((x11, x21, x22)):
        out_ref[k], out_ref[k + 3] = split(x)


def scale_tail(scales, n):
    row = lax.broadcasted_iota(jnp.int32, (EXTRA, n), 0)
    total = jnp.zeros((EXTRA, n), F32)
    for t in range(scales.shape[0]):
        rest = jnp.full((EXTRA, n), scales[t, 0], F32)
        for k in range(3):
            part = rest.astype(BF16).astype(F32)
            total = jnp.where(row == 3 * t + k, part, total)
            rest = rest - part
    return total.astype(BF16)


def pack_kernel(scales, packed, message, pivot, sem):
    n = pivot.shape[1]
    tall = message.shape[0] - EXTRA
    tile_copy = pltpu.make_async_copy(packed.at[0:n, 0:n], pivot.at[0:n], sem.at[0])
    block_copy = pltpu.make_async_copy(packed.at[:, 0:n], message.at[0:tall], sem.at[1])
    tile_copy.start()
    block_copy.start()
    tail = scale_tail(scales, n)
    pivot[n:, :] = tail
    message[tall:, :] = tail
    tile_copy.wait()
    block_copy.wait()


def take(tiles, mask, target):
    for k, tile in enumerate(tiles):

        @pl.when(mask == 2 * k)
        def _(tile=tile):
            n = target.shape[0]
            target[...] = tile[:n, :].astype(F32) * scale_row(tile, 0, n)


def first_kernel(pivot, out_ref, inv, low, rest):
    n = pivot.shape[1]
    first_half(pivot[:n, :].astype(F32) * scale_row(pivot, 0, n), inv, low, rest)
    second_half(inv, low, rest, out_ref)


def second_kernel(x0, *refs):
    tiles, out_ref, left, tile, inv, low, rest = refs[:-6], *refs[-6:]
    n = 2 * HALF
    r = lax.axis_index("prow")
    out_ref[0:6] = x0[...]
    take(tiles, r ^ 2, left)
    take(tiles, r ^ 4, tile)
    high, part = split(left[...])
    cat = join(x0, 0)
    both = jnp.concatenate([cat[:, :n], cat[:, :n], cat[:, n:]], axis=1)
    panel = dot_nt(jnp.concatenate([high, part, high], axis=1), both).astype(BF16)
    for k in range(4):
        i, j = divmod(k, 2)
        out_ref[12 + k] = panel[i * HALF : (i + 1) * HALF, j * HALF : (j + 1) * HALF]
    tile[...] = tile[...] - dot_nt(panel, panel)
    first_half(tile, inv, low, rest)
    second_half(inv, low, rest, out_ref.at[6:12])


def join(x, base):
    zero = jnp.zeros((HALF, HALF), BF16)
    upper = jnp.concatenate([x[base], zero, x[base + 3], zero], axis=1)
    lower = jnp.concatenate([x[base + 1], x[base + 2], x[base + 4], x[base + 5]], axis=1)
    return jnp.concatenate([upper, lower], axis=0)


VMEM = pl.BlockSpec(memory_space=pltpu.VMEM)
SMEM = pl.BlockSpec(memory_space=pltpu.SMEM)
HBM = pl.BlockSpec(memory_space=pltpu.HBM)
BLOCK = jax.ShapeDtypeStruct((HALF, HALF), F32)
PARTS = jax.ShapeDtypeStruct((6, HALF, HALF), BF16)
FACTORS = jax.ShapeDtypeStruct((16, HALF, HALF), BF16)


def factor_call(kernel, name, outs, args, specs=None, scratch=(), work=1):
    return pl.pallas_call(
        kernel,
        out_shape=outs,
        in_specs=specs or [VMEM] * len(args),
        out_specs=(VMEM,) * len(outs),
        scratch_shapes=scratch,
        compiler_params=pltpu.CompilerParams(vmem_limit_bytes=24 << 20),
        cost_estimate=pl.CostEstimate(flops=work * 5_000_000_000, bytes_accessed=1 << 20, transcendentals=0),
        name=name,
    )(*args)


def update_kernel(geometry, table, scales, packed, factors, factors_other, *rest):
    ratio, nr, nc, tpr, tpc, n, count = geometry
    here = (rest[0:2], rest[2:4])
    there = (rest[4:6], rest[6:8])
    blocks = rest[8 : 8 + count]
    out, stored, result, block, rowp, colp, rowl, xs, sem = rest[8 + count :]
    r = lax.axis_index("prow")
    c = lax.axis_index("pcol")
    tall = tpr * n

    reads = [pltpu.make_async_copy(packed.at[t * n : (t + 1) * n], stored.at[t], sem.at[0, t]) for t in range(tpr)]
    writes = [pltpu.make_async_copy(result.at[t], out.at[t * n : (t + 1) * n], sem.at[1, t]) for t in range(tpr)]
    for copy in reads:
        copy.start()

    def when(condition, target, value):
        @pl.when(condition)
        def _():
            target[...] = value[...]

    when(r % 2 == 0, xs, factors)
    when(r % 2 == 1, xs, factors_other)
    cat0 = join(xs, 0).T
    cat1 = join(xs, 6).T
    cat1 = jnp.concatenate([cat1[:n], cat1[:n], cat1[n:]], axis=0)
    panel = jnp.concatenate(
        [jnp.concatenate([xs[12], xs[13]], axis=1), jnp.concatenate([xs[14], xs[15]], axis=1)], axis=0
    ).T

    def solve(each):
        for t in range(tpr):
            rows = slice(t * n, (t + 1) * n)
            a0 = block[0, rows, :]
            raw0 = dot_nn(jnp.concatenate([a0, a0], axis=1), cat0)
            p0 = (raw0 * scale_row(block[0], t, tall)).astype(BF16)
            s1 = scale_row(block[1], t, tall)
            left = block[1, rows, :].astype(F32) * s1 - dot_nn(p0, panel)
            high, low = split(left)
            f1 = dot_nn(jnp.concatenate([high, low, high], axis=1), cat1)
            each(t, raw0, f1, s1, p0, f1.astype(BF16))

    same = (r % 2) == (c % 2)
    early = jnp.where(c < 2, 0, 1)
    for g in range(ratio):
        for half, panel_index in enumerate((early, 1 - early)):
            target = block.at[panel_index]
            when(same, target, here[half][g])
            when(jnp.logical_not(same), target, there[half][g])

        def keep_column(t, raw0, f1, s1, p0, p1, g=g):
            colp[t * ratio + g, :n, :] = p0.T
            colp[t * ratio + g, n:, :] = p1.T

        solve(keep_column)

    for panel_index in range(2):
        index = table[2 * (r * nc + c) + panel_index]
        for k in range(count):
            when(index == k, block.at[panel_index], blocks[k])

    def keep_row(t, raw0, f1, s1, p0, p1):
        rowp[t, :, :n] = p0
        rowp[t, :, n:] = p1

        @pl.when(c == 0)
        def _():
            rowl[t] = raw0

        @pl.when(c == 1)
        def _():
            rowl[t] = f1 / s1

    solve(keep_row)

    for t in range(tpr):
        reads[t].wait()
        true_row = t * nr + r
        for q in range(tpc):
            true_col = q * nc + c
            cols = slice(q * n, (q + 1) * n)

            @pl.when(true_row < true_col)
            def _():
                result[t, :, cols] = stored[t, :, cols]

            @pl.when(jnp.logical_and(true_row >= true_col, true_col >= 2))
            def _():
                change = dot_nn(rowp[t], colp[q])
                inverse = 1.0 / jnp.full((1, n), scales[t, q], F32)
                result[t, :, cols] = (stored[t, :, cols].astype(F32) - change * inverse).astype(BF16)

            if q * nc < 2:

                @pl.when(jnp.logical_and(true_row >= true_col, true_col < 2))
                def _():
                    row = lax.broadcasted_iota(jnp.int32, (n, n), 0)
                    col = lax.broadcasted_iota(jnp.int32, (n, n), 1)
                    keep = jnp.logical_or(row >= col, true_row != true_col)
                    result[t, :, cols] = jnp.where(keep, rowl[t], 0.0).astype(BF16)

        writes[t].start()
    for copy in writes:
        copy.wait()


def update(table, scales, packed, arrays, blocks, nr, nc, tpr, tpc, n):
    geometry = (nr // nc, nr, nc, tpr, tpc, n, len(blocks))
    tall = blocks[0].shape[0]
    return pl.pallas_call(
        functools.partial(update_kernel, geometry),
        out_shape=jax.ShapeDtypeStruct(packed.shape, BF16),
        in_specs=[SMEM, SMEM, HBM] + [VMEM] * (len(arrays) + len(blocks)),
        out_specs=HBM,
        scratch_shapes=[
            pltpu.VMEM((tpr, n, tpc * n), BF16),
            pltpu.VMEM((tpr, n, tpc * n), BF16),
            pltpu.VMEM((2, tall, n), BF16),
            pltpu.VMEM((tpr, n, 2 * n), BF16),
            pltpu.VMEM((tpc, 2 * n, n), BF16),
            pltpu.VMEM((tpr, n, n), F32),
            pltpu.VMEM(FACTORS.shape, BF16),
            pltpu.SemaphoreType.DMA((2, tpr)),
        ],
        compiler_params=pltpu.CompilerParams(vmem_limit_bytes=40 << 20),
        cost_estimate=pl.CostEstimate(flops=4_000_000_000, bytes_accessed=8 << 20, transcendentals=0),
        name="update_tiles",
    )(table, scales, packed, *arrays, *blocks)


def row_plan(nr, nc):
    if (nr, nc) == (8, 4):
        first = {0: [(1, 2)], 1: [(0, 1), (1, 2)], 4: [(1, 0), (0, 2)], 5: [(0, 1), (1, 2)]}
        second = {0: [(0, 1), (1, 0)], 1: [(1, 0)], 4: [(1, 2), (0, 1)], 5: [(0, 2), (1, 0)]}
        third = {0: [(1, 2, 2), (2, 3, 1)], 1: [(1, 2, 1), (2, 3, 1)], 4: [(2, 3, 2)], 5: [(2, 3, 1)]}
        fourth = {0: [(2, 3, 3)], 1: [(2, 3, 3)], 4: [(2, 3, 1)], 5: [(2, 3, 2)]}
        for r in (2, 6, 3, 7):
            u = r % 4
            first[r] = [(1, u), (0, 1)]
            second[r] = [(0, u), (1, 0)]
            third[r] = [(u, 5 - u, 1)]
            fourth[r] = [(u, 5 - u, 2)]
        turns = (first, second, third, fourth)
        return [[(r, *move[:2], move[2] if len(move) > 2 else 0) for r in turn for move in turn[r]] for turn in turns]
    rounds = [[], []]
    for r in range(nr):
        want = r % nc
        rounds[0].append((r, 0, 1, 0) if want == 1 else (r, 1, want, 0))
        if want > 1:
            rounds[1].append((r, 0, want, 0))
    done = {move[:3] for turn in rounds for move in turn}
    for shift in range(1, nc):
        moves = [(r, a, (a + shift) % nc, 0) for r in range(nr) for a in range(2)]
        rounds.append([move for move in moves if move[:3] not in done])
    return rounds


def on_device(nr, nc, packed, tile_scales):
    tpr, tpc = tile_scales.shape
    n = packed.shape[0] // tpr
    r = lax.axis_index("prow")
    c = lax.axis_index("pcol")
    def choose(options, index):
        value = options[0]
        for k in range(1, len(options)):
            value = jnp.where(index == k, options[k], value)
        return value

    def send(x, pairs):
        table = [(a * nc + b, d * nc + e) for (a, b), (d, e) in pairs]
        return lax.ppermute(x, ("prow", "pcol"), table)

    message, pivot = pl.pallas_call(
        pack_kernel,
        out_shape=(jax.ShapeDtypeStruct((tpr * n + EXTRA, n), BF16), jax.ShapeDtypeStruct((n + EXTRA, n), BF16)),
        in_specs=[SMEM, HBM],
        out_specs=(VMEM,) * 2,
        scratch_shapes=[pltpu.SemaphoreType.DMA((2,))],
        compiler_params=pltpu.CompilerParams(vmem_limit_bytes=48 << 20),
        name="pack_panel",
    )(tile_scales, packed)

    came = [send(pivot, [((1, 0), (2, k)), ((1, 1), (4, (k + 1) % nc))]) for k in range(nc)]
    index = jnp.where(r == 4, (c + nc - 1) % nc, c)
    *came, own = lax.optimization_barrier((*came, pivot))

    blank = [pltpu.VMEM((HALF, HALF), F32)] * 3
    whole = [pltpu.VMEM((n, n), F32)] * 2
    (x0,) = factor_call(first_kernel, "factor_first", (PARTS,), (own,), None, blank, 2)

    rounds = row_plan(nr, nc)
    blocks = [message]
    holds = {(a, p, p): 0 for a in range(nr) for p in range(2)}

    def send_round(turn):
        used = sorted({k for *_, k in turn})
        operand = blocks[used[0]]
        for k in used[1:]:
            hits = [r * nc + c == a * nc + b for a, b, _, j in turn if j == k]
            operand = jnp.where(functools.reduce(jnp.logical_or, hits), blocks[k], operand)
        for a, b, d, k in turn:
            panel = next(p for p in range(2) if holds.get((a, b, p)) == k)
            holds[a, d, panel] = len(blocks)
        blocks.append(send(operand, [((a, b), (a, d)) for a, b, d, _ in turn]))

    send_round(rounds[0])
    send_round(rounds[1])

    x0, first = lax.optimization_barrier((x0, blocks[1]))
    x0 = choose([x0] + [send(x0, [((0, 0), (0, k))]) for k in range(1, nc)], c)
    got = [send(x0, [((0, e), (mask, e)) for e in range(nc)]) for mask in range(2, nr, 2)]
    x0 = choose([x0] + got, r // 2)
    tile = choose(came, index)
    tiles = [tile]
    for mask in range(2, nr, 2):
        tiles.append(send(tile, [((a, e), (a ^ mask, e)) for a in (2, 4) for e in range(nc)]))

    ratio = nr // nc
    part = [jnp.where(c == 0, message, first)]
    message, late, _ = lax.optimization_barrier((message, blocks[2], x0))
    blocks[2] = late
    own_late = blocks[1] if (nr, nc) != (8, 4) else jnp.where(r == 0, late, blocks[1])
    part.append(jnp.where(c == 0, own_late, jnp.where(c == 1, message, late)))
    near = []
    for x in part:
        got = []
        for mask in range(2, nr, 2):
            pairs = [((e + nc * g, e), ((e + nc * g) ^ mask, e)) for e in range(nc) for g in range(ratio)]
            got.append(send(x, pairs))
        near.append(got)
    for turn in rounds[2:]:
        send_round(turn)

    (factors,) = factor_call(second_kernel, "factor_second", (FACTORS,), (x0, *tiles), None, whole + blank, 2)
    factors_other = send(factors, [((a, e), (a + 1, e)) for a in range(0, nr, 2) for e in range(nc)])

    *near[1], _ = lax.optimization_barrier((*near[1], factors))
    pairs = [((a, e), (a ^ 1, e)) for a in range(nr) for e in range(nc) if a % 2 == e % 2]
    cols = []
    for x, got in zip(part, near):
        for g in range(ratio):
            cols.append(choose([x] + got, (r ^ (c + nc * g)) // 2))
    cols_other = [send(x, pairs) for x in cols]
    table = np.array([holds[a, b, p] for a in range(nr) for b in range(nc) for p in range(2)], np.int32)
    return update(table, tile_scales, packed, (factors, factors_other, *cols, *cols_other), blocks, nr, nc, tpr, tpc, n)


def solution(mesh):
    nr = mesh.shape["prow"]
    nc = mesh.shape["pcol"]
    return jax.shard_map(
        functools.partial(on_device, nr, nc),
        mesh=mesh,
        in_specs=(P("prow", "pcol"), P("prow", "pcol")),
        out_specs=P("prow", "pcol"),
        check_vma=False,
    )
```

```python
import functools

import jax
import jax.numpy as jnp
import numpy as np
from jax import lax
from jax.experimental import pallas as pl
from jax.experimental.pallas import tpu as pltpu
from jax.sharding import PartitionSpec as P

F32 = jnp.float32
BF16 = jnp.bfloat16
HALF = 128
EXTRA = 16


def dot_nt(a, b, precision=None):
    dims = (((1,), (1,)), ((), ()))
    return lax.dot_general(a, b, dims, precision=precision, preferred_element_type=F32)


def dot_nn(a, b, precision=None):
    dims = (((1,), (0,)), ((), ()))
    return lax.dot_general(a, b, dims, precision=precision, preferred_element_type=F32)


HIGHEST = lax.Precision.HIGHEST


def inverse_factor(a):
    n = a.shape[0]
    blocks = n // 8
    full = (8, n)
    rows = [a[8 * i : 8 * i + 8, :] for i in range(blocks)]
    lane = lax.broadcasted_iota(jnp.int32, full, 1)
    sub = lax.broadcasted_iota(jnp.int32, full, 0)

    def column(x, k):
        return jnp.broadcast_to(x[:, k : k + 1], full)

    def row(x, k):
        return jnp.broadcast_to(x[k : k + 1, :], full)

    out = []
    own = [column(rows[0], k) for k in range(8)]
    for t in range(blocks):
        base = 8 * t
        here = jnp.logical_and(lane >= base, lane < base + 8)
        s = {(j, k): row(own[k], j) for j in range(8) for k in range(j, 8)}
        c = {}
        for i in range(t + 1, blocks):
            for j in range(8):
                c[i, j] = column(rows[i], base + j)
        last = t + 1 == blocks
        if not last:
            own = [column(rows[t + 1], base + 8 + k) for k in range(8)]
        for i in range(t + 1, blocks):
            rows[i] = jnp.where(here, 0.0, rows[i])
        b = [jnp.where(here, jnp.where(lane == base + j, 1.0, 0.0), row(rows[t], j)) for j in range(8)]
        d = [] if last else [c[t + 1, j] for j in range(8)]
        m = {}
        z = []
        x = jnp.zeros(full, F32)
        for j in range(8):
            r0 = pl.reciprocal(s[j, j], approx=True)
            e = 2.0 - s[j, j] * r0
            r = r0 * e
            for k in range(j + 1, 8):
                m[j, k] = s[j, k] * r
            for k in range(j + 1, 8):
                for l in range(k, 8):
                    if k == j + 1 and l == k:
                        s[k, l] = s[k, l] - ((s[j, k] * s[j, k]) * r0) * e
                    else:
                        s[k, l] = s[k, l] - m[j, k] * s[j, l]
                b[k] = b[k] - m[j, k] * b[j]
            z.append(r * b[j])
            if not last:
                for k in range(j + 1, 8):
                    d[k] = d[k] - m[j, k] * d[j]
                w = d[j] * r
                own = [own[k] - w * row(d[j], k) for k in range(8)]
                rows[t + 1] = rows[t + 1] - d[j] * z[j]
            x = jnp.where(sub == j, lax.rsqrt(s[j, j]) * b[j], x)
        out.append(jnp.where(lane < base + 8, x, 0.0))
        if t + 2 < blocks:
            y = list(z)
            for k in range(7, 0, -1):
                for j in range(k):
                    y[j] = y[j] - m[j, k] * y[k]
            for i in range(t + 2, blocks):
                for j in range(8):
                    rows[i] = rows[i] - c[i, j] * y[j]
    return jnp.concatenate(out, axis=0)


def split(x):
    high = x.astype(BF16)
    return high, (x - high.astype(F32)).astype(BF16)


def scale_row(ref, tile, n):
    tail = ref[n:, :].astype(F32)
    return tail[3 * tile : 3 * tile + 1] + tail[3 * tile + 1 : 3 * tile + 2] + tail[3 * tile + 2 : 3 * tile + 3]


def first_half(tile, inv_ref, low_ref, rest_ref):
    x = inverse_factor(tile[:HALF, :HALF])
    factor = dot_nt(tile[HALF:, :HALF], x, HIGHEST)
    inv_ref[...] = x
    low_ref[...] = factor
    rest_ref[...] = tile[HALF:, HALF:] - dot_nt(factor, factor, HIGHEST)


def second_half(inv_ref, low_ref, rest_ref, out_ref):
    x22 = inverse_factor(rest_ref[...])
    x11 = inv_ref[...]
    x21 = -dot_nn(x22, dot_nn(low_ref[...], x11, HIGHEST), HIGHEST)
    for k, x in enumerate((x11, x21, x22)):
        out_ref[k], out_ref[k + 3] = split(x)


def scale_tail(scales, n):
    row = lax.broadcasted_iota(jnp.int32, (EXTRA, n), 0)
    total = jnp.zeros((EXTRA, n), F32)
    for t in range(scales.shape[0]):
        rest = jnp.full((EXTRA, n), scales[t, 0], F32)
        for k in range(3):
            part = rest.astype(BF16).astype(F32)
            total = jnp.where(row == 3 * t + k, part, total)
            rest = rest - part
    return total.astype(BF16)


def start_kernel(scales, packed, message, pivot, x0_ref, inv, low, rest, sem):
    n = pivot.shape[1]
    tall = message.shape[0] - EXTRA
    tile_copy = pltpu.make_async_copy(packed.at[0:n, 0:n], pivot.at[0:n], sem.at[0])
    block_copy = pltpu.make_async_copy(packed.at[:, 0:n], message.at[0:tall], sem.at[1])
    tile_copy.start()
    block_copy.start()
    tail = scale_tail(scales, n)
    pivot[n:, :] = tail
    message[tall:, :] = tail
    tile_copy.wait()
    block_copy.wait()

    @pl.when(jnp.logical_and(lax.axis_index("prow") == 0, lax.axis_index("pcol") == 0))
    def _():
        first_half(pivot[:n, :].astype(F32) * scale_row(pivot, 0, n), inv, low, rest)
        second_half(inv, low, rest, x0_ref)


def second_kernel(x0, pair, out_ref, inv, low, rest):
    n = 2 * HALF

    @pl.when(lax.axis_index("prow") % 2 == 0)
    def _():
        out_ref[0:6] = x0[...]
        a = pair[0, :n, :]
        solved = dot_nt(jnp.concatenate([a, a], axis=1), join(x0, 0)) * scale_row(pair[0], 0, n)
        panel = solved.astype(BF16)
        for k in range(4):
            i, j = divmod(k, 2)
            out_ref[12 + k] = panel[i * HALF : (i + 1) * HALF, j * HALF : (j + 1) * HALF]
        tile = pair[1, :n, :].astype(F32) * scale_row(pair[1], 0, n) - dot_nt(panel, panel)
        first_half(tile, inv, low, rest)
        second_half(inv, low, rest, out_ref.at[6:12])


def join(x, base):
    zero = jnp.zeros((HALF, HALF), BF16)
    upper = jnp.concatenate([x[base], zero, x[base + 3], zero], axis=1)
    lower = jnp.concatenate([x[base + 1], x[base + 2], x[base + 4], x[base + 5]], axis=1)
    return jnp.concatenate([upper, lower], axis=0)


VMEM = pl.BlockSpec(memory_space=pltpu.VMEM)
SMEM = pl.BlockSpec(memory_space=pltpu.SMEM)
HBM = pl.BlockSpec(memory_space=pltpu.HBM)
BLOCK = jax.ShapeDtypeStruct((HALF, HALF), F32)
PARTS = jax.ShapeDtypeStruct((6, HALF, HALF), BF16)
FACTORS = jax.ShapeDtypeStruct((16, HALF, HALF), BF16)


def factor_call(kernel, name, outs, args, specs=None, scratch=(), work=1):
    return pl.pallas_call(
        kernel,
        out_shape=outs,
        in_specs=specs or [VMEM] * len(args),
        out_specs=(VMEM,) * len(outs),
        scratch_shapes=scratch,
        compiler_params=pltpu.CompilerParams(vmem_limit_bytes=24 << 20),
        cost_estimate=pl.CostEstimate(flops=work * 5_000_000_000, bytes_accessed=1 << 20, transcendentals=0),
        name=name,
    )(*args)


def update_kernel(geometry, table, scales, packed, factors, factors_other, *rest):
    ratio, nr, nc, tpr, tpc, n, count = geometry
    here = (rest[0:2], rest[2:4])
    there = (rest[4:6], rest[6:8])
    blocks = rest[8 : 8 + count]
    out, stored, result, block, rowp, colp, rowl, xs, sem = rest[8 + count :]
    r = lax.axis_index("prow")
    c = lax.axis_index("pcol")
    tall = tpr * n

    reads = [pltpu.make_async_copy(packed.at[t * n : (t + 1) * n], stored.at[t], sem.at[0, t]) for t in range(tpr)]
    writes = [pltpu.make_async_copy(result.at[t], out.at[t * n : (t + 1) * n], sem.at[1, t]) for t in range(tpr)]
    for copy in reads:
        copy.start()

    def when(condition, target, value):
        @pl.when(condition)
        def _():
            target[...] = value[...]

    when(r % 2 == 0, xs, factors)
    when(r % 2 == 1, xs, factors_other)
    cat0 = join(xs, 0).T
    cat1 = join(xs, 6).T
    cat1 = jnp.concatenate([cat1[:n], cat1[:n], cat1[n:]], axis=0)
    panel = jnp.concatenate(
        [jnp.concatenate([xs[12], xs[13]], axis=1), jnp.concatenate([xs[14], xs[15]], axis=1)], axis=0
    ).T

    def solve(each):
        for t in range(tpr):
            rows = slice(t * n, (t + 1) * n)
            a0 = block[0, rows, :]
            raw0 = dot_nn(jnp.concatenate([a0, a0], axis=1), cat0)
            p0 = (raw0 * scale_row(block[0], t, tall)).astype(BF16)
            s1 = scale_row(block[1], t, tall)
            left = block[1, rows, :].astype(F32) * s1 - dot_nn(p0, panel)
            high, low = split(left)
            f1 = dot_nn(jnp.concatenate([high, low, high], axis=1), cat1)
            each(t, raw0, f1, s1, p0, f1.astype(BF16))

    same = (r % 2) == (c % 2)
    early = jnp.where(c < 2, 0, 1)
    swap = r // 4 if (nr, nc) == (8, 4) else 0
    for g in range(ratio):
        for half, panel_index in enumerate((early, 1 - early)):
            target = block.at[panel_index]
            when(same, target, here[half][g])
            when(jnp.logical_not(same), target, there[half][g])

        def keep_column(t, raw0, f1, s1, p0, p1, g=g):
            colp[t * ratio + (swap ^ g), :n, :] = p0.T
            colp[t * ratio + (swap ^ g), n:, :] = p1.T

        solve(keep_column)

    for panel_index in range(2):
        index = table[2 * (r * nc + c) + panel_index]
        for k in range(count):
            when(index == k, block.at[panel_index], blocks[k])

    def keep_row(t, raw0, f1, s1, p0, p1):
        rowp[t, :, :n] = p0
        rowp[t, :, n:] = p1

        @pl.when(c == 0)
        def _():
            rowl[t] = raw0

        @pl.when(c == 1)
        def _():
            rowl[t] = f1 / s1

    solve(keep_row)

    for t in range(tpr):
        reads[t].wait()
        true_row = t * nr + r
        for q in range(tpc):
            true_col = q * nc + c
            cols = slice(q * n, (q + 1) * n)

            @pl.when(true_row < true_col)
            def _():
                result[t, :, cols] = stored[t, :, cols]

            @pl.when(jnp.logical_and(true_row >= true_col, true_col >= 2))
            def _():
                change = dot_nn(rowp[t], colp[q])
                inverse = 1.0 / jnp.full((1, n), scales[t, q], F32)
                result[t, :, cols] = (stored[t, :, cols].astype(F32) - change * inverse).astype(BF16)

            if q * nc < 2:

                @pl.when(jnp.logical_and(true_row >= true_col, true_col < 2))
                def _():
                    row = lax.broadcasted_iota(jnp.int32, (n, n), 0)
                    col = lax.broadcasted_iota(jnp.int32, (n, n), 1)
                    keep = jnp.logical_or(row >= col, true_row != true_col)
                    result[t, :, cols] = jnp.where(keep, rowl[t], 0.0).astype(BF16)

        writes[t].start()
    for copy in writes:
        copy.wait()


def update(table, scales, packed, arrays, blocks, nr, nc, tpr, tpc, n):
    geometry = (nr // nc, nr, nc, tpr, tpc, n, len(blocks))
    tall = blocks[0].shape[0]
    return pl.pallas_call(
        functools.partial(update_kernel, geometry),
        out_shape=jax.ShapeDtypeStruct(packed.shape, BF16),
        in_specs=[SMEM, SMEM, HBM] + [VMEM] * (len(arrays) + len(blocks)),
        out_specs=HBM,
        scratch_shapes=[
            pltpu.VMEM((tpr, n, tpc * n), BF16),
            pltpu.VMEM((tpr, n, tpc * n), BF16),
            pltpu.VMEM((2, tall, n), BF16),
            pltpu.VMEM((tpr, n, 2 * n), BF16),
            pltpu.VMEM((tpc, 2 * n, n), BF16),
            pltpu.VMEM((tpr, n, n), F32),
            pltpu.VMEM(FACTORS.shape, BF16),
            pltpu.SemaphoreType.DMA((2, tpr)),
        ],
        compiler_params=pltpu.CompilerParams(vmem_limit_bytes=40 << 20),
        cost_estimate=pl.CostEstimate(flops=4_000_000_000, bytes_accessed=8 << 20, transcendentals=0),
        name="update_tiles",
    )(table, scales, packed, *arrays, *blocks)


def row_plan(nr, nc):
    if (nr, nc) == (8, 4):
        first = {0: [(1, 2)], 1: [(0, 1), (1, 2)], 4: [(1, 0), (0, 2)], 5: [(0, 1), (1, 2)]}
        second = {0: [(0, 1), (1, 0)], 1: [(1, 0)], 4: [(1, 2), (0, 1)], 5: [(0, 2), (1, 0)]}
        third = {0: [(0, 2), (2, 3, 1)], 1: [(0, 2), (2, 3, 1)], 4: [(2, 3, 1)], 5: [(2, 3, 1)]}
        fourth = {0: [(2, 3, 3)], 1: [(2, 3, 3)], 4: [(2, 3, 2)], 5: [(2, 3, 2)]}
        for r in (2, 6, 3, 7):
            u = r % 4
            first[r] = [(1, u), (0, 1)]
            second[r] = [(0, u), (1, 0)]
            third[r] = [(u, 5 - u, 1)]
            fourth[r] = [(u, 5 - u, 2)]
        turns = (first, second, third, fourth)
        return [[(r, *move[:2], move[2] if len(move) > 2 else 0) for r in turn for move in turn[r]] for turn in turns]
    rounds = [[], []]
    for r in range(nr):
        want = r % nc
        rounds[0].append((r, 0, 1, 0) if want == 1 else (r, 1, want, 0))
        if want > 1:
            rounds[1].append((r, 0, want, 0))
    done = {move[:3] for turn in rounds for move in turn}
    for shift in range(1, nc):
        moves = [(r, a, (a + shift) % nc, 0) for r in range(nr) for a in range(2)]
        rounds.append([move for move in moves if move[:3] not in done])
    return rounds


def on_device(nr, nc, packed, tile_scales):
    tpr, tpc = tile_scales.shape
    n = packed.shape[0] // tpr
    r = lax.axis_index("prow")
    c = lax.axis_index("pcol")
    def choose(options, index):
        value = options[0]
        for k in range(1, len(options)):
            value = jnp.where(index == k, options[k], value)
        return value

    def send(x, pairs):
        table = [(a * nc + b, d * nc + e) for (a, b), (d, e) in pairs]
        return lax.ppermute(x, ("prow", "pcol"), table)

    blank = [pltpu.VMEM((HALF, HALF), F32)] * 3
    message, pivot, x0 = factor_call(
        start_kernel,
        "pack_and_factor",
        (jax.ShapeDtypeStruct((tpr * n + EXTRA, n), BF16), jax.ShapeDtypeStruct((n + EXTRA, n), BF16), PARTS),
        (tile_scales, pltpu.with_memory_space_constraint(packed, pltpu.HBM)),
        [SMEM, HBM],
        blank + [pltpu.SemaphoreType.DMA((2,))],
    )

    rounds = row_plan(nr, nc)
    blocks = [message]
    holds = {(a, p, p): 0 for a in range(nr) for p in range(2)}

    def send_round(turn):
        used = sorted({k for *_, k in turn})
        operand = blocks[used[0]]
        for k in used[1:]:
            hits = [r * nc + c == a * nc + b for a, b, _, j in turn if j == k]
            operand = jnp.where(functools.reduce(jnp.logical_or, hits), blocks[k], operand)
        for a, b, d, k in turn:
            panel = next(p for p in range(2) if holds.get((a, b, p)) == k)
            holds[a, d, panel] = len(blocks)
        blocks.append(send(operand, [((a, b), (a, d)) for a, b, d, _ in turn]))

    send_round(rounds[0])
    send_round(rounds[1])

    step = nc // 2
    hops = []
    while step:
        takes = (c // step) % 2 == 1
        x0 = jnp.where(takes, send(x0, [((0, k), (0, k + step)) for k in range(0, nc, 2 * step)]), x0)
        hops.append(x0)
        step //= 2
    if nc == 4:
        got = send(pivot, [((1, 0), (1, 2)), ((1, 1), (1, 3))])
        held = jnp.where(c < 2, pivot, got)
        other = send(held, [((1, k), (1, k ^ 1)) for k in range(nc)])
        pair = jnp.stack([jnp.where(c % 2 == 0, held, other), jnp.where(c % 2 == 0, other, held)])
    else:
        left = pivot
        right = jnp.where(c == 1, pivot, 0)
        for k in range(1, nc):
            left = jnp.where(c == k, send(pivot, [((1, 0), (1, k))]), left)
        for k in range(nc):
            if k != 1:
                right = jnp.where(c == k, send(pivot, [((1, 1), (1, k))]), right)
        pair = jnp.stack([left, right])
    x0, pair, blocks[0], blocks[1] = lax.optimization_barrier((x0, pair, blocks[0], blocks[1]))

    u = r % nc
    ratio = nr // nc
    grid = (nr, nc) == (8, 4)

    def columns(x):
        if grid:
            got = send(x, [((e + 4 * g, e), ((e + 4 * g) ^ 2, e)) for e in range(nc) for g in range(2)])
            side = jnp.where(u == c, x, got)
            return [side, send(side, [((a, e), (a ^ 4, e)) for a in range(nr) for e in range(nc) if a % 2 == e % 2])]
        near = [x]
        for mask in range(2, nr, 2):
            pairs = [((e + nc * g, e), ((e + nc * g) ^ mask, e)) for e in range(nc) for g in range(ratio)]
            near.append(send(x, pairs))
        return [choose(near, (r ^ (c + nc * g)) // 2) for g in range(ratio)]

    cols = columns(jnp.where(c == 0, blocks[0], blocks[1]))
    send_round(rounds[2])

    x0_strides = [k for k in (2, 4) if grid] or [1 << k for k in range(nr.bit_length() - 2, 0, -1)]
    done = [0]
    pair_done = [1]
    for level, stride in enumerate(x0_strides):
        x0 = jnp.where((r // stride) % 2 == 1, send(x0, [((a, e), (a + stride, e)) for a in done for e in range(nc)]), x0)
        done += [a + stride for a in done]
        stride = x0_strides[-1 - level]
        pairs = [((a, e), ((a & ~1) + stride, e)) for a in pair_done for e in range(nc)]
        pair = jnp.where((r // stride) % 2 == 1, send(pair, pairs), pair)
        pair_done += [(a & ~1) + stride for a in pair_done]
        x0, pair, blocks[2] = lax.optimization_barrier((x0, pair, blocks[2]))
        if level == 0:
            b_block = blocks[2]
    pair = jnp.where(r == 0, send(pair, [((1, e), (0, e)) for e in range(nc)]), pair)

    late = jnp.where(r == 0, b_block, blocks[1]) if grid else blocks[1]
    cols += columns(jnp.where(c == 0, late, jnp.where(c == 1, blocks[0], b_block)))
    (factors,) = factor_call(second_kernel, "factor_second", (FACTORS,), (x0, pair), None, blank, 2)
    factors_other = send(factors, [((a, e), (a + 1, e)) for a in range(0, nr, 2) for e in range(nc)])
    for turn in rounds[3:]:
        send_round(turn)

    pairs = [((a, e), (a ^ 1, e)) for a in range(nr) for e in range(nc) if a % 2 == e % 2]
    cols_other = [send(x, pairs) for x in cols]
    table = np.array([holds[a, b, p] for a in range(nr) for b in range(nc) for p in range(2)], np.int32)
    packed = pltpu.with_memory_space_constraint(packed, pltpu.HBM)
    return update(table, tile_scales, packed, (factors, factors_other, *cols, *cols_other), blocks, nr, nc, tpr, tpc, n)


def solution(mesh):
    nr = mesh.shape["prow"]
    nc = mesh.shape["pcol"]
    return jax.shard_map(
        functools.partial(on_device, nr, nc),
        mesh=mesh,
        in_specs=(P("prow", "pcol"), P("prow", "pcol")),
        out_specs=P("prow", "pcol"),
        check_vma=False,
    )
```

```python
import functools

import jax
import jax.numpy as jnp
import numpy as np
from jax import lax
from jax.experimental import pallas as pl
from jax.experimental.pallas import tpu as pltpu
from jax.sharding import PartitionSpec as P

F32 = jnp.float32
BF16 = jnp.bfloat16
HALF = 128
EXTRA = 16


def dot_nt(a, b, precision=None):
    dims = (((1,), (1,)), ((), ()))
    return lax.dot_general(a, b, dims, precision=precision, preferred_element_type=F32)


def dot_nn(a, b, precision=None):
    dims = (((1,), (0,)), ((), ()))
    return lax.dot_general(a, b, dims, precision=precision, preferred_element_type=F32)


HIGHEST = lax.Precision.HIGHEST


def inverse_factor(a):
    n = a.shape[0]
    blocks = n // 8
    full = (8, n)
    rows = [a[8 * i : 8 * i + 8, :] for i in range(blocks)]
    lane = lax.broadcasted_iota(jnp.int32, full, 1)
    sub = lax.broadcasted_iota(jnp.int32, full, 0)

    def column(x, k):
        return jnp.broadcast_to(x[:, k : k + 1], full)

    def row(x, k):
        return jnp.broadcast_to(x[k : k + 1, :], full)

    out = []
    own = [column(rows[0], k) for k in range(8)]
    for t in range(blocks):
        base = 8 * t
        here = jnp.logical_and(lane >= base, lane < base + 8)
        s = {(j, k): row(own[k], j) for j in range(8) for k in range(j, 8)}
        c = {}
        for i in range(t + 1, blocks):
            for j in range(8):
                c[i, j] = column(rows[i], base + j)
        last = t + 1 == blocks
        if not last:
            own = [column(rows[t + 1], base + 8 + k) for k in range(8)]
        for i in range(t + 1, blocks):
            rows[i] = jnp.where(here, 0.0, rows[i])
        b = [jnp.where(here, jnp.where(lane == base + j, 1.0, 0.0), row(rows[t], j)) for j in range(8)]
        d = [] if last else [c[t + 1, j] for j in range(8)]
        m = {}
        z = []
        x = jnp.zeros(full, F32)
        for j in range(8):
            r0 = pl.reciprocal(s[j, j], approx=True)
            e = 2.0 - s[j, j] * r0
            r = r0 * e
            for k in range(j + 1, 8):
                m[j, k] = s[j, k] * r
            for k in range(j + 1, 8):
                for l in range(k, 8):
                    if k == j + 1 and l == k:
                        s[k, l] = s[k, l] - ((s[j, k] * s[j, k]) * r0) * e
                    else:
                        s[k, l] = s[k, l] - m[j, k] * s[j, l]
                b[k] = b[k] - m[j, k] * b[j]
            z.append(r * b[j])
            if not last:
                for k in range(j + 1, 8):
                    d[k] = d[k] - m[j, k] * d[j]
                w = d[j] * r
                own = [own[k] - w * row(d[j], k) for k in range(8)]
                rows[t + 1] = rows[t + 1] - d[j] * z[j]
            x = jnp.where(sub == j, lax.rsqrt(s[j, j]) * b[j], x)
        out.append(jnp.where(lane < base + 8, x, 0.0))
        if t + 2 < blocks:
            y = list(z)
            for k in range(7, 0, -1):
                for j in range(k):
                    y[j] = y[j] - m[j, k] * y[k]
            for i in range(t + 2, blocks):
                for j in range(8):
                    rows[i] = rows[i] - c[i, j] * y[j]
    return jnp.concatenate(out, axis=0)


def split(x):
    high = x.astype(BF16)
    return high, (x - high.astype(F32)).astype(BF16)


def scale_row(ref, tile, n):
    tail = ref[n:, :].astype(F32)
    return tail[3 * tile : 3 * tile + 1] + tail[3 * tile + 1 : 3 * tile + 2] + tail[3 * tile + 2 : 3 * tile + 3]


def first_half(tile, inv_ref, low_ref, rest_ref):
    x = inverse_factor(tile[:HALF, :HALF])
    factor = dot_nt(tile[HALF:, :HALF], x, HIGHEST)
    inv_ref[...] = x
    low_ref[...] = factor
    rest_ref[...] = tile[HALF:, HALF:] - dot_nt(factor, factor, HIGHEST)


def second_half(inv_ref, low_ref, rest_ref, out_ref):
    x22 = inverse_factor(rest_ref[...])
    x11 = inv_ref[...]
    x21 = -dot_nn(x22, dot_nn(low_ref[...], x11, HIGHEST), HIGHEST)
    for k, x in enumerate((x11, x21, x22)):
        out_ref[k], out_ref[k + 3] = split(x)


def scale_tail(scales, n):
    row = lax.broadcasted_iota(jnp.int32, (EXTRA, n), 0)
    total = jnp.zeros((EXTRA, n), F32)
    for t in range(scales.shape[0]):
        rest = jnp.full((EXTRA, n), scales[t, 0], F32)
        for k in range(3):
            part = rest.astype(BF16).astype(F32)
            total = jnp.where(row == 3 * t + k, part, total)
            rest = rest - part
    return total.astype(BF16)


def start_kernel(scales, packed, message, pivot, x0_ref, inv, low, rest, sem):
    n = pivot.shape[1]
    tall = message.shape[0] - EXTRA
    tile_copy = pltpu.make_async_copy(packed.at[0:n, 0:n], pivot.at[0:n], sem.at[0])
    block_copy = pltpu.make_async_copy(packed.at[:, 0:n], message.at[0:tall], sem.at[1])
    tile_copy.start()
    block_copy.start()
    tail = scale_tail(scales, n)
    pivot[n:, :] = tail
    message[tall:, :] = tail
    tile_copy.wait()
    block_copy.wait()

    @pl.when(jnp.logical_and(lax.axis_index("prow") == 0, lax.axis_index("pcol") == 0))
    def _():
        first_half(pivot[:n, :].astype(F32) * scale_row(pivot, 0, n), inv, low, rest)
        second_half(inv, low, rest, x0_ref)


def second_kernel(x0, pair, out_ref, inv, low, rest):
    n = 2 * HALF

    @pl.when(lax.axis_index("prow") % 2 == 0)
    def _():
        out_ref[0:6] = x0[...]
        a = pair[0, :n, :]
        solved = dot_nt(jnp.concatenate([a, a], axis=1), join(x0, 0)) * scale_row(pair[0], 0, n)
        panel = solved.astype(BF16)
        for k in range(4):
            i, j = divmod(k, 2)
            out_ref[12 + k] = panel[i * HALF : (i + 1) * HALF, j * HALF : (j + 1) * HALF]
        tile = pair[1, :n, :].astype(F32) * scale_row(pair[1], 0, n) - dot_nt(panel, panel)
        first_half(tile, inv, low, rest)
        second_half(inv, low, rest, out_ref.at[6:12])


def join(x, base):
    zero = jnp.zeros((HALF, HALF), BF16)
    upper = jnp.concatenate([x[base], zero, x[base + 3], zero], axis=1)
    lower = jnp.concatenate([x[base + 1], x[base + 2], x[base + 4], x[base + 5]], axis=1)
    return jnp.concatenate([upper, lower], axis=0)


VMEM = pl.BlockSpec(memory_space=pltpu.VMEM)
SMEM = pl.BlockSpec(memory_space=pltpu.SMEM)
HBM = pl.BlockSpec(memory_space=pltpu.HBM)
BLOCK = jax.ShapeDtypeStruct((HALF, HALF), F32)
PARTS = jax.ShapeDtypeStruct((6, HALF, HALF), BF16)
FACTORS = jax.ShapeDtypeStruct((16, HALF, HALF), BF16)


def factor_call(kernel, name, outs, args, specs=None, scratch=(), work=1):
    return pl.pallas_call(
        kernel,
        out_shape=outs,
        in_specs=specs or [VMEM] * len(args),
        out_specs=(VMEM,) * len(outs),
        scratch_shapes=scratch,
        compiler_params=pltpu.CompilerParams(vmem_limit_bytes=24 << 20),
        cost_estimate=pl.CostEstimate(flops=work * 5_000_000_000, bytes_accessed=1 << 20, transcendentals=0),
        name=name,
    )(*args)


def update_kernel(geometry, table, scales, packed, factors, factors_other, *rest):
    ratio, nr, nc, tpr, tpc, n, count = geometry
    here = (rest[0:2], rest[2:4])
    there = (rest[4:6], rest[6:8])
    blocks = rest[8 : 8 + count]
    out, stored, result, block, rowp, colp, rowl, xs, sem = rest[8 + count :]
    r = lax.axis_index("prow")
    c = lax.axis_index("pcol")
    tall = tpr * n

    reads = [pltpu.make_async_copy(packed.at[t * n : (t + 1) * n], stored.at[t], sem.at[0, t]) for t in range(tpr)]
    writes = [pltpu.make_async_copy(result.at[t], out.at[t * n : (t + 1) * n], sem.at[1, t]) for t in range(tpr)]
    for copy in reads:
        copy.start()

    def when(condition, target, value):
        @pl.when(condition)
        def _():
            target[...] = value[...]

    when(r % 2 == 0, xs, factors)
    when(r % 2 == 1, xs, factors_other)
    cat0 = join(xs, 0).T
    cat1 = join(xs, 6).T
    cat1 = jnp.concatenate([cat1[:n], cat1[:n], cat1[n:]], axis=0)
    panel = jnp.concatenate(
        [jnp.concatenate([xs[12], xs[13]], axis=1), jnp.concatenate([xs[14], xs[15]], axis=1)], axis=0
    ).T

    def solve(each):
        for t in range(tpr):
            rows = slice(t * n, (t + 1) * n)
            a0 = block[0, rows, :]
            raw0 = dot_nn(jnp.concatenate([a0, a0], axis=1), cat0)
            p0 = (raw0 * scale_row(block[0], t, tall)).astype(BF16)
            s1 = scale_row(block[1], t, tall)
            left = block[1, rows, :].astype(F32) * s1 - dot_nn(p0, panel)
            high, low = split(left)
            f1 = dot_nn(jnp.concatenate([high, low, high], axis=1), cat1)
            each(t, raw0, f1, s1, p0, f1.astype(BF16))

    same = (r % 2) == (c % 2)
    early = jnp.where(c < 2, 0, 1)
    swap = r // 4 if (nr, nc) == (8, 4) else 0
    for g in range(ratio):
        for half, panel_index in enumerate((early, 1 - early)):
            target = block.at[panel_index]
            when(same, target, here[half][g])
            when(jnp.logical_not(same), target, there[half][g])

        def keep_column(t, raw0, f1, s1, p0, p1, g=g):
            colp[t * ratio + (swap ^ g), :n, :] = p0.T
            colp[t * ratio + (swap ^ g), n:, :] = p1.T

        solve(keep_column)

    for panel_index in range(2):
        index = table[2 * (r * nc + c) + panel_index]
        for k in range(count):
            when(index == k, block.at[panel_index], blocks[k])

    def keep_row(t, raw0, f1, s1, p0, p1):
        rowp[t, :, :n] = p0
        rowp[t, :, n:] = p1

        @pl.when(c == 0)
        def _():
            rowl[t] = raw0

        @pl.when(c == 1)
        def _():
            rowl[t] = f1 / s1

    solve(keep_row)

    for t in range(tpr):
        reads[t].wait()
        true_row = t * nr + r
        for q in range(tpc):
            true_col = q * nc + c
            cols = slice(q * n, (q + 1) * n)

            @pl.when(true_row < true_col)
            def _():
                result[t, :, cols] = stored[t, :, cols]

            @pl.when(jnp.logical_and(true_row >= true_col, true_col >= 2))
            def _():
                change = dot_nn(rowp[t], colp[q])
                inverse = 1.0 / jnp.full((1, n), scales[t, q], F32)
                result[t, :, cols] = (stored[t, :, cols].astype(F32) - change * inverse).astype(BF16)

            if q * nc < 2:

                @pl.when(jnp.logical_and(true_row >= true_col, true_col < 2))
                def _():
                    row = lax.broadcasted_iota(jnp.int32, (n, n), 0)
                    col = lax.broadcasted_iota(jnp.int32, (n, n), 1)
                    keep = jnp.logical_or(row >= col, true_row != true_col)
                    result[t, :, cols] = jnp.where(keep, rowl[t], 0.0).astype(BF16)

        writes[t].start()
    for copy in writes:
        copy.wait()


def update(table, scales, packed, arrays, blocks, nr, nc, tpr, tpc, n):
    geometry = (nr // nc, nr, nc, tpr, tpc, n, len(blocks))
    tall = blocks[0].shape[0]
    return pl.pallas_call(
        functools.partial(update_kernel, geometry),
        out_shape=jax.ShapeDtypeStruct(packed.shape, BF16),
        in_specs=[SMEM, SMEM, HBM] + [VMEM] * (len(arrays) + len(blocks)),
        out_specs=HBM,
        scratch_shapes=[
            pltpu.VMEM((tpr, n, tpc * n), BF16),
            pltpu.VMEM((tpr, n, tpc * n), BF16),
            pltpu.VMEM((2, tall, n), BF16),
            pltpu.VMEM((tpr, n, 2 * n), BF16),
            pltpu.VMEM((tpc, 2 * n, n), BF16),
            pltpu.VMEM((tpr, n, n), F32),
            pltpu.VMEM(FACTORS.shape, BF16),
            pltpu.SemaphoreType.DMA((2, tpr)),
        ],
        compiler_params=pltpu.CompilerParams(vmem_limit_bytes=40 << 20),
        cost_estimate=pl.CostEstimate(flops=4_000_000_000, bytes_accessed=8 << 20, transcendentals=0),
        name="update_tiles",
    )(table, scales, packed, *arrays, *blocks)


def row_plan(nr, nc):
    if (nr, nc) == (8, 4):
        first = {0: [(1, 2)], 1: [(0, 1), (1, 2)], 4: [(1, 0), (0, 2)], 5: [(0, 1), (1, 2)]}
        second = {0: [(0, 1), (1, 0)], 1: [(1, 0)], 4: [(1, 2), (0, 1)], 5: [(0, 2), (1, 0)]}
        third = {0: [(0, 2), (2, 3, 1)], 1: [(0, 2), (2, 3, 1)], 4: [(2, 3, 1)], 5: [(2, 3, 1)]}
        fourth = {0: [(2, 3, 3)], 1: [(2, 3, 3)], 4: [(2, 3, 2)], 5: [(2, 3, 2)]}
        for r in (2, 6, 3, 7):
            u = r % 4
            first[r] = [(1, u), (0, 1)]
            second[r] = [(0, u), (1, 0)]
            third[r] = [(u, 5 - u, 1)]
            fourth[r] = [(u, 5 - u, 2)]
        turns = (first, second, third, fourth)
        return [[(r, *move[:2], move[2] if len(move) > 2 else 0) for r in turn for move in turn[r]] for turn in turns]
    rounds = [[], []]
    for r in range(nr):
        want = r % nc
        rounds[0].append((r, 0, 1, 0) if want == 1 else (r, 1, want, 0))
        if want > 1:
            rounds[1].append((r, 0, want, 0))
    done = {move[:3] for turn in rounds for move in turn}
    for shift in range(1, nc):
        moves = [(r, a, (a + shift) % nc, 0) for r in range(nr) for a in range(2)]
        rounds.append([move for move in moves if move[:3] not in done])
    return rounds


def on_device(nr, nc, packed, tile_scales):
    tpr, tpc = tile_scales.shape
    n = packed.shape[0] // tpr
    r = lax.axis_index("prow")
    c = lax.axis_index("pcol")
    def choose(options, index):
        value = options[0]
        for k in range(1, len(options)):
            value = jnp.where(index == k, options[k], value)
        return value

    def send(x, pairs):
        table = [(a * nc + b, d * nc + e) for (a, b), (d, e) in pairs]
        return lax.ppermute(x, ("prow", "pcol"), table)

    blank = [pltpu.VMEM((HALF, HALF), F32)] * 3
    message, pivot, x0 = factor_call(
        start_kernel,
        "pack_and_factor",
        (jax.ShapeDtypeStruct((tpr * n + EXTRA, n), BF16), jax.ShapeDtypeStruct((n + EXTRA, n), BF16), PARTS),
        (tile_scales, pltpu.with_memory_space_constraint(packed, pltpu.HBM)),
        [SMEM, HBM],
        blank + [pltpu.SemaphoreType.DMA((2,))],
    )

    rounds = row_plan(nr, nc)
    blocks = [message]
    holds = {(a, p, p): 0 for a in range(nr) for p in range(2)}

    def send_round(turn):
        used = sorted({k for *_, k in turn})
        operand = blocks[used[0]]
        for k in used[1:]:
            hits = [r * nc + c == a * nc + b for a, b, _, j in turn if j == k]
            operand = jnp.where(functools.reduce(jnp.logical_or, hits), blocks[k], operand)
        for a, b, d, k in turn:
            panel = next(p for p in range(2) if holds.get((a, b, p)) == k)
            holds[a, d, panel] = len(blocks)
        blocks.append(send(operand, [((a, b), (a, d)) for a, b, d, _ in turn]))

    send_round(rounds[0])
    send_round(rounds[1])

    step = nc // 2
    while step:
        takes = (c // step) % 2 == 1
        x0 = jnp.where(takes, send(x0, [((0, k), (0, k + step)) for k in range(0, nc, 2 * step)]), x0)
        step //= 2
        if step:
            x0, blocks[1] = lax.optimization_barrier((x0, blocks[1]))
    if nc == 4:
        got = send(pivot, [((1, 0), (1, 2)), ((1, 1), (1, 3))])
        held = jnp.where(c < 2, pivot, got)
        other = send(held, [((1, k), (1, k ^ 1)) for k in range(nc)])
        pair = jnp.stack([jnp.where(c % 2 == 0, held, other), jnp.where(c % 2 == 0, other, held)])
    else:
        left = pivot
        right = jnp.where(c == 1, pivot, 0)
        for k in range(1, nc):
            left = jnp.where(c == k, send(pivot, [((1, 0), (1, k))]), left)
        for k in range(nc):
            if k != 1:
                right = jnp.where(c == k, send(pivot, [((1, 1), (1, k))]), right)
        pair = jnp.stack([left, right])
    x0, pair, *blocks = lax.optimization_barrier((x0, pair, *blocks))

    u = r % nc
    ratio = nr // nc
    grid = (nr, nc) == (8, 4)

    def column_start(x):
        if grid:
            return [x, send(x, [((e + 4 * g, e), ((e + 4 * g) ^ 2, e)) for e in range(nc) for g in range(2)])]
        near = [x]
        for mask in range(2, nr, 2):
            pairs = [((e + nc * g, e), ((e + nc * g) ^ mask, e)) for e in range(nc) for g in range(ratio)]
            near.append(send(x, pairs))
        return near

    def column_end(near):
        if grid:
            side = jnp.where(u == c, *near)
            return [side, send(side, [((a, e), (a ^ 4, e)) for a in range(nr) for e in range(nc) if a % 2 == e % 2])]
        return [choose(near, (r ^ (c + nc * g)) // 2) for g in range(ratio)]

    cols = column_end(column_start(jnp.where(c == 0, blocks[0], blocks[1])))
    send_round(rounds[2])

    x0_strides = [k for k in (2, 4) if grid] or [1 << k for k in range(nr.bit_length() - 2, 0, -1)]
    done = [0]
    pair_done = [1]
    for level, stride in enumerate(x0_strides):
        x0 = jnp.where((r // stride) % 2 == 1, send(x0, [((a, e), (a + stride, e)) for a in done for e in range(nc)]), x0)
        done += [a + stride for a in done]
        stride = x0_strides[-1 - level]
        pairs = [((a, e), ((a & ~1) + stride, e)) for a in pair_done for e in range(nc)]
        pair = jnp.where((r // stride) % 2 == 1, send(pair, pairs), pair)
        pair_done += [(a & ~1) + stride for a in pair_done]
        if level == 0:
            x0, pair, own, early, late = lax.optimization_barrier((x0, pair, *blocks[:3]))
        else:
            x0, pair = lax.optimization_barrier((x0, pair))
    pair = jnp.where(r == 0, send(pair, [((1, e), (0, e)) for e in range(nc)]), pair)

    left = jnp.where(r == 0, late, early) if grid else early
    near = column_start(jnp.where(c == 0, left, jnp.where(c == 1, own, late)))
    (factors,) = factor_call(second_kernel, "factor_second", (FACTORS,), (x0, pair), None, blank, 2)

    factors, *rest = lax.optimization_barrier((factors, *cols, *near, *blocks[3:]))
    cols, near, blocks[3:] = rest[:ratio], rest[ratio : ratio + len(near)], rest[ratio + len(near) :]
    cols += column_end(near)
    factors_other = send(factors, [((a, e), (a + 1, e)) for a in range(0, nr, 2) for e in range(nc)])
    for turn in rounds[3:]:
        send_round(turn)

    pairs = [((a, e), (a ^ 1, e)) for a in range(nr) for e in range(nc) if a % 2 == e % 2]
    cols_other = [send(x, pairs) for x in cols]
    table = np.array([holds[a, b, p] for a in range(nr) for b in range(nc) for p in range(2)], np.int32)
    packed = pltpu.with_memory_space_constraint(packed, pltpu.HBM)
    return update(table, tile_scales, packed, (factors, factors_other, *cols, *cols_other), blocks, nr, nc, tpr, tpc, n)


def solution(mesh):
    nr = mesh.shape["prow"]
    nc = mesh.shape["pcol"]
    return jax.shard_map(
        functools.partial(on_device, nr, nc),
        mesh=mesh,
        in_specs=(P("prow", "pcol"), P("prow", "pcol")),
        out_specs=P("prow", "pcol"),
        check_vma=False,
    )
```

```python
import functools

import jax
import jax.numpy as jnp
import numpy as np
from jax import lax
from jax.experimental import pallas as pl
from jax.experimental.pallas import tpu as pltpu
from jax.sharding import PartitionSpec as P

F32 = jnp.float32
BF16 = jnp.bfloat16
HALF = 128
EXTRA = 16


def dot_nt(a, b, precision=None):
    dims = (((1,), (1,)), ((), ()))
    return lax.dot_general(a, b, dims, precision=precision, preferred_element_type=F32)


def dot_nn(a, b, precision=None):
    dims = (((1,), (0,)), ((), ()))
    return lax.dot_general(a, b, dims, precision=precision, preferred_element_type=F32)


HIGHEST = lax.Precision.HIGHEST


def inverse_factor(a):
    n = a.shape[0]
    blocks = n // 8
    full = (8, n)
    rows = [a[8 * i : 8 * i + 8, :] for i in range(blocks)]
    lane = lax.broadcasted_iota(jnp.int32, full, 1)
    sub = lax.broadcasted_iota(jnp.int32, full, 0)

    def column(x, k):
        return jnp.broadcast_to(x[:, k : k + 1], full)

    def row(x, k):
        return jnp.broadcast_to(x[k : k + 1, :], full)

    out = []
    own = [column(rows[0], k) for k in range(8)]
    for t in range(blocks):
        base = 8 * t
        here = jnp.logical_and(lane >= base, lane < base + 8)
        s = {(j, k): row(own[k], j) for j in range(8) for k in range(j, 8)}
        c = {}
        for i in range(t + 1, blocks):
            for j in range(8):
                c[i, j] = column(rows[i], base + j)
        last = t + 1 == blocks
        if not last:
            own = [column(rows[t + 1], base + 8 + k) for k in range(8)]
        for i in range(t + 1, blocks):
            rows[i] = jnp.where(here, 0.0, rows[i])
        b = [jnp.where(here, jnp.where(lane == base + j, 1.0, 0.0), row(rows[t], j)) for j in range(8)]
        d = [] if last else [c[t + 1, j] for j in range(8)]
        m = {}
        z = []
        x = jnp.zeros(full, F32)
        for j in range(8):
            r0 = pl.reciprocal(s[j, j], approx=True)
            e = 2.0 - s[j, j] * r0
            r = r0 * e
            for k in range(j + 1, 8):
                m[j, k] = s[j, k] * r
            for k in range(j + 1, 8):
                for l in range(k, 8):
                    if k == j + 1 and l == k:
                        s[k, l] = s[k, l] - ((s[j, k] * s[j, k]) * r0) * e
                    else:
                        s[k, l] = s[k, l] - m[j, k] * s[j, l]
                b[k] = b[k] - m[j, k] * b[j]
            z.append(r * b[j])
            if not last:
                for k in range(j + 1, 8):
                    d[k] = d[k] - m[j, k] * d[j]
                w = d[j] * r
                own = [own[k] - w * row(d[j], k) for k in range(8)]
                rows[t + 1] = rows[t + 1] - d[j] * z[j]
            x = jnp.where(sub == j, lax.rsqrt(s[j, j]) * b[j], x)
        out.append(jnp.where(lane < base + 8, x, 0.0))
        if t + 2 < blocks:
            y = list(z)
            for k in range(7, 0, -1):
                for j in range(k):
                    y[j] = y[j] - m[j, k] * y[k]
            for i in range(t + 2, blocks):
                for j in range(8):
                    rows[i] = rows[i] - c[i, j] * y[j]
    return jnp.concatenate(out, axis=0)


def split(x):
    high = x.astype(BF16)
    return high, (x - high.astype(F32)).astype(BF16)


def scale_row(ref, tile, n):
    tail = ref[n:, :].astype(F32)
    return tail[3 * tile : 3 * tile + 1] + tail[3 * tile + 1 : 3 * tile + 2] + tail[3 * tile + 2 : 3 * tile + 3]


def first_half(tile, inv_ref, low_ref, rest_ref):
    x = inverse_factor(tile[:HALF, :HALF])
    factor = dot_nt(tile[HALF:, :HALF], x, HIGHEST)
    inv_ref[...] = x
    low_ref[...] = factor
    rest_ref[...] = tile[HALF:, HALF:] - dot_nt(factor, factor, HIGHEST)


def second_half(inv_ref, low_ref, rest_ref, out_ref):
    x22 = inverse_factor(rest_ref[...])
    x11 = inv_ref[...]
    x21 = -dot_nn(x22, dot_nn(low_ref[...], x11, HIGHEST), HIGHEST)
    for k, x in enumerate((x11, x21, x22)):
        out_ref[k], out_ref[k + 3] = split(x)


def scale_tail(scales, n):
    row = lax.broadcasted_iota(jnp.int32, (EXTRA, n), 0)
    total = jnp.zeros((EXTRA, n), F32)
    for t in range(scales.shape[0]):
        rest = jnp.full((EXTRA, n), scales[t, 0], F32)
        for k in range(3):
            part = rest.astype(BF16).astype(F32)
            total = jnp.where(row == 3 * t + k, part, total)
            rest = rest - part
    return total.astype(BF16)


def pack_kernel(scales, packed, message, pivot, sem):
    n = pivot.shape[1]
    tall = message.shape[0] - EXTRA
    tile_copy = pltpu.make_async_copy(packed.at[0:n, 0:n], pivot.at[0:n], sem.at[0])
    block_copy = pltpu.make_async_copy(packed.at[:, 0:n], message.at[0:tall], sem.at[1])
    tile_copy.start()
    block_copy.start()
    tail = scale_tail(scales, n)
    pivot[n:, :] = tail
    message[tall:, :] = tail
    tile_copy.wait()
    block_copy.wait()


def take(tiles, mask, target):
    for k, tile in enumerate(tiles):

        @pl.when(mask == 2 * k)
        def _(tile=tile):
            n = target.shape[0]
            target[...] = tile[:n, :].astype(F32) * scale_row(tile, 0, n)


def factor_kernel(*refs):
    tiles, out_ref, left, tile, inv, low, rest = refs[:-6], *refs[-6:]
    n = 2 * HALF
    r = lax.axis_index("prow")

    @pl.when(r % 2 == 0)
    def _():
        take(tiles, r, tile)
        take(tiles, r ^ 2, left)
        first_half(tile, inv, low, rest)
        second_half(inv, low, rest, out_ref.at[0:6])
        take(tiles, r ^ 4, tile)
        high, part = split(left[...])
        cat = join(out_ref, 0)
        both = jnp.concatenate([cat[:, :n], cat[:, :n], cat[:, n:]], axis=1)
        panel = dot_nt(jnp.concatenate([high, part, high], axis=1), both).astype(BF16)
        for k in range(4):
            i, j = divmod(k, 2)
            out_ref[12 + k] = panel[i * HALF : (i + 1) * HALF, j * HALF : (j + 1) * HALF]
        tile[...] = tile[...] - dot_nt(panel, panel)
        first_half(tile, inv, low, rest)
        second_half(inv, low, rest, out_ref.at[6:12])


def join(x, base):
    zero = jnp.zeros((HALF, HALF), BF16)
    upper = jnp.concatenate([x[base], zero, x[base + 3], zero], axis=1)
    lower = jnp.concatenate([x[base + 1], x[base + 2], x[base + 4], x[base + 5]], axis=1)
    return jnp.concatenate([upper, lower], axis=0)


VMEM = pl.BlockSpec(memory_space=pltpu.VMEM)
SMEM = pl.BlockSpec(memory_space=pltpu.SMEM)
HBM = pl.BlockSpec(memory_space=pltpu.HBM)
BLOCK = jax.ShapeDtypeStruct((HALF, HALF), F32)
PARTS = jax.ShapeDtypeStruct((6, HALF, HALF), BF16)
FACTORS = jax.ShapeDtypeStruct((16, HALF, HALF), BF16)


def factor_call(kernel, name, outs, args, specs=None, scratch=(), work=1):
    return pl.pallas_call(
        kernel,
        out_shape=outs,
        in_specs=specs or [VMEM] * len(args),
        out_specs=(VMEM,) * len(outs),
        scratch_shapes=scratch,
        compiler_params=pltpu.CompilerParams(vmem_limit_bytes=24 << 20),
        cost_estimate=pl.CostEstimate(flops=work * 5_000_000_000, bytes_accessed=1 << 20, transcendentals=0),
        name=name,
    )(*args)


def update_kernel(geometry, scales, packed, factors, factors_other, *rest):
    ratio, nr, nc, tpr, tpc, n = geometry
    here, there, mine, relayed = rest[0:2], rest[2:4], rest[4], rest[5]
    out, stored, result, block, rowp, colp, rowl, xs, sem = rest[6:]
    r = lax.axis_index("prow")
    c = lax.axis_index("pcol")
    tall = tpr * n

    reads = [pltpu.make_async_copy(packed.at[t * n : (t + 1) * n], stored.at[t], sem.at[0, t]) for t in range(tpr)]
    writes = [pltpu.make_async_copy(result.at[t], out.at[t * n : (t + 1) * n], sem.at[1, t]) for t in range(tpr)]
    for copy in reads:
        copy.start()

    def when(condition, target, value):
        @pl.when(condition)
        def _():
            target[...] = value[...]

    when(r % 2 == 0, xs, factors)
    when(r % 2 == 1, xs, factors_other)
    cat0 = join(xs, 0).T
    cat1 = join(xs, 6).T
    cat1 = jnp.concatenate([cat1[:n], cat1[:n], cat1[n:]], axis=0)
    panel = jnp.concatenate(
        [jnp.concatenate([xs[12], xs[13]], axis=1), jnp.concatenate([xs[14], xs[15]], axis=1)], axis=0
    ).T

    def solve(each):
        for t in range(tpr):
            rows = slice(t * n, (t + 1) * n)
            a0 = block[0, rows, :]
            raw0 = dot_nn(jnp.concatenate([a0, a0], axis=1), cat0)
            p0 = (raw0 * scale_row(block[0], t, tall)).astype(BF16)
            s1 = scale_row(block[1], t, tall)
            left = block[1, rows, :].astype(F32) * s1 - dot_nn(p0, panel)
            high, low = split(left)
            f1 = dot_nn(jnp.concatenate([high, low, high], axis=1), cat1)
            each(t, raw0, f1, s1, p0, f1.astype(BF16))

    same = (r % 2) == (c % 2)
    for g in range(ratio):
        when(same, block, here[g])
        when(jnp.logical_not(same), block, there[g])

        def keep_column(t, raw0, f1, s1, p0, p1, g=g):
            colp[t * ratio + g, :n, :] = p0.T
            colp[t * ratio + g, n:, :] = p1.T

        solve(keep_column)

    late = jnp.logical_and(nc == 4, jnp.where(r % 4 == 3, c == 2, c == 3))
    when(late, block, relayed)
    when(jnp.logical_not(late), block, mine)

    def keep_row(t, raw0, f1, s1, p0, p1):
        rowp[t, :, :n] = p0
        rowp[t, :, n:] = p1

        @pl.when(c == 0)
        def _():
            rowl[t] = raw0

        @pl.when(c == 1)
        def _():
            rowl[t] = f1 / s1

    solve(keep_row)

    for t in range(tpr):
        reads[t].wait()
        true_row = t * nr + r
        for q in range(tpc):
            true_col = q * nc + c
            cols = slice(q * n, (q + 1) * n)

            @pl.when(true_row < true_col)
            def _():
                result[t, :, cols] = stored[t, :, cols]

            @pl.when(jnp.logical_and(true_row >= true_col, true_col >= 2))
            def _():
                change = dot_nn(rowp[t], colp[q])
                inverse = 1.0 / jnp.full((1, n), scales[t, q], F32)
                result[t, :, cols] = (stored[t, :, cols].astype(F32) - change * inverse).astype(BF16)

            if q * nc < 2:

                @pl.when(jnp.logical_and(true_row >= true_col, true_col < 2))
                def _():
                    row = lax.broadcasted_iota(jnp.int32, (n, n), 0)
                    col = lax.broadcasted_iota(jnp.int32, (n, n), 1)
                    keep = jnp.logical_or(row >= col, true_row != true_col)
                    result[t, :, cols] = jnp.where(keep, rowl[t], 0.0).astype(BF16)

        writes[t].start()
    for copy in writes:
        copy.wait()


def update(scales, packed, arrays, nr, nc, tpr, tpc, n):
    geometry = (nr // nc, nr, nc, tpr, tpc, n)
    tall = arrays[-1].shape[1]
    return pl.pallas_call(
        functools.partial(update_kernel, geometry),
        out_shape=jax.ShapeDtypeStruct(packed.shape, BF16),
        in_specs=[SMEM, HBM] + [VMEM] * len(arrays),
        out_specs=HBM,
        scratch_shapes=[
            pltpu.VMEM((tpr, n, tpc * n), BF16),
            pltpu.VMEM((tpr, n, tpc * n), BF16),
            pltpu.VMEM((2, tall, n), BF16),
            pltpu.VMEM((tpr, n, 2 * n), BF16),
            pltpu.VMEM((tpc, 2 * n, n), BF16),
            pltpu.VMEM((tpr, n, n), F32),
            pltpu.VMEM(FACTORS.shape, BF16),
            pltpu.SemaphoreType.DMA((2, tpr)),
        ],
        compiler_params=pltpu.CompilerParams(vmem_limit_bytes=40 << 20),
        cost_estimate=pl.CostEstimate(flops=4_000_000_000, bytes_accessed=8 << 20, transcendentals=0),
        name="update_tiles",
    )(scales, packed, *arrays)


def on_device(nr, nc, packed, tile_scales):
    tpr, tpc = tile_scales.shape
    n = packed.shape[0] // tpr
    r = lax.axis_index("prow")
    c = lax.axis_index("pcol")
    def send(x, pairs):
        table = [(a * nc + b, d * nc + e) for (a, b), (d, e) in pairs]
        return lax.ppermute(x, ("prow", "pcol"), table)

    message, pivot = pl.pallas_call(
        pack_kernel,
        out_shape=(jax.ShapeDtypeStruct((tpr * n + EXTRA, n), BF16), jax.ShapeDtypeStruct((n + EXTRA, n), BF16)),
        in_specs=[SMEM, HBM],
        out_specs=(VMEM,) * 2,
        scratch_shapes=[pltpu.SemaphoreType.DMA((2,))],
        compiler_params=pltpu.CompilerParams(vmem_limit_bytes=48 << 20),
        name="pack_panel",
    )(tile_scales, pltpu.with_memory_space_constraint(packed, pltpu.HBM))

    came = []
    for k in range(nc):
        pairs = [((1, 0), (2, k)), ((1, 1), (4, (k + 1) % nc))]
        came.append(send(pivot, pairs + [((0, 0), (0, k))] * (k > 0)))
    index = jnp.where(r == 4, (c + nc - 1) % nc, c)
    tile = jnp.where((r == 0) & (c == 0), pivot, came[0])
    for k in range(1, nc):
        tile = jnp.where(index == k, came[k], tile)
    tiles = [tile]
    for mask in range(2, nr, 2):
        tiles.append(send(tile, [((a, e), (a ^ mask, e)) for a in (0, 2, 4) for e in range(nc)]))
    u = r % nc
    if nc == 4:
        first = {0: [(1, 0), (0, 2)], 1: [(0, 1), (1, 2)], 2: [(1, 2), (0, 1)], 3: [(1, 3), (0, 1)]}
        second = {0: [(1, 2), (0, 1)], 1: [(0, 2), (1, 0)], 2: [(0, 2), (1, 0)], 3: [(0, 3), (1, 0)]}
        turns = [[((a, x), (a, y)) for a in range(nr) for x, y in t[a % 4]] for t in (first, second)]
        got = [send(message, turn) for turn in turns]
        *tiles, got[0], got[1] = lax.optimization_barrier((*tiles, *got))
        swap = (u == 0) == (c >= 2)
        m0 = jnp.where(c == 0, message, jnp.where(swap, got[0], got[1]))
        m0 = jnp.where(c == 1, jnp.where(u == 0, got[1], got[0]), m0)
        m1 = jnp.where(c == 1, message, jnp.where(swap, got[1], got[0]))
        m1 = jnp.where(c == 0, jnp.where(u == 0, got[0], got[1]), m1)
        mine = jnp.stack([m0, m1])
        relayed = send(mine, [((a, 3), (a, 2)) if a % 4 == 3 else ((a, 2), (a, 3)) for a in range(nr)])
    else:
        m0 = message
        m1 = jnp.where(c == 1, message, 0)
        for k in range(1, nc):
            m0 = jnp.where(c == k, send(message, [((a, 0), (a, k)) for a in range(nr)]), m0)
        for k in range(nc):
            if k != 1:
                m1 = jnp.where(c == k, send(message, [((a, 1), (a, k)) for a in range(nr)]), m1)
        mine = jnp.stack([m0, m1])
        relayed = mine

    ratio = nr // nc
    near = []
    for mask in range(2, nr, 2):
        pairs = [((e + nc * g, e), ((e + nc * g) ^ mask, e)) for e in range(nc) for g in range(ratio)]
        near.append(send(mine, pairs))
    scratch = [pltpu.VMEM((n, n), F32)] * 2 + [pltpu.VMEM((HALF, HALF), F32)] * 3
    (factors,) = factor_call(factor_kernel, "factor_pivots", (FACTORS,), tuple(tiles), None, scratch, 4)
    factors_other = send(factors, [((a, e), (a + 1, e)) for a in range(0, nr, 2) for e in range(nc)])
    *near, _ = lax.optimization_barrier((*near, factors))
    cols = [mine] * ratio
    for k, got in enumerate(near):
        cols = [jnp.where((r ^ (c + nc * g)) // 2 == k + 1, got, cols[g]) for g in range(ratio)]
    pairs = [((a, e), (a ^ 1, e)) for a in range(nr) for e in range(nc) if a % 2 == e % 2]
    cols_other = [send(x, pairs) for x in cols]
    packed = pltpu.with_memory_space_constraint(packed, pltpu.HBM)
    arrays = (factors, factors_other, *cols, *cols_other, mine, relayed)
    return update(tile_scales, packed, arrays, nr, nc, tpr, tpc, n)


def solution(mesh):
    nr = mesh.shape["prow"]
    nc = mesh.shape["pcol"]
    return jax.shard_map(
        functools.partial(on_device, nr, nc),
        mesh=mesh,
        in_specs=(P("prow", "pcol"), P("prow", "pcol")),
        out_specs=P("prow", "pcol"),
        check_vma=False,
    )
```

```python
import functools

import jax
import jax.numpy as jnp
import numpy as np
from jax import lax
from jax.experimental import pallas as pl
from jax.experimental.pallas import tpu as pltpu
from jax.sharding import PartitionSpec as P

F32 = jnp.float32
BF16 = jnp.bfloat16
HALF = 128
EXTRA = 16


def dot_nt(a, b, precision=None):
    dims = (((1,), (1,)), ((), ()))
    return lax.dot_general(a, b, dims, precision=precision, preferred_element_type=F32)


def dot_nn(a, b, precision=None):
    dims = (((1,), (0,)), ((), ()))
    return lax.dot_general(a, b, dims, precision=precision, preferred_element_type=F32)


HIGHEST = lax.Precision.HIGHEST


def inverse_factor(a):
    n = a.shape[0]
    blocks = n // 8
    full = (8, n)
    rows = [a[8 * i : 8 * i + 8, :] for i in range(blocks)]
    lane = lax.broadcasted_iota(jnp.int32, full, 1)
    sub = lax.broadcasted_iota(jnp.int32, full, 0)

    def column(x, k):
        return jnp.broadcast_to(x[:, k : k + 1], full)

    def row(x, k):
        return jnp.broadcast_to(x[k : k + 1, :], full)

    out = []
    own = [column(rows[0], k) for k in range(8)]
    for t in range(blocks):
        base = 8 * t
        here = jnp.logical_and(lane >= base, lane < base + 8)
        s = {(j, k): row(own[k], j) for j in range(8) for k in range(j, 8)}
        c = {}
        for i in range(t + 1, blocks):
            for j in range(8):
                c[i, j] = column(rows[i], base + j)
        last = t + 1 == blocks
        if not last:
            own = [column(rows[t + 1], base + 8 + k) for k in range(8)]
        for i in range(t + 1, blocks):
            rows[i] = jnp.where(here, 0.0, rows[i])
        b = [jnp.where(here, jnp.where(lane == base + j, 1.0, 0.0), row(rows[t], j)) for j in range(8)]
        d = [] if last else [c[t + 1, j] for j in range(8)]
        m = {}
        z = []
        x = jnp.zeros(full, F32)
        for j in range(8):
            r0 = pl.reciprocal(s[j, j], approx=True)
            e = 2.0 - s[j, j] * r0
            r = r0 * e
            for k in range(j + 1, 8):
                m[j, k] = s[j, k] * r
            for k in range(j + 1, 8):
                for l in range(k, 8):
                    if k == j + 1 and l == k:
                        s[k, l] = s[k, l] - ((s[j, k] * s[j, k]) * r0) * e
                    else:
                        s[k, l] = s[k, l] - m[j, k] * s[j, l]
                b[k] = b[k] - m[j, k] * b[j]
            z.append(r * b[j])
            if not last:
                for k in range(j + 1, 8):
                    d[k] = d[k] - m[j, k] * d[j]
                w = d[j] * r
                own = [own[k] - w * row(d[j], k) for k in range(8)]
                rows[t + 1] = rows[t + 1] - d[j] * z[j]
            x = jnp.where(sub == j, lax.rsqrt(s[j, j]) * b[j], x)
        out.append(jnp.where(lane < base + 8, x, 0.0))
        if t + 2 < blocks:
            y = list(z)
            for k in range(7, 0, -1):
                for j in range(k):
                    y[j] = y[j] - m[j, k] * y[k]
            for i in range(t + 2, blocks):
                for j in range(8):
                    rows[i] = rows[i] - c[i, j] * y[j]
    return jnp.concatenate(out, axis=0)


def split(x):
    high = x.astype(BF16)
    return high, (x - high.astype(F32)).astype(BF16)


def scale_row(ref, tile, n):
    tail = ref[n:, :].astype(F32)
    return tail[3 * tile : 3 * tile + 1] + tail[3 * tile + 1 : 3 * tile + 2] + tail[3 * tile + 2 : 3 * tile + 3]


def first_half(tile, inv_ref, low_ref, rest_ref):
    x = inverse_factor(tile[:HALF, :HALF])
    factor = dot_nt(tile[HALF:, :HALF], x, HIGHEST)
    inv_ref[...] = x
    low_ref[...] = factor
    rest_ref[...] = tile[HALF:, HALF:] - dot_nt(factor, factor, HIGHEST)


def second_half(inv_ref, low_ref, rest_ref, out_ref):
    x22 = inverse_factor(rest_ref[...])
    x11 = inv_ref[...]
    x21 = -dot_nn(x22, dot_nn(low_ref[...], x11, HIGHEST), HIGHEST)
    for k, x in enumerate((x11, x21, x22)):
        out_ref[k], out_ref[k + 3] = split(x)


def scale_tail(scales, n):
    row = lax.broadcasted_iota(jnp.int32, (EXTRA, n), 0)
    total = jnp.zeros((EXTRA, n), F32)
    for t in range(scales.shape[0]):
        rest = jnp.full((EXTRA, n), scales[t, 0], F32)
        for k in range(3):
            part = rest.astype(BF16).astype(F32)
            total = jnp.where(row == 3 * t + k, part, total)
            rest = rest - part
    return total.astype(BF16)


def pack_kernel(scales, packed, message, pivot, sem):
    n = pivot.shape[1]
    tall = message.shape[0] - EXTRA
    tile_copy = pltpu.make_async_copy(packed.at[0:n, 0:n], pivot.at[0:n], sem.at[0])
    block_copy = pltpu.make_async_copy(packed.at[:, 0:n], message.at[0:tall], sem.at[1])
    tile_copy.start()
    block_copy.start()
    tail = scale_tail(scales, n)
    pivot[n:, :] = tail
    message[tall:, :] = tail
    tile_copy.wait()
    block_copy.wait()


def take(tiles, mask, target):
    for k, tile in enumerate(tiles):

        @pl.when(mask == 2 * k)
        def _(tile=tile):
            n = target.shape[0]
            target[...] = tile[:n, :].astype(F32) * scale_row(tile, 0, n)


def first_kernel(*refs):
    tiles, out_ref, tile, inv, low, rest = refs[:-5], *refs[-5:]
    r = lax.axis_index("prow")

    @pl.when(r % 2 == 0)
    def _():
        take(tiles, r, tile)
        first_half(tile, inv, low, rest)
        second_half(inv, low, rest, out_ref)


def second_kernel(x0, *refs):
    tiles, out_ref, left, tile, inv, low, rest = refs[:-6], *refs[-6:]
    n = 2 * HALF
    r = lax.axis_index("prow")

    @pl.when(r % 2 == 0)
    def _():
        out_ref[0:6] = x0[...]
        take(tiles, r ^ 2, left)
        take(tiles, r ^ 4, tile)
        high, part = split(left[...])
        cat = join(x0, 0)
        both = jnp.concatenate([cat[:, :n], cat[:, :n], cat[:, n:]], axis=1)
        panel = dot_nt(jnp.concatenate([high, part, high], axis=1), both).astype(BF16)
        for k in range(4):
            i, j = divmod(k, 2)
            out_ref[12 + k] = panel[i * HALF : (i + 1) * HALF, j * HALF : (j + 1) * HALF]
        tile[...] = tile[...] - dot_nt(panel, panel)
        first_half(tile, inv, low, rest)
        second_half(inv, low, rest, out_ref.at[6:12])


def join(x, base):
    zero = jnp.zeros((HALF, HALF), BF16)
    upper = jnp.concatenate([x[base], zero, x[base + 3], zero], axis=1)
    lower = jnp.concatenate([x[base + 1], x[base + 2], x[base + 4], x[base + 5]], axis=1)
    return jnp.concatenate([upper, lower], axis=0)


VMEM = pl.BlockSpec(memory_space=pltpu.VMEM)
SMEM = pl.BlockSpec(memory_space=pltpu.SMEM)
HBM = pl.BlockSpec(memory_space=pltpu.HBM)
BLOCK = jax.ShapeDtypeStruct((HALF, HALF), F32)
PARTS = jax.ShapeDtypeStruct((6, HALF, HALF), BF16)
FACTORS = jax.ShapeDtypeStruct((16, HALF, HALF), BF16)


def factor_call(kernel, name, outs, args, specs=None, scratch=(), work=1):
    return pl.pallas_call(
        kernel,
        out_shape=outs,
        in_specs=specs or [VMEM] * len(args),
        out_specs=(VMEM,) * len(outs),
        scratch_shapes=scratch,
        compiler_params=pltpu.CompilerParams(vmem_limit_bytes=24 << 20),
        cost_estimate=pl.CostEstimate(flops=work * 5_000_000_000, bytes_accessed=1 << 20, transcendentals=0),
        name=name,
    )(*args)


def update_kernel(geometry, table, scales, packed, factors, factors_other, *rest):
    ratio, nr, nc, tpr, tpc, n, count = geometry
    here = (rest[0:2], rest[2:4])
    there = (rest[4:6], rest[6:8])
    blocks = rest[8 : 8 + count]
    out, stored, result, block, rowp, colp, rowl, xs, sem = rest[8 + count :]
    r = lax.axis_index("prow")
    c = lax.axis_index("pcol")
    tall = tpr * n

    reads = [pltpu.make_async_copy(packed.at[t * n : (t + 1) * n], stored.at[t], sem.at[0, t]) for t in range(tpr)]
    writes = [pltpu.make_async_copy(result.at[t], out.at[t * n : (t + 1) * n], sem.at[1, t]) for t in range(tpr)]
    for copy in reads:
        copy.start()

    def when(condition, target, value):
        @pl.when(condition)
        def _():
            target[...] = value[...]

    when(r % 2 == 0, xs, factors)
    when(r % 2 == 1, xs, factors_other)
    cat0 = join(xs, 0).T
    cat1 = join(xs, 6).T
    cat1 = jnp.concatenate([cat1[:n], cat1[:n], cat1[n:]], axis=0)
    panel = jnp.concatenate(
        [jnp.concatenate([xs[12], xs[13]], axis=1), jnp.concatenate([xs[14], xs[15]], axis=1)], axis=0
    ).T

    def solve(each):
        for t in range(tpr):
            rows = slice(t * n, (t + 1) * n)
            a0 = block[0, rows, :]
            raw0 = dot_nn(jnp.concatenate([a0, a0], axis=1), cat0)
            p0 = (raw0 * scale_row(block[0], t, tall)).astype(BF16)
            s1 = scale_row(block[1], t, tall)
            left = block[1, rows, :].astype(F32) * s1 - dot_nn(p0, panel)
            high, low = split(left)
            f1 = dot_nn(jnp.concatenate([high, low, high], axis=1), cat1)
            each(t, raw0, f1, s1, p0, f1.astype(BF16))

    same = (r % 2) == (c % 2)
    early = jnp.where(c < 2, 0, 1)
    swap = r // 4 if (nr, nc) == (8, 4) else 0
    for g in range(ratio):
        for slot in range(ratio):
            chosen = (swap ^ g) == slot
            when(jnp.logical_and(chosen, same), block.at[early], here[0][slot])
            when(jnp.logical_and(chosen, jnp.logical_not(same)), block.at[early], there[0][slot])
        when(same, block.at[1 - early], here[1][g])
        when(jnp.logical_not(same), block.at[1 - early], there[1][g])

        def keep_column(t, raw0, f1, s1, p0, p1, g=g):
            colp[t * ratio + g, :n, :] = p0.T
            colp[t * ratio + g, n:, :] = p1.T

        solve(keep_column)

    for panel_index in range(2):
        index = table[2 * (r * nc + c) + panel_index]
        for k in range(count):
            when(index == k, block.at[panel_index], blocks[k])

    def keep_row(t, raw0, f1, s1, p0, p1):
        rowp[t, :, :n] = p0
        rowp[t, :, n:] = p1

        @pl.when(c == 0)
        def _():
            rowl[t] = raw0

        @pl.when(c == 1)
        def _():
            rowl[t] = f1 / s1

    solve(keep_row)

    for t in range(tpr):
        reads[t].wait()
        true_row = t * nr + r
        for q in range(tpc):
            true_col = q * nc + c
            cols = slice(q * n, (q + 1) * n)

            @pl.when(true_row < true_col)
            def _():
                result[t, :, cols] = stored[t, :, cols]

            @pl.when(jnp.logical_and(true_row >= true_col, true_col >= 2))
            def _():
                change = dot_nn(rowp[t], colp[q])
                inverse = 1.0 / jnp.full((1, n), scales[t, q], F32)
                result[t, :, cols] = (stored[t, :, cols].astype(F32) - change * inverse).astype(BF16)

            if q * nc < 2:

                @pl.when(jnp.logical_and(true_row >= true_col, true_col < 2))
                def _():
                    row = lax.broadcasted_iota(jnp.int32, (n, n), 0)
                    col = lax.broadcasted_iota(jnp.int32, (n, n), 1)
                    keep = jnp.logical_or(row >= col, true_row != true_col)
                    result[t, :, cols] = jnp.where(keep, rowl[t], 0.0).astype(BF16)

        writes[t].start()
    for copy in writes:
        copy.wait()


def update(table, scales, packed, arrays, blocks, nr, nc, tpr, tpc, n):
    geometry = (nr // nc, nr, nc, tpr, tpc, n, len(blocks))
    tall = blocks[0].shape[0]
    return pl.pallas_call(
        functools.partial(update_kernel, geometry),
        out_shape=jax.ShapeDtypeStruct(packed.shape, BF16),
        in_specs=[SMEM, SMEM, HBM] + [VMEM] * (len(arrays) + len(blocks)),
        out_specs=HBM,
        scratch_shapes=[
            pltpu.VMEM((tpr, n, tpc * n), BF16),
            pltpu.VMEM((tpr, n, tpc * n), BF16),
            pltpu.VMEM((2, tall, n), BF16),
            pltpu.VMEM((tpr, n, 2 * n), BF16),
            pltpu.VMEM((tpc, 2 * n, n), BF16),
            pltpu.VMEM((tpr, n, n), F32),
            pltpu.VMEM(FACTORS.shape, BF16),
            pltpu.SemaphoreType.DMA((2, tpr)),
        ],
        compiler_params=pltpu.CompilerParams(vmem_limit_bytes=40 << 20),
        cost_estimate=pl.CostEstimate(flops=4_000_000_000, bytes_accessed=8 << 20, transcendentals=0),
        name="update_tiles",
    )(table, scales, packed, *arrays, *blocks)


def row_plan(nr, nc):
    if (nr, nc) == (8, 4):
        first = {0: [(1, 2)], 1: [(0, 1), (1, 2)], 4: [(1, 0), (0, 2)], 5: [(0, 1), (1, 2)]}
        second = {0: [(0, 1), (1, 0)], 1: [(1, 0)], 4: [(1, 2), (0, 1)], 5: [(0, 2), (1, 0)]}
        third = {0: [(0, 2), (2, 3, 1)], 1: [(0, 2), (2, 3, 1)], 4: [(2, 3, 1)], 5: [(2, 3, 1)]}
        fourth = {0: [(2, 3, 3)], 1: [(2, 3, 3)], 4: [(2, 3, 2)], 5: [(2, 3, 2)]}
        for r in (2, 6, 3, 7):
            u = r % 4
            first[r] = [(1, u), (0, 1)]
            second[r] = [(0, u), (1, 0)]
            third[r] = [(u, 5 - u, 1)]
            fourth[r] = [(u, 5 - u, 2)]
        turns = (first, second, third, fourth)
        return [[(r, *move[:2], move[2] if len(move) > 2 else 0) for r in turn for move in turn[r]] for turn in turns]
    rounds = [[], []]
    for r in range(nr):
        want = r % nc
        rounds[0].append((r, 0, 1, 0) if want == 1 else (r, 1, want, 0))
        if want > 1:
            rounds[1].append((r, 0, want, 0))
    done = {move[:3] for turn in rounds for move in turn}
    for shift in range(1, nc):
        moves = [(r, a, (a + shift) % nc, 0) for r in range(nr) for a in range(2)]
        rounds.append([move for move in moves if move[:3] not in done])
    return rounds


def on_device(nr, nc, packed, tile_scales):
    tpr, tpc = tile_scales.shape
    n = packed.shape[0] // tpr
    r = lax.axis_index("prow")
    c = lax.axis_index("pcol")
    def choose(options, index):
        value = options[0]
        for k in range(1, len(options)):
            value = jnp.where(index == k, options[k], value)
        return value

    def send(x, pairs):
        table = [(a * nc + b, d * nc + e) for (a, b), (d, e) in pairs]
        return lax.ppermute(x, ("prow", "pcol"), table)

    message, pivot = pl.pallas_call(
        pack_kernel,
        out_shape=(jax.ShapeDtypeStruct((tpr * n + EXTRA, n), BF16), jax.ShapeDtypeStruct((n + EXTRA, n), BF16)),
        in_specs=[SMEM, HBM],
        out_specs=(VMEM,) * 2,
        scratch_shapes=[pltpu.SemaphoreType.DMA((2,))],
        compiler_params=pltpu.CompilerParams(vmem_limit_bytes=48 << 20),
        name="pack_panel",
    )(tile_scales, pltpu.with_memory_space_constraint(packed, pltpu.HBM))

    came = []
    for k in range(nc):
        pairs = [((1, 0), (2, k)), ((1, 1), (4, (k + 1) % nc))]
        came.append(send(pivot, pairs + [((0, 0), (0, k))] * (k > 0)))
    index = jnp.where(r == 4, (c + nc - 1) % nc, c)
    tile = jnp.where((r == 0) & (c == 0), pivot, came[0])
    for k in range(1, nc):
        tile = jnp.where(index == k, came[k], tile)
    tiles = [tile]
    for mask in range(2, nr, 2):
        tiles.append(send(tile, [((a, e), (a ^ mask, e)) for a in (0, 2, 4) for e in range(nc)]))
    rounds = row_plan(nr, nc)
    blocks = [message]
    holds = {(a, p, p): 0 for a in range(nr) for p in range(2)}

    def send_round(turn):
        used = sorted({k for *_, k in turn})
        operand = blocks[used[0]]
        for k in used[1:]:
            hits = [r * nc + c == a * nc + b for a, b, _, j in turn if j == k]
            operand = jnp.where(functools.reduce(jnp.logical_or, hits), blocks[k], operand)
        for a, b, d, k in turn:
            panel = next(p for p in range(2) if holds.get((a, b, p)) == k)
            holds[a, d, panel] = len(blocks)
        blocks.append(send(operand, [((a, b), (a, d)) for a, b, d, _ in turn]))

    send_round(rounds[0])
    send_round(rounds[1])
    u = r % nc
    ratio = nr // nc
    grid = (nr, nc) == (8, 4)
    parity = [((a, e), (a ^ 4, e)) for a in range(nr) for e in range(nc) if a % 2 == e % 2]

    def star(x):
        near = [x]
        for mask in range(2, nr, 2):
            pairs = [((e + nc * g, e), ((e + nc * g) ^ mask, e)) for e in range(nc) for g in range(ratio)]
            near.append(send(x, pairs))
        return near

    def ends(near):
        return [choose(near, (r ^ (c + nc * g)) // 2) for g in range(ratio)]

    *tiles, blocks[0], blocks[1] = lax.optimization_barrier((*tiles, *blocks[:2]))
    early = jnp.where(c == 0, blocks[0], blocks[1])
    if grid:
        near = [early, send(early, [((e + 4 * g, e), ((e + 4 * g) ^ 2, e)) for e in range(nc) for g in range(2)])]
    else:
        near = star(early)
    square = pltpu.VMEM((n, n), F32)
    blank = [pltpu.VMEM((HALF, HALF), F32)] * 3
    (x0,) = factor_call(first_kernel, "factor_first", (PARTS,), tuple(tiles), None, [square] + blank, 2)

    x0, *rest = lax.optimization_barrier((x0, *near, *blocks))
    near, blocks = rest[: len(near)], rest[len(near) :]
    if grid:
        side = jnp.where(u == c, *near)
        cols = [side, send(side, parity)]
        late = jnp.where(r == 0, blocks[2], blocks[1])
    else:
        cols = ends(near)
        late = blocks[1]
    near = star(jnp.where(c == 0, late, jnp.where(c == 1, blocks[0], blocks[2])))
    send_round(rounds[2])
    scratch = [square] * 2 + blank
    (factors,) = factor_call(second_kernel, "factor_second", (FACTORS,), (x0, *tiles), None, scratch, 2)
    factors, *rest = lax.optimization_barrier((factors, *cols, *near, *blocks[3:]))
    cols, near, blocks[3:] = rest[:ratio], rest[ratio : ratio + len(near)], rest[ratio + len(near) :]
    cols += ends(near)

    factors_other = send(factors, [((a, e), (a + 1, e)) for a in range(0, nr, 2) for e in range(nc)])
    for turn in rounds[3:]:
        send_round(turn)
    pairs = [((a, e), (a ^ 1, e)) for a in range(nr) for e in range(nc) if a % 2 == e % 2]
    cols_other = [send(x, pairs) for x in cols]
    table = np.array([holds[a, b, p] for a in range(nr) for b in range(nc) for p in range(2)], np.int32)
    packed = pltpu.with_memory_space_constraint(packed, pltpu.HBM)
    return update(table, tile_scales, packed, (factors, factors_other, *cols, *cols_other), blocks, nr, nc, tpr, tpc, n)


def solution(mesh):
    nr = mesh.shape["prow"]
    nc = mesh.shape["pcol"]
    return jax.shard_map(
        functools.partial(on_device, nr, nc),
        mesh=mesh,
        in_specs=(P("prow", "pcol"), P("prow", "pcol")),
        out_specs=P("prow", "pcol"),
        check_vma=False,
    )
```

```python
import functools

import jax
import jax.numpy as jnp
import numpy as np
from jax import lax
from jax.experimental import pallas as pl
from jax.experimental.pallas import tpu as pltpu
from jax.sharding import PartitionSpec as P

F32 = jnp.float32
BF16 = jnp.bfloat16
HALF = 128
EXTRA = 16


def dot_nt(a, b, precision=None):
    dims = (((1,), (1,)), ((), ()))
    return lax.dot_general(a, b, dims, precision=precision, preferred_element_type=F32)


def dot_nn(a, b, precision=None):
    dims = (((1,), (0,)), ((), ()))
    return lax.dot_general(a, b, dims, precision=precision, preferred_element_type=F32)


HIGHEST = lax.Precision.HIGHEST


def inverse_factor(a):
    n = a.shape[0]
    blocks = n // 8
    full = (8, n)
    rows = [a[8 * i : 8 * i + 8, :] for i in range(blocks)]
    lane = lax.broadcasted_iota(jnp.int32, full, 1)
    sub = lax.broadcasted_iota(jnp.int32, full, 0)

    def column(x, k):
        return jnp.broadcast_to(x[:, k : k + 1], full)

    def row(x, k):
        return jnp.broadcast_to(x[k : k + 1, :], full)

    out = []
    own = [column(rows[0], k) for k in range(8)]
    for t in range(blocks):
        base = 8 * t
        here = jnp.logical_and(lane >= base, lane < base + 8)
        s = {(j, k): row(own[k], j) for j in range(8) for k in range(j, 8)}
        c = {}
        for i in range(t + 1, blocks):
            for j in range(8):
                c[i, j] = column(rows[i], base + j)
        last = t + 1 == blocks
        if not last:
            own = [column(rows[t + 1], base + 8 + k) for k in range(8)]
        for i in range(t + 1, blocks):
            rows[i] = jnp.where(here, 0.0, rows[i])
        b = [jnp.where(here, jnp.where(lane == base + j, 1.0, 0.0), row(rows[t], j)) for j in range(8)]
        d = [] if last else [c[t + 1, j] for j in range(8)]
        m = {}
        z = []
        x = jnp.zeros(full, F32)
        for j in range(8):
            r0 = pl.reciprocal(s[j, j], approx=True)
            e = 2.0 - s[j, j] * r0
            r = r0 * e
            for k in range(j + 1, 8):
                m[j, k] = s[j, k] * r
            for k in range(j + 1, 8):
                for l in range(k, 8):
                    if k == j + 1 and l == k:
                        s[k, l] = s[k, l] - ((s[j, k] * s[j, k]) * r0) * e
                    else:
                        s[k, l] = s[k, l] - m[j, k] * s[j, l]
                b[k] = b[k] - m[j, k] * b[j]
            z.append(r * b[j])
            if not last:
                for k in range(j + 1, 8):
                    d[k] = d[k] - m[j, k] * d[j]
                w = d[j] * r
                own = [own[k] - w * row(d[j], k) for k in range(8)]
                rows[t + 1] = rows[t + 1] - d[j] * z[j]
            x = jnp.where(sub == j, lax.rsqrt(s[j, j]) * b[j], x)
        out.append(jnp.where(lane < base + 8, x, 0.0))
        if t + 2 < blocks:
            y = list(z)
            for k in range(7, 0, -1):
                for j in range(k):
                    y[j] = y[j] - m[j, k] * y[k]
            for i in range(t + 2, blocks):
                for j in range(8):
                    rows[i] = rows[i] - c[i, j] * y[j]
    return jnp.concatenate(out, axis=0)


def split(x):
    high = x.astype(BF16)
    return high, (x - high.astype(F32)).astype(BF16)


def scale_row(ref, tile, n):
    tail = ref[n:, :].astype(F32)
    return tail[3 * tile : 3 * tile + 1] + tail[3 * tile + 1 : 3 * tile + 2] + tail[3 * tile + 2 : 3 * tile + 3]


def first_half(tile, inv_ref, low_ref, rest_ref):
    x = inverse_factor(tile[:HALF, :HALF])
    factor = dot_nt(tile[HALF:, :HALF], x, HIGHEST)
    inv_ref[...] = x
    low_ref[...] = factor
    rest_ref[...] = tile[HALF:, HALF:] - dot_nt(factor, factor, HIGHEST)


def second_half(inv_ref, low_ref, rest_ref, out_ref):
    x22 = inverse_factor(rest_ref[...])
    x11 = inv_ref[...]
    x21 = -dot_nn(x22, dot_nn(low_ref[...], x11, HIGHEST), HIGHEST)
    for k, x in enumerate((x11, x21, x22)):
        out_ref[k], out_ref[k + 3] = split(x)


def scale_tail(scales, n):
    row = lax.broadcasted_iota(jnp.int32, (EXTRA, n), 0)
    total = jnp.zeros((EXTRA, n), F32)
    for t in range(scales.shape[0]):
        rest = jnp.full((EXTRA, n), scales[t, 0], F32)
        for k in range(3):
            part = rest.astype(BF16).astype(F32)
            total = jnp.where(row == 3 * t + k, part, total)
            rest = rest - part
    return total.astype(BF16)


def pack_kernel(scales, packed, message, pivot, sem):
    n = pivot.shape[1]
    tall = message.shape[0] - EXTRA
    tile_copy = pltpu.make_async_copy(packed.at[0:n, 0:n], pivot.at[0:n], sem.at[0])
    block_copy = pltpu.make_async_copy(packed.at[:, 0:n], message.at[0:tall], sem.at[1])
    tile_copy.start()
    block_copy.start()
    tail = scale_tail(scales, n)
    pivot[n:, :] = tail
    message[tall:, :] = tail
    tile_copy.wait()
    block_copy.wait()


def take(tiles, mask, target):
    for k, tile in enumerate(tiles):

        @pl.when(mask == 2 * k)
        def _(tile=tile):
            n = target.shape[0]
            target[...] = tile[:n, :].astype(F32) * scale_row(tile, 0, n)


def first_kernel(*refs):
    tiles, out_ref, tile, inv, low, rest = refs[:-5], *refs[-5:]
    r = lax.axis_index("prow")

    @pl.when(r % 2 == 0)
    def _():
        take(tiles, r, tile)
        first_half(tile, inv, low, rest)
        second_half(inv, low, rest, out_ref)


def second_kernel(x0, *refs):
    tiles, out_ref, left, tile, inv, low, rest = refs[:-6], *refs[-6:]
    n = 2 * HALF
    r = lax.axis_index("prow")

    @pl.when(r % 2 == 0)
    def _():
        out_ref[0:6] = x0[...]
        take(tiles, r ^ 2, left)
        take(tiles, r ^ 4, tile)
        high, part = split(left[...])
        cat = join(x0, 0)
        both = jnp.concatenate([cat[:, :n], cat[:, :n], cat[:, n:]], axis=1)
        panel = dot_nt(jnp.concatenate([high, part, high], axis=1), both).astype(BF16)
        for k in range(4):
            i, j = divmod(k, 2)
            out_ref[12 + k] = panel[i * HALF : (i + 1) * HALF, j * HALF : (j + 1) * HALF]
        tile[...] = tile[...] - dot_nt(panel, panel)
        first_half(tile, inv, low, rest)
        second_half(inv, low, rest, out_ref.at[6:12])


def join(x, base):
    zero = jnp.zeros((HALF, HALF), BF16)
    upper = jnp.concatenate([x[base], zero, x[base + 3], zero], axis=1)
    lower = jnp.concatenate([x[base + 1], x[base + 2], x[base + 4], x[base + 5]], axis=1)
    return jnp.concatenate([upper, lower], axis=0)


VMEM = pl.BlockSpec(memory_space=pltpu.VMEM)
SMEM = pl.BlockSpec(memory_space=pltpu.SMEM)
HBM = pl.BlockSpec(memory_space=pltpu.HBM)
BLOCK = jax.ShapeDtypeStruct((HALF, HALF), F32)
PARTS = jax.ShapeDtypeStruct((6, HALF, HALF), BF16)
FACTORS = jax.ShapeDtypeStruct((16, HALF, HALF), BF16)


def factor_call(kernel, name, outs, args, specs=None, scratch=(), work=1):
    return pl.pallas_call(
        kernel,
        out_shape=outs,
        in_specs=specs or [VMEM] * len(args),
        out_specs=(VMEM,) * len(outs),
        scratch_shapes=scratch,
        compiler_params=pltpu.CompilerParams(vmem_limit_bytes=24 << 20),
        cost_estimate=pl.CostEstimate(flops=work * 5_000_000_000, bytes_accessed=0, transcendentals=0),
        name=name,
    )(*args)


def update_kernel(geometry, scales, packed, factors, factors_other, *rest):
    ratio, nr, nc, tpr, tpc, n = geometry
    here, there, mine, relayed = rest[0:2], rest[2:4], rest[4], rest[5]
    out, stored, result, block, rowp, colp, rowl, xs, sem = rest[6:]
    r = lax.axis_index("prow")
    c = lax.axis_index("pcol")
    tall = tpr * n

    reads = [pltpu.make_async_copy(packed.at[t * n : (t + 1) * n], stored.at[t], sem.at[0, t]) for t in range(tpr)]
    writes = [pltpu.make_async_copy(result.at[t], out.at[t * n : (t + 1) * n], sem.at[1, t]) for t in range(tpr)]
    for copy in reads:
        copy.start()

    def when(condition, target, value):
        @pl.when(condition)
        def _():
            target[...] = value[...]

    when(r % 2 == 0, xs, factors)
    when(r % 2 == 1, xs, factors_other)
    cat0 = join(xs, 0).T
    cat1 = join(xs, 6).T
    cat1 = jnp.concatenate([cat1[:n], cat1[:n], cat1[n:]], axis=0)
    panel = jnp.concatenate(
        [jnp.concatenate([xs[12], xs[13]], axis=1), jnp.concatenate([xs[14], xs[15]], axis=1)], axis=0
    ).T

    def solve(each):
        for t in range(tpr):
            rows = slice(t * n, (t + 1) * n)
            a0 = block[0, rows, :]
            raw0 = dot_nn(jnp.concatenate([a0, a0], axis=1), cat0)
            p0 = (raw0 * scale_row(block[0], t, tall)).astype(BF16)
            s1 = scale_row(block[1], t, tall)
            left = block[1, rows, :].astype(F32) * s1 - dot_nn(p0, panel)
            high, low = split(left)
            f1 = dot_nn(jnp.concatenate([high, low, high], axis=1), cat1)
            each(t, raw0, f1, s1, p0, f1.astype(BF16))

    same = (r % 2) == (c % 2)
    early = jnp.where(c < 2, 0, 1)
    for g in range(ratio):
        for half, panel_index in enumerate((early, 1 - early)):
            when(same, block.at[panel_index], here[g].at[half])
            when(jnp.logical_not(same), block.at[panel_index], there[g].at[half])

        def keep_column(t, raw0, f1, s1, p0, p1, g=g):
            colp[t * ratio + g, :n, :] = p0.T
            colp[t * ratio + g, n:, :] = p1.T

        solve(keep_column)

    late = jnp.logical_and(nc == 4, jnp.where(r % 4 == 3, c == 2, c == 3))
    when(late, block, relayed)
    when(jnp.logical_not(late), block, mine)

    def keep_row(t, raw0, f1, s1, p0, p1):
        rowp[t, :, :n] = p0
        rowp[t, :, n:] = p1

        @pl.when(c == 0)
        def _():
            rowl[t] = raw0

        @pl.when(c == 1)
        def _():
            rowl[t] = f1 / s1

    solve(keep_row)

    for t in range(tpr):
        reads[t].wait()
        true_row = t * nr + r
        for q in range(tpc):
            true_col = q * nc + c
            cols = slice(q * n, (q + 1) * n)

            @pl.when(true_row < true_col)
            def _():
                result[t, :, cols] = stored[t, :, cols]

            @pl.when(jnp.logical_and(true_row >= true_col, true_col >= 2))
            def _():
                change = dot_nn(rowp[t], colp[q])
                inverse = 1.0 / jnp.full((1, n), scales[t, q], F32)
                result[t, :, cols] = (stored[t, :, cols].astype(F32) - change * inverse).astype(BF16)

            if q * nc < 2:

                @pl.when(jnp.logical_and(true_row >= true_col, true_col < 2))
                def _():
                    row = lax.broadcasted_iota(jnp.int32, (n, n), 0)
                    col = lax.broadcasted_iota(jnp.int32, (n, n), 1)
                    keep = jnp.logical_or(row >= col, true_row != true_col)
                    result[t, :, cols] = jnp.where(keep, rowl[t], 0.0).astype(BF16)

        writes[t].start()
    for copy in writes:
        copy.wait()


def update(scales, packed, arrays, nr, nc, tpr, tpc, n):
    geometry = (nr // nc, nr, nc, tpr, tpc, n)
    tall = arrays[-1].shape[1]
    return pl.pallas_call(
        functools.partial(update_kernel, geometry),
        out_shape=jax.ShapeDtypeStruct(packed.shape, BF16),
        in_specs=[SMEM, HBM] + [VMEM] * len(arrays),
        out_specs=HBM,
        scratch_shapes=[
            pltpu.VMEM((tpr, n, tpc * n), BF16),
            pltpu.VMEM((tpr, n, tpc * n), BF16),
            pltpu.VMEM((2, tall, n), BF16),
            pltpu.VMEM((tpr, n, 2 * n), BF16),
            pltpu.VMEM((tpc, 2 * n, n), BF16),
            pltpu.VMEM((tpr, n, n), F32),
            pltpu.VMEM(FACTORS.shape, BF16),
            pltpu.SemaphoreType.DMA((2, tpr)),
        ],
        compiler_params=pltpu.CompilerParams(vmem_limit_bytes=40 << 20),
        cost_estimate=pl.CostEstimate(flops=4_000_000_000, bytes_accessed=8 << 20, transcendentals=0),
        name="update_tiles",
    )(scales, packed, *arrays)


def on_device(nr, nc, packed, tile_scales):
    tpr, tpc = tile_scales.shape
    n = packed.shape[0] // tpr
    r = lax.axis_index("prow")
    c = lax.axis_index("pcol")
    def choose(options, index):
        value = options[0]
        for k in range(1, len(options)):
            value = jnp.where(index == k, options[k], value)
        return value

    def send(x, pairs):
        table = [(a * nc + b, d * nc + e) for (a, b), (d, e) in pairs]
        return lax.ppermute(x, ("prow", "pcol"), table)

    message, pivot = pl.pallas_call(
        pack_kernel,
        out_shape=(jax.ShapeDtypeStruct((tpr * n + EXTRA, n), BF16), jax.ShapeDtypeStruct((n + EXTRA, n), BF16)),
        in_specs=[SMEM, HBM],
        out_specs=(VMEM,) * 2,
        scratch_shapes=[pltpu.SemaphoreType.DMA((2,))],
        compiler_params=pltpu.CompilerParams(vmem_limit_bytes=48 << 20),
        name="pack_panel",
    )(tile_scales, pltpu.with_memory_space_constraint(packed, pltpu.HBM))

    came = []
    for k in range(nc):
        pairs = [((1, 0), (2, k)), ((1, 1), (4, (k + 1) % nc))]
        came.append(send(pivot, pairs + [((0, 0), (0, k))] * (k > 0)))
    index = jnp.where(r == 4, (c + nc - 1) % nc, c)
    tile = jnp.where((r == 0) & (c == 0), pivot, came[0])
    for k in range(1, nc):
        tile = jnp.where(index == k, came[k], tile)
    tiles = [tile]
    for mask in range(2, nr, 2):
        tiles.append(send(tile, [((a, e), (a ^ mask, e)) for a in (0, 2, 4) for e in range(nc)]))
    u = r % nc
    if nc == 4:
        first = {0: [(1, 0), (0, 2)], 1: [(0, 1), (1, 2)], 2: [(1, 2), (0, 1)], 3: [(1, 3), (0, 1)]}
        second = {0: [(1, 2), (0, 1)], 1: [(0, 2), (1, 0)], 2: [(0, 2), (1, 0)], 3: [(0, 3), (1, 0)]}
        turns = [[((a, x), (a, y)) for a in range(nr) for x, y in t[a % 4]] for t in (first, second)]
        got = [send(message, turn) for turn in turns]
    else:
        got = [jnp.zeros_like(message)] * 2
        for panel in range(2):
            for k in range(nc):
                if k != panel:
                    came = send(message, [((a, panel), (a, k)) for a in range(nr)])
                    slot = panel if k == 0 else 1 - panel if k > 1 else 0
                    got[slot] = jnp.where(c == k, came, got[slot])
    *tiles, got[0] = lax.optimization_barrier((*tiles, got[0]))

    ratio = nr // nc

    def star(x):
        near = [x]
        for mask in range(2, nr, 2):
            pairs = [((e + nc * g, e), ((e + nc * g) ^ mask, e)) for e in range(nc) for g in range(ratio)]
            near.append(send(x, pairs))
        return near

    early = star(jnp.where(c == 0, message, got[0]))
    square = pltpu.VMEM((n, n), F32)
    blank = [pltpu.VMEM((HALF, HALF), F32)] * 3
    (x0,) = factor_call(first_kernel, "factor_first", (PARTS,), tuple(tiles), None, [square] + blank, 0)
    x0, *got = lax.optimization_barrier((x0, *got))
    if nc == 4:
        swap = (u == 0) == (c >= 2)
        m0 = jnp.where(c == 0, message, jnp.where(swap, got[0], got[1]))
        m0 = jnp.where(c == 1, jnp.where(u == 0, got[1], got[0]), m0)
        m1 = jnp.where(c == 1, message, jnp.where(swap, got[1], got[0]))
        m1 = jnp.where(c == 0, jnp.where(u == 0, got[0], got[1]), m1)
        mine = jnp.stack([m0, m1])
        relayed = send(mine, [((a, 3), (a, 2)) if a % 4 == 3 else ((a, 2), (a, 3)) for a in range(nr)])
    else:
        m0 = jnp.where(c == 0, message, jnp.where(c == 1, got[0], got[1]))
        mine = jnp.stack([m0, jnp.where(c == 1, message, got[0])])
        relayed = mine
    late = star(jnp.where(c == 0, got[0], jnp.where(c == 1, message, got[1])))
    scratch = [square] * 2 + blank
    (factors,) = factor_call(second_kernel, "factor_second", (FACTORS,), (x0, *tiles), None, scratch, 2)

    factors_other = send(factors, [((a, e), (a + 1, e)) for a in range(0, nr, 2) for e in range(nc)])
    factors, *near = lax.optimization_barrier((factors, *early, *late))
    early, late = near[: len(early)], near[len(early) :]
    cols = []
    for g in range(ratio):
        mask = (r ^ (c + nc * g)) // 2
        cols.append(jnp.stack([choose(early, mask), choose(late, mask)]))
    pairs = [((a, e), (a ^ 1, e)) for a in range(nr) for e in range(nc) if a % 2 == e % 2]
    cols_other = [send(x, pairs) for x in cols]
    packed = pltpu.with_memory_space_constraint(packed, pltpu.HBM)
    arrays = (factors, factors_other, *cols, *cols_other, mine, relayed)
    return update(tile_scales, packed, arrays, nr, nc, tpr, tpc, n)


def solution(mesh):
    nr = mesh.shape["prow"]
    nc = mesh.shape["pcol"]
    return jax.shard_map(
        functools.partial(on_device, nr, nc),
        mesh=mesh,
        in_specs=(P("prow", "pcol"), P("prow", "pcol")),
        out_specs=P("prow", "pcol"),
        check_vma=False,
    )
```

```python
import functools

import jax
import jax.numpy as jnp
import numpy as np
from jax import lax
from jax.experimental import pallas as pl
from jax.experimental.pallas import tpu as pltpu
from jax.sharding import PartitionSpec as P

F32 = jnp.float32
BF16 = jnp.bfloat16
HALF = 128
EXTRA = 16


def dot_nt(a, b, precision=None):
    dims = (((1,), (1,)), ((), ()))
    return lax.dot_general(a, b, dims, precision=precision, preferred_element_type=F32)


def dot_nn(a, b, precision=None):
    dims = (((1,), (0,)), ((), ()))
    return lax.dot_general(a, b, dims, precision=precision, preferred_element_type=F32)


HIGHEST = lax.Precision.HIGHEST


def inverse_factor(a):
    n = a.shape[0]
    blocks = n // 8
    full = (8, n)
    rows = [a[8 * i : 8 * i + 8, :] for i in range(blocks)]
    lane = lax.broadcasted_iota(jnp.int32, full, 1)
    sub = lax.broadcasted_iota(jnp.int32, full, 0)

    def column(x, k):
        return jnp.broadcast_to(x[:, k : k + 1], full)

    def row(x, k):
        return jnp.broadcast_to(x[k : k + 1, :], full)

    out = []
    own = [column(rows[0], k) for k in range(8)]
    for t in range(blocks):
        base = 8 * t
        here = jnp.logical_and(lane >= base, lane < base + 8)
        s = {(j, k): row(own[k], j) for j in range(8) for k in range(j, 8)}
        c = {}
        for i in range(t + 1, blocks):
            for j in range(8):
                c[i, j] = column(rows[i], base + j)
        last = t + 1 == blocks
        if not last:
            own = [column(rows[t + 1], base + 8 + k) for k in range(8)]
        for i in range(t + 1, blocks):
            rows[i] = jnp.where(here, 0.0, rows[i])
        b = [jnp.where(here, jnp.where(lane == base + j, 1.0, 0.0), row(rows[t], j)) for j in range(8)]
        d = [] if last else [c[t + 1, j] for j in range(8)]
        m = {}
        z = []
        x = jnp.zeros(full, F32)
        for j in range(8):
            r0 = pl.reciprocal(s[j, j], approx=True)
            e = 2.0 - s[j, j] * r0
            r = r0 * e
            for k in range(j + 1, 8):
                m[j, k] = s[j, k] * r
            for k in range(j + 1, 8):
                for l in range(k, 8):
                    if k == j + 1 and l == k:
                        s[k, l] = s[k, l] - ((s[j, k] * s[j, k]) * r0) * e
                    else:
                        s[k, l] = s[k, l] - m[j, k] * s[j, l]
                b[k] = b[k] - m[j, k] * b[j]
            z.append(r * b[j])
            if not last:
                for k in range(j + 1, 8):
                    d[k] = d[k] - m[j, k] * d[j]
                w = d[j] * r
                own = [own[k] - w * row(d[j], k) for k in range(8)]
                rows[t + 1] = rows[t + 1] - d[j] * z[j]
            x = jnp.where(sub == j, lax.rsqrt(s[j, j]) * b[j], x)
        out.append(jnp.where(lane < base + 8, x, 0.0))
        if t + 2 < blocks:
            y = list(z)
            for k in range(7, 0, -1):
                for j in range(k):
                    y[j] = y[j] - m[j, k] * y[k]
            for i in range(t + 2, blocks):
                for j in range(8):
                    rows[i] = rows[i] - c[i, j] * y[j]
    return jnp.concatenate(out, axis=0)


def split(x):
    high = x.astype(BF16)
    return high, (x - high.astype(F32)).astype(BF16)


def scale_row(ref, tile, n):
    tail = ref[n:, :].astype(F32)
    return tail[3 * tile : 3 * tile + 1] + tail[3 * tile + 1 : 3 * tile + 2] + tail[3 * tile + 2 : 3 * tile + 3]


def first_half(tile, inv_ref, low_ref, rest_ref):
    x = inverse_factor(tile[:HALF, :HALF])
    factor = dot_nt(tile[HALF:, :HALF], x, HIGHEST)
    inv_ref[...] = x
    low_ref[...] = factor
    rest_ref[...] = tile[HALF:, HALF:] - dot_nt(factor, factor, HIGHEST)


def second_half(inv_ref, low_ref, rest_ref, out_ref):
    x22 = inverse_factor(rest_ref[...])
    x11 = inv_ref[...]
    x21 = -dot_nn(x22, dot_nn(low_ref[...], x11, HIGHEST), HIGHEST)
    for k, x in enumerate((x11, x21, x22)):
        out_ref[k], out_ref[k + 3] = split(x)


def scale_tail(scales, n):
    row = lax.broadcasted_iota(jnp.int32, (EXTRA, n), 0)
    total = jnp.zeros((EXTRA, n), F32)
    for t in range(scales.shape[0]):
        rest = jnp.full((EXTRA, n), scales[t, 0], F32)
        for k in range(3):
            part = rest.astype(BF16).astype(F32)
            total = jnp.where(row == 3 * t + k, part, total)
            rest = rest - part
    return total.astype(BF16)


def pack_kernel(scales, packed, message, pivot, sem):
    n = pivot.shape[1]
    tall = message.shape[0] - EXTRA
    tile_copy = pltpu.make_async_copy(packed.at[0:n, 0:n], pivot.at[0:n], sem.at[0])
    block_copy = pltpu.make_async_copy(packed.at[:, 0:n], message.at[0:tall], sem.at[1])
    tile_copy.start()
    block_copy.start()
    tail = scale_tail(scales, n)
    pivot[n:, :] = tail
    message[tall:, :] = tail
    tile_copy.wait()
    block_copy.wait()


def take(tiles, mask, target):
    for k, tile in enumerate(tiles):

        @pl.when(mask == 2 * k)
        def _(tile=tile):
            n = target.shape[0]
            target[...] = tile[:n, :].astype(F32) * scale_row(tile, 0, n)


def factor_kernel(*refs):
    tiles, out_ref, left, tile, inv, low, rest = refs[:-6], *refs[-6:]
    n = 2 * HALF
    r = lax.axis_index("prow")
    place = r - r % 2

    @pl.when(r % 2 != lax.axis_index("pcol") % 2)
    def _():
        take(tiles, place, tile)
        take(tiles, place ^ 2, left)
        first_half(tile, inv, low, rest)
        second_half(inv, low, rest, out_ref.at[0:6])
        take(tiles, place ^ 4, tile)
        high, part = split(left[...])
        cat = join(out_ref, 0)
        both = jnp.concatenate([cat[:, :n], cat[:, :n], cat[:, n:]], axis=1)
        panel = dot_nt(jnp.concatenate([high, part, high], axis=1), both).astype(BF16)
        for k in range(4):
            i, j = divmod(k, 2)
            out_ref[12 + k] = panel[i * HALF : (i + 1) * HALF, j * HALF : (j + 1) * HALF]
        tile[...] = tile[...] - dot_nt(panel, panel)
        first_half(tile, inv, low, rest)
        second_half(inv, low, rest, out_ref.at[6:12])


def join(x, base):
    zero = jnp.zeros((HALF, HALF), BF16)
    upper = jnp.concatenate([x[base], zero, x[base + 3], zero], axis=1)
    lower = jnp.concatenate([x[base + 1], x[base + 2], x[base + 4], x[base + 5]], axis=1)
    return jnp.concatenate([upper, lower], axis=0)


VMEM = pl.BlockSpec(memory_space=pltpu.VMEM)
SMEM = pl.BlockSpec(memory_space=pltpu.SMEM)
HBM = pl.BlockSpec(memory_space=pltpu.HBM)
BLOCK = jax.ShapeDtypeStruct((HALF, HALF), F32)
PARTS = jax.ShapeDtypeStruct((6, HALF, HALF), BF16)
FACTORS = jax.ShapeDtypeStruct((16, HALF, HALF), BF16)


def factor_call(kernel, name, outs, args, specs=None, scratch=(), work=1):
    return pl.pallas_call(
        kernel,
        out_shape=outs,
        in_specs=specs or [VMEM] * len(args),
        out_specs=(VMEM,) * len(outs),
        scratch_shapes=scratch,
        compiler_params=pltpu.CompilerParams(vmem_limit_bytes=24 << 20),
        cost_estimate=pl.CostEstimate(flops=work * 5_000_000_000, bytes_accessed=0, transcendentals=0),
        name=name,
    )(*args)


def update_kernel(geometry, scales, packed, factors, factors_other, *rest):
    ratio, nr, nc, tpr, tpc, n = geometry
    here, there, mine, relayed = rest[0:2], rest[2:4], rest[4], rest[5]
    out, stored, result, block, rowp, colp, rowl, xs, sem = rest[6:]
    r = lax.axis_index("prow")
    c = lax.axis_index("pcol")
    tall = tpr * n

    reads = [pltpu.make_async_copy(packed.at[t * n : (t + 1) * n], stored.at[t], sem.at[0, t]) for t in range(tpr)]
    writes = [pltpu.make_async_copy(result.at[t], out.at[t * n : (t + 1) * n], sem.at[1, t]) for t in range(tpr)]
    for copy in reads:
        copy.start()

    def when(condition, target, value):
        @pl.when(condition)
        def _():
            target[...] = value[...]

    same = (r % 2) == (c % 2)
    when(jnp.logical_not(same), xs, factors)
    when(same, xs, factors_other)
    cat0 = join(xs, 0).T
    cat1 = join(xs, 6).T
    cat1 = jnp.concatenate([cat1[:n], cat1[:n], cat1[n:]], axis=0)
    panel = jnp.concatenate(
        [jnp.concatenate([xs[12], xs[13]], axis=1), jnp.concatenate([xs[14], xs[15]], axis=1)], axis=0
    ).T

    def solve(each):
        for t in range(tpr):
            rows = slice(t * n, (t + 1) * n)
            a0 = block[0, rows, :]
            raw0 = dot_nn(jnp.concatenate([a0, a0], axis=1), cat0)
            p0 = (raw0 * scale_row(block[0], t, tall)).astype(BF16)
            s1 = scale_row(block[1], t, tall)
            left = block[1, rows, :].astype(F32) * s1 - dot_nn(p0, panel)
            high, low = split(left)
            f1 = dot_nn(jnp.concatenate([high, low, high], axis=1), cat1)
            each(t, raw0, f1, s1, p0, f1.astype(BF16))

    early = jnp.where(c < 2, 0, 1)
    swap = r // 4 if (nr, nc) == (8, 4) else 0
    for g in range(ratio):
        for slot in range(ratio):
            chosen = (swap ^ g) == slot
            for half, panel_index in enumerate((early, 1 - early)):
                when(jnp.logical_and(chosen, same), block.at[panel_index], here[slot].at[half])
                when(jnp.logical_and(chosen, jnp.logical_not(same)), block.at[panel_index], there[slot].at[half])

        def keep_column(t, raw0, f1, s1, p0, p1, g=g):
            colp[t * ratio + g, :n, :] = p0.T
            colp[t * ratio + g, n:, :] = p1.T

        solve(keep_column)

    late = jnp.logical_and(nc == 4, jnp.where(r % 2 == 1, c == 2, c == 3))
    when(late, block, relayed)
    when(jnp.logical_not(late), block, mine)

    def keep_row(t, raw0, f1, s1, p0, p1):
        rowp[t, :, :n] = p0
        rowp[t, :, n:] = p1

        @pl.when(c == 0)
        def _():
            rowl[t] = raw0

        @pl.when(c == 1)
        def _():
            rowl[t] = f1 / s1

    solve(keep_row)

    for t in range(tpr):
        reads[t].wait()
        true_row = t * nr + r
        for q in range(tpc):
            true_col = q * nc + c
            cols = slice(q * n, (q + 1) * n)

            @pl.when(true_row < true_col)
            def _():
                result[t, :, cols] = stored[t, :, cols]

            @pl.when(jnp.logical_and(true_row >= true_col, true_col >= 2))
            def _():
                change = dot_nn(rowp[t], colp[q])
                inverse = 1.0 / jnp.full((1, n), scales[t, q], F32)
                result[t, :, cols] = (stored[t, :, cols].astype(F32) - change * inverse).astype(BF16)

            if q * nc < 2:

                @pl.when(jnp.logical_and(true_row >= true_col, true_col < 2))
                def _():
                    row = lax.broadcasted_iota(jnp.int32, (n, n), 0)
                    col = lax.broadcasted_iota(jnp.int32, (n, n), 1)
                    keep = jnp.logical_or(row >= col, true_row != true_col)
                    result[t, :, cols] = jnp.where(keep, rowl[t], 0.0).astype(BF16)

        writes[t].start()
    for copy in writes:
        copy.wait()


def update(scales, packed, arrays, nr, nc, tpr, tpc, n):
    geometry = (nr // nc, nr, nc, tpr, tpc, n)
    tall = arrays[-1].shape[1]
    return pl.pallas_call(
        functools.partial(update_kernel, geometry),
        out_shape=jax.ShapeDtypeStruct(packed.shape, BF16),
        in_specs=[SMEM, HBM] + [VMEM] * len(arrays),
        out_specs=HBM,
        scratch_shapes=[
            pltpu.VMEM((tpr, n, tpc * n), BF16),
            pltpu.VMEM((tpr, n, tpc * n), BF16),
            pltpu.VMEM((2, tall, n), BF16),
            pltpu.VMEM((tpr, n, 2 * n), BF16),
            pltpu.VMEM((tpc, 2 * n, n), BF16),
            pltpu.VMEM((tpr, n, n), F32),
            pltpu.VMEM(FACTORS.shape, BF16),
            pltpu.SemaphoreType.DMA((2, tpr)),
        ],
        compiler_params=pltpu.CompilerParams(vmem_limit_bytes=40 << 20),
        cost_estimate=pl.CostEstimate(flops=4_000_000_000, bytes_accessed=8 << 20, transcendentals=0),
        name="update_tiles",
    )(scales, packed, *arrays)


def on_device(nr, nc, packed, tile_scales):
    tpr, tpc = tile_scales.shape
    n = packed.shape[0] // tpr
    r = lax.axis_index("prow")
    c = lax.axis_index("pcol")
    def choose(options, index):
        value = options[0]
        for k in range(1, len(options)):
            value = jnp.where(index == k, options[k], value)
        return value

    def send(x, pairs):
        table = [(a * nc + b, d * nc + e) for (a, b), (d, e) in pairs]
        return lax.ppermute(x, ("prow", "pcol"), table)

    message, pivot = pl.pallas_call(
        pack_kernel,
        out_shape=(jax.ShapeDtypeStruct((tpr * n + EXTRA, n), BF16), jax.ShapeDtypeStruct((n + EXTRA, n), BF16)),
        in_specs=[SMEM, HBM],
        out_specs=(VMEM,) * 2,
        scratch_shapes=[pltpu.SemaphoreType.DMA((2,))],
        compiler_params=pltpu.CompilerParams(vmem_limit_bytes=48 << 20),
        name="pack_panel",
    )(tile_scales, pltpu.with_memory_space_constraint(packed, pltpu.HBM))

    other = [(k + 1) % 2 for k in range(nc)]
    came = []
    for k in range(nc):
        came.append(send(pivot, [((0, 0), (other[k], k)), ((1, 0), (2 + other[k], k)), ((1, 1), (4 + other[k], k))]))
    tile = choose(came, c)
    tiles = [tile]
    for mask in range(2, nr, 2):
        tiles.append(send(tile, [((a + other[e], e), ((a + other[e]) ^ mask, e)) for a in (0, 2, 4) for e in range(nc)]))
    scratch = [pltpu.VMEM((n, n), F32)] * 2 + [pltpu.VMEM((HALF, HALF), F32)] * 3
    (factors,) = factor_call(factor_kernel, "factor_pivots", (FACTORS,), tuple(tiles), None, scratch, 0)

    u = r % nc
    if nc == 4:
        first = {0: [(1, 0), (0, 2)], 1: [(0, 1), (1, 3)], 2: [(1, 2), (0, 1)], 3: [(1, 3), (0, 1)]}
        second = {0: [(1, 2), (0, 1)], 1: [(0, 3), (1, 0)], 2: [(0, 2), (1, 0)], 3: [(0, 3), (1, 0)]}
        turns = [[((a, x), (a, y)) for a in range(nr) for x, y in t[a % 4]] for t in (first, second)]
        got = [send(message, turn) for turn in turns]
    else:
        got = [jnp.zeros_like(message)] * 2
        for panel in range(2):
            for k in range(nc):
                if k != panel:
                    came = send(message, [((a, panel), (a, k)) for a in range(nr)])
                    slot = panel if k == 0 else 1 - panel if k > 1 else 0
                    got[slot] = jnp.where(c == k, came, got[slot])
    factors, *got = lax.optimization_barrier((factors, *got))

    ratio = nr // nc

    parity = [(a, e) for a in range(nr) for e in range(nc) if a % 2 == e % 2]

    def spread(x):
        if (nr, nc) == (8, 4):
            got = send(x, [((e + 4 * g, e), ((e + 4 * g) ^ 2, e)) for e in range(nc) for g in range(2)])
            side = jnp.where(u == c, x, got)
            return [side, send(side, [((a, e), (a ^ 4, e)) for a, e in parity])]
        near = [x]
        for mask in range(2, nr, 2):
            pairs = [((e + nc * g, e), ((e + nc * g) ^ mask, e)) for e in range(nc) for g in range(ratio)]
            near.append(send(x, pairs))
        return [choose(near, (r ^ (c + nc * g)) // 2) for g in range(ratio)]

    early = spread(jnp.where(c == 0, message, got[0]))
    late = spread(jnp.where(c == 0, got[0], jnp.where(c == 1, message, got[1])))
    if nc == 4:
        swap = (u == 0) == (c >= 2)
        m0 = jnp.where(c == 0, message, jnp.where(swap, got[0], got[1]))
        m0 = jnp.where(c == 1, jnp.where(u == 0, got[1], got[0]), m0)
        m1 = jnp.where(c == 1, message, jnp.where(swap, got[1], got[0]))
        m1 = jnp.where(c == 0, jnp.where(u == 0, got[0], got[1]), m1)
        mine = jnp.stack([m0, m1])
        relayed = send(mine, [((a, 3), (a, 2)) if a % 2 else ((a, 2), (a, 3)) for a in range(nr)])
    else:
        m0 = jnp.where(c == 0, message, jnp.where(c == 1, got[0], got[1]))
        mine = jnp.stack([m0, jnp.where(c == 1, message, got[0])])
        relayed = mine

    cols = [jnp.stack([early[g], late[g]]) for g in range(ratio)]
    cols_other = [send(x, [((a, e), (a ^ 1, e)) for a, e in parity]) for x in cols]
    factors_other = send(factors, [((a ^ 1, e), (a, e)) for a, e in parity])
    packed = pltpu.with_memory_space_constraint(packed, pltpu.HBM)
    arrays = (factors, factors_other, *cols, *cols_other, mine, relayed)
    return update(tile_scales, packed, arrays, nr, nc, tpr, tpc, n)


def solution(mesh):
    nr = mesh.shape["prow"]
    nc = mesh.shape["pcol"]
    return jax.shard_map(
        functools.partial(on_device, nr, nc),
        mesh=mesh,
        in_specs=(P("prow", "pcol"), P("prow", "pcol")),
        out_specs=P("prow", "pcol"),
        check_vma=False,
    )
```

```python
import functools

import jax
import jax.numpy as jnp
import numpy as np
from jax import lax
from jax.experimental import pallas as pl
from jax.experimental.pallas import tpu as pltpu
from jax.sharding import PartitionSpec as P

F32 = jnp.float32
BF16 = jnp.bfloat16
HALF = 128
EXTRA = 16


def dot_nt(a, b, precision=None):
    dims = (((1,), (1,)), ((), ()))
    return lax.dot_general(a, b, dims, precision=precision, preferred_element_type=F32)


def dot_nn(a, b, precision=None):
    dims = (((1,), (0,)), ((), ()))
    return lax.dot_general(a, b, dims, precision=precision, preferred_element_type=F32)


HIGHEST = lax.Precision.HIGHEST


def inverse_factor(a):
    n = a.shape[0]
    blocks = n // 8
    full = (8, n)
    rows = [a[8 * i : 8 * i + 8, :] for i in range(blocks)]
    lane = lax.broadcasted_iota(jnp.int32, full, 1)
    sub = lax.broadcasted_iota(jnp.int32, full, 0)

    def column(x, k):
        return jnp.broadcast_to(x[:, k : k + 1], full)

    def row(x, k):
        return jnp.broadcast_to(x[k : k + 1, :], full)

    out = []
    own = [column(rows[0], k) for k in range(8)]
    for t in range(blocks):
        base = 8 * t
        here = jnp.logical_and(lane >= base, lane < base + 8)
        s = {(j, k): row(own[k], j) for j in range(8) for k in range(j, 8)}
        c = {}
        for i in range(t + 1, blocks):
            for j in range(8):
                c[i, j] = column(rows[i], base + j)
        last = t + 1 == blocks
        if not last:
            own = [column(rows[t + 1], base + 8 + k) for k in range(8)]
        for i in range(t + 1, blocks):
            rows[i] = jnp.where(here, 0.0, rows[i])
        b = [jnp.where(here, jnp.where(lane == base + j, 1.0, 0.0), row(rows[t], j)) for j in range(8)]
        d = [] if last else [c[t + 1, j] for j in range(8)]
        m = {}
        z = []
        x = jnp.zeros(full, F32)
        for j in range(8):
            r0 = pl.reciprocal(s[j, j], approx=True)
            e = 2.0 - s[j, j] * r0
            r = r0 * e
            for k in range(j + 1, 8):
                m[j, k] = s[j, k] * r
            for k in range(j + 1, 8):
                for l in range(k, 8):
                    if k == j + 1 and l == k:
                        s[k, l] = s[k, l] - ((s[j, k] * s[j, k]) * r0) * e
                    else:
                        s[k, l] = s[k, l] - m[j, k] * s[j, l]
                b[k] = b[k] - m[j, k] * b[j]
            z.append(r * b[j])
            if not last:
                for k in range(j + 1, 8):
                    d[k] = d[k] - m[j, k] * d[j]
                w = d[j] * r
                own = [own[k] - w * row(d[j], k) for k in range(8)]
                rows[t + 1] = rows[t + 1] - d[j] * z[j]
            x = jnp.where(sub == j, lax.rsqrt(s[j, j]) * b[j], x)
        out.append(jnp.where(lane < base + 8, x, 0.0))
        if t + 2 < blocks:
            y = list(z)
            for k in range(7, 0, -1):
                for j in range(k):
                    y[j] = y[j] - m[j, k] * y[k]
            for i in range(t + 2, blocks):
                for j in range(8):
                    rows[i] = rows[i] - c[i, j] * y[j]
    return jnp.concatenate(out, axis=0)


def split(x):
    high = x.astype(BF16)
    return high, (x - high.astype(F32)).astype(BF16)


def scale_row(ref, tile, n):
    tail = ref[n:, :].astype(F32)
    return tail[3 * tile : 3 * tile + 1] + tail[3 * tile + 1 : 3 * tile + 2] + tail[3 * tile + 2 : 3 * tile + 3]


def first_half(tile, inv_ref, low_ref, rest_ref):
    x = inverse_factor(tile[:HALF, :HALF])
    factor = dot_nt(tile[HALF:, :HALF], x, HIGHEST)
    inv_ref[...] = x
    low_ref[...] = factor
    rest_ref[...] = tile[HALF:, HALF:] - dot_nt(factor, factor, HIGHEST)


def second_half(inv_ref, low_ref, rest_ref, out_ref):
    x22 = inverse_factor(rest_ref[...])
    x11 = inv_ref[...]
    x21 = -dot_nn(x22, dot_nn(low_ref[...], x11, HIGHEST), HIGHEST)
    for k, x in enumerate((x11, x21, x22)):
        out_ref[k], out_ref[k + 3] = split(x)


def scale_tail(scales, n):
    row = lax.broadcasted_iota(jnp.int32, (EXTRA, n), 0)
    total = jnp.zeros((EXTRA, n), F32)
    for t in range(scales.shape[0]):
        rest = jnp.full((EXTRA, n), scales[t, 0], F32)
        for k in range(3):
            part = rest.astype(BF16).astype(F32)
            total = jnp.where(row == 3 * t + k, part, total)
            rest = rest - part
    return total.astype(BF16)


def pack_kernel(scales, packed, message, pivot, sem):
    n = pivot.shape[1]
    tall = message.shape[0] - EXTRA
    tile_copy = pltpu.make_async_copy(packed.at[0:n, 0:n], pivot.at[0:n], sem.at[0])
    block_copy = pltpu.make_async_copy(packed.at[:, 0:n], message.at[0:tall], sem.at[1])
    tile_copy.start()
    block_copy.start()
    tail = scale_tail(scales, n)
    pivot[n:, :] = tail
    message[tall:, :] = tail
    tile_copy.wait()
    block_copy.wait()


def take(tiles, mask, target):
    for k, tile in enumerate(tiles):

        @pl.when(mask == 2 * k)
        def _(tile=tile):
            n = target.shape[0]
            target[...] = tile[:n, :].astype(F32) * scale_row(tile, 0, n)


def factor_kernel(*refs):
    tiles, out_ref, left, tile, inv, low, rest = refs[:-6], *refs[-6:]
    n = 2 * HALF
    r = lax.axis_index("prow")
    place = r - r % 2

    @pl.when(r % 2 != lax.axis_index("pcol") % 2)
    def _():
        take(tiles, place, tile)
        take(tiles, place ^ 2, left)
        first_half(tile, inv, low, rest)
        second_half(inv, low, rest, out_ref.at[0:6])
        take(tiles, place ^ 4, tile)
        high, part = split(left[...])
        cat = join(out_ref, 0)
        both = jnp.concatenate([cat[:, :n], cat[:, :n], cat[:, n:]], axis=1)
        panel = dot_nt(jnp.concatenate([high, part, high], axis=1), both).astype(BF16)
        for k in range(4):
            i, j = divmod(k, 2)
            out_ref[12 + k] = panel[i * HALF : (i + 1) * HALF, j * HALF : (j + 1) * HALF]
        tile[...] = tile[...] - dot_nt(panel, panel)
        first_half(tile, inv, low, rest)
        second_half(inv, low, rest, out_ref.at[6:12])


def join(x, base):
    zero = jnp.zeros((HALF, HALF), BF16)
    upper = jnp.concatenate([x[base], zero, x[base + 3], zero], axis=1)
    lower = jnp.concatenate([x[base + 1], x[base + 2], x[base + 4], x[base + 5]], axis=1)
    return jnp.concatenate([upper, lower], axis=0)


VMEM = pl.BlockSpec(memory_space=pltpu.VMEM)
SMEM = pl.BlockSpec(memory_space=pltpu.SMEM)
HBM = pl.BlockSpec(memory_space=pltpu.HBM)
BLOCK = jax.ShapeDtypeStruct((HALF, HALF), F32)
PARTS = jax.ShapeDtypeStruct((6, HALF, HALF), BF16)
FACTORS = jax.ShapeDtypeStruct((16, HALF, HALF), BF16)


def factor_call(kernel, name, outs, args, specs=None, scratch=(), work=1):
    return pl.pallas_call(
        kernel,
        out_shape=outs,
        in_specs=specs or [VMEM] * len(args),
        out_specs=(VMEM,) * len(outs),
        scratch_shapes=scratch,
        compiler_params=pltpu.CompilerParams(vmem_limit_bytes=24 << 20),
        cost_estimate=pl.CostEstimate(flops=work * 5_000_000_000, bytes_accessed=0, transcendentals=0),
        name=name,
    )(*args)


def update_kernel(geometry, table, scales, packed, factors, factors_other, *rest):
    ratio, nr, nc, tpr, tpc, n, count = geometry
    here, there, blocks = rest[0:2], rest[2:4], rest[4 : 4 + count]
    out, stored, result, block, rowp, colp, rowl, xs, sem = rest[4 + count :]
    r = lax.axis_index("prow")
    c = lax.axis_index("pcol")
    tall = tpr * n

    reads = [pltpu.make_async_copy(packed.at[t * n : (t + 1) * n], stored.at[t], sem.at[0, t]) for t in range(tpr)]
    writes = [pltpu.make_async_copy(result.at[t], out.at[t * n : (t + 1) * n], sem.at[1, t]) for t in range(tpr)]
    for copy in reads:
        copy.start()

    def when(condition, target, value):
        @pl.when(condition)
        def _():
            target[...] = value[...]

    same = (r % 2) == (c % 2)
    when(jnp.logical_not(same), xs, factors)
    when(same, xs, factors_other)
    cat0 = join(xs, 0).T
    cat1 = join(xs, 6).T
    cat1 = jnp.concatenate([cat1[:n], cat1[:n], cat1[n:]], axis=0)
    panel = jnp.concatenate(
        [jnp.concatenate([xs[12], xs[13]], axis=1), jnp.concatenate([xs[14], xs[15]], axis=1)], axis=0
    ).T

    def solve(each):
        for t in range(tpr):
            rows = slice(t * n, (t + 1) * n)
            a0 = block[0, rows, :]
            raw0 = dot_nn(jnp.concatenate([a0, a0], axis=1), cat0)
            p0 = (raw0 * scale_row(block[0], t, tall)).astype(BF16)
            s1 = scale_row(block[1], t, tall)
            left = block[1, rows, :].astype(F32) * s1 - dot_nn(p0, panel)
            high, low = split(left)
            f1 = dot_nn(jnp.concatenate([high, low, high], axis=1), cat1)
            each(t, raw0, f1, s1, p0, f1.astype(BF16))

    early = jnp.where(c == 2, 1, 0) if nc == 4 else jnp.where(c < 2, 0, 1)
    swap = r // 4 if (nr, nc) == (8, 4) else 0
    for g in range(ratio):
        for slot in range(ratio):
            chosen = (swap ^ g) == slot
            for half, panel_index in enumerate((early, 1 - early)):
                when(jnp.logical_and(chosen, same), block.at[panel_index], here[slot].at[half])
                when(jnp.logical_and(chosen, jnp.logical_not(same)), block.at[panel_index], there[slot].at[half])

        def keep_column(t, raw0, f1, s1, p0, p1, g=g):
            colp[t * ratio + g, :n, :] = p0.T
            colp[t * ratio + g, n:, :] = p1.T

        solve(keep_column)

    for panel_index in range(2):
        index = table[2 * (r * nc + c) + panel_index]
        for k in range(count):
            when(index == k, block.at[panel_index], blocks[k])

    def keep_row(t, raw0, f1, s1, p0, p1):
        rowp[t, :, :n] = p0
        rowp[t, :, n:] = p1

        @pl.when(c == 0)
        def _():
            rowl[t] = raw0

        @pl.when(c == 1)
        def _():
            rowl[t] = f1 / s1

    solve(keep_row)

    for t in range(tpr):
        reads[t].wait()
        true_row = t * nr + r
        for q in range(tpc):
            true_col = q * nc + c
            cols = slice(q * n, (q + 1) * n)

            @pl.when(true_row < true_col)
            def _():
                result[t, :, cols] = stored[t, :, cols]

            @pl.when(jnp.logical_and(true_row >= true_col, true_col >= 2))
            def _():
                change = dot_nn(rowp[t], colp[q])
                inverse = 1.0 / jnp.full((1, n), scales[t, q], F32)
                result[t, :, cols] = (stored[t, :, cols].astype(F32) - change * inverse).astype(BF16)

            if q * nc < 2:

                @pl.when(jnp.logical_and(true_row >= true_col, true_col < 2))
                def _():
                    row = lax.broadcasted_iota(jnp.int32, (n, n), 0)
                    col = lax.broadcasted_iota(jnp.int32, (n, n), 1)
                    keep = jnp.logical_or(row >= col, true_row != true_col)
                    result[t, :, cols] = jnp.where(keep, rowl[t], 0.0).astype(BF16)

        writes[t].start()
    for copy in writes:
        copy.wait()


def update(table, scales, packed, arrays, blocks, nr, nc, tpr, tpc, n):
    geometry = (nr // nc, nr, nc, tpr, tpc, n, len(blocks))
    tall = blocks[0].shape[0]
    return pl.pallas_call(
        functools.partial(update_kernel, geometry),
        out_shape=jax.ShapeDtypeStruct(packed.shape, BF16),
        in_specs=[SMEM, SMEM, HBM] + [VMEM] * (len(arrays) + len(blocks)),
        out_specs=HBM,
        scratch_shapes=[
            pltpu.VMEM((tpr, n, tpc * n), BF16),
            pltpu.VMEM((tpr, n, tpc * n), BF16),
            pltpu.VMEM((2, tall, n), BF16),
            pltpu.VMEM((tpr, n, 2 * n), BF16),
            pltpu.VMEM((tpc, 2 * n, n), BF16),
            pltpu.VMEM((tpr, n, n), F32),
            pltpu.VMEM(FACTORS.shape, BF16),
            pltpu.SemaphoreType.DMA((2, tpr)),
        ],
        compiler_params=pltpu.CompilerParams(vmem_limit_bytes=40 << 20),
        cost_estimate=pl.CostEstimate(flops=4_000_000_000, bytes_accessed=8 << 20, transcendentals=0),
        name="update_tiles",
    )(table, scales, packed, *arrays, *blocks)


def on_device(nr, nc, packed, tile_scales):
    tpr, tpc = tile_scales.shape
    n = packed.shape[0] // tpr
    r = lax.axis_index("prow")
    c = lax.axis_index("pcol")
    def choose(options, index):
        value = options[0]
        for k in range(1, len(options)):
            value = jnp.where(index == k, options[k], value)
        return value

    def send(x, pairs):
        table = [(a * nc + b, d * nc + e) for (a, b), (d, e) in pairs]
        return lax.ppermute(x, ("prow", "pcol"), table)

    message, pivot = pl.pallas_call(
        pack_kernel,
        out_shape=(jax.ShapeDtypeStruct((tpr * n + EXTRA, n), BF16), jax.ShapeDtypeStruct((n + EXTRA, n), BF16)),
        in_specs=[SMEM, HBM],
        out_specs=(VMEM,) * 2,
        scratch_shapes=[pltpu.SemaphoreType.DMA((2,))],
        compiler_params=pltpu.CompilerParams(vmem_limit_bytes=48 << 20),
        name="pack_panel",
    )(tile_scales, pltpu.with_memory_space_constraint(packed, pltpu.HBM))

    other = [(k + 1) % 2 for k in range(nc)]
    came = []
    for k in range(nc):
        came.append(send(pivot, [((0, 0), (other[k], k)), ((1, 0), (2 + other[k], k)), ((1, 1), (4 + other[k], k))]))
    tile = choose(came, c)
    tiles = [tile]
    for mask in range(2, nr, 2):
        tiles.append(send(tile, [((a + other[e], e), ((a + other[e]) ^ mask, e)) for a in (0, 2, 4) for e in range(nc)]))
    scratch = [pltpu.VMEM((n, n), F32)] * 2 + [pltpu.VMEM((HALF, HALF), F32)] * 3
    (factors,) = factor_call(factor_kernel, "factor_pivots", (FACTORS,), tuple(tiles), None, scratch, 0)

    u = r % nc
    blocks = [message]
    holds = {(a, p, p): 0 for a in range(nr) for p in range(2)}

    def send_round(operand, moves):
        for a, b, d, k in moves:
            holds[a, d, next(p for p in range(2) if holds.get((a, b, p)) == k)] = len(blocks)
        blocks.append(send(operand, [((a, b), (a, d)) for a, b, d, _ in moves]))

    if nc == 4:
        first = {0: [(1, 0), (0, 2)], 1: [(0, 1), (1, 3)], 2: [(1, 2), (0, 1)], 3: [(0, 3), (1, 0)]}
        second = {0: [(1, 2), (0, 1)], 1: [(0, 3), (1, 0)], 2: [(0, 2), (1, 0)], 3: [(1, 3), (0, 1)]}
        light = ({0: [(1, 0)], 1: [(0, 1)]}, {0: [(0, 2), (1, 3)], 1: [(0, 3), (1, 2)]})
        for turn, alone in zip((first, second), light):
            send_round(message, [(a, *move, 0) for a in range(nr) for move in alone.get(a, turn[a % 4])])
    else:
        kept = [[], []]
        for k in range(nc):
            for panel in range(2):
                if k != panel:
                    kept[panel if k == 0 else 1 - panel if k > 1 else 0].append((k, panel))
        for slot in range(2):
            value = jnp.zeros_like(message)
            for k, panel in kept[slot]:
                came = send(message, [((a, panel), (a, k)) for a in range(nr)])
                value = jnp.where(c == k, came, value)
                for a in range(nr):
                    holds[a, k, panel] = slot + 1
            blocks.append(value)
    factors, blocks[0], blocks[1] = lax.optimization_barrier((factors, *blocks[:2]))

    ratio = nr // nc

    parity = [(a, e) for a in range(nr) for e in range(nc) if a % 2 == e % 2]

    def spread_start(x):
        if (nr, nc) == (8, 4):
            return [x, send(x, [((e + 4 * g, e), ((e + 4 * g) ^ 2, e)) for e in range(nc) for g in range(2)])]
        near = [x]
        for mask in range(2, nr, 2):
            pairs = [((e + nc * g, e), ((e + nc * g) ^ mask, e)) for e in range(nc) for g in range(ratio)]
            near.append(send(x, pairs))
        return near

    def spread_end(near):
        if (nr, nc) == (8, 4):
            side = jnp.where(u == c, *near)
            return [side, send(side, [((a, e), (a ^ 4, e)) for a, e in parity])]
        return [choose(near, (r ^ (c + nc * g)) // 2) for g in range(ratio)]

    near = spread_start(jnp.where(c == 0, blocks[0], blocks[1]))
    blocks[2], _ = lax.optimization_barrier((blocks[2], near[1]))
    early = spread_end(near)
    late = spread_end(spread_start(jnp.where(c == 0, blocks[1], jnp.where(c == 1, blocks[0], blocks[2]))))
    if nc == 4:
        moves = [(0, 0, 1, 0), (0, 2, 3, 2), (0, 3, 2, 2), (1, 1, 0, 0), (1, 2, 3, 2), (1, 3, 2, 2)]
        relays = [(a, 3, 2) if a % 2 else (a, 2, 3) for a in range(2, nr)]
        send_round(blocks[1], [(*move, 1) for move in relays])
        send_round(jnp.where(c < 2, blocks[0], blocks[2]), moves + [(*move, 2) for move in relays])

    cols = [jnp.stack([early[g], late[g]]) for g in range(ratio)]
    cols_other = [send(x, [((a, e), (a ^ 1, e)) for a, e in parity]) for x in cols]
    factors_other = send(factors, [((a ^ 1, e), (a, e)) for a, e in parity])
    packed = pltpu.with_memory_space_constraint(packed, pltpu.HBM)
    table = np.array([holds[a, b, p] for a in range(nr) for b in range(nc) for p in range(2)], np.int32)
    return update(table, tile_scales, packed, (factors, factors_other, *cols, *cols_other), blocks, nr, nc, tpr, tpc, n)


def solution(mesh):
    nr = mesh.shape["prow"]
    nc = mesh.shape["pcol"]
    return jax.shard_map(
        functools.partial(on_device, nr, nc),
        mesh=mesh,
        in_specs=(P("prow", "pcol"), P("prow", "pcol")),
        out_specs=P("prow", "pcol"),
        check_vma=False,
    )
```

```python
import functools

import jax
import jax.numpy as jnp
import numpy as np
from jax import lax
from jax.experimental import pallas as pl
from jax.experimental.pallas import tpu as pltpu
from jax.sharding import PartitionSpec as P

F32 = jnp.float32
BF16 = jnp.bfloat16
HALF = 128
EXTRA = 16


def dot_nt(a, b, precision=None):
    dims = (((1,), (1,)), ((), ()))
    return lax.dot_general(a, b, dims, precision=precision, preferred_element_type=F32)


def dot_nn(a, b, precision=None):
    dims = (((1,), (0,)), ((), ()))
    return lax.dot_general(a, b, dims, precision=precision, preferred_element_type=F32)


HIGHEST = lax.Precision.HIGHEST


def inverse_factor(a):
    n = a.shape[0]
    blocks = n // 8
    full = (8, n)
    rows = [a[8 * i : 8 * i + 8, :] for i in range(blocks)]
    lane = lax.broadcasted_iota(jnp.int32, full, 1)
    sub = lax.broadcasted_iota(jnp.int32, full, 0)

    def column(x, k):
        return jnp.broadcast_to(x[:, k : k + 1], full)

    def row(x, k):
        return jnp.broadcast_to(x[k : k + 1, :], full)

    out = []
    own = [column(rows[0], k) for k in range(8)]
    for t in range(blocks):
        base = 8 * t
        here = jnp.logical_and(lane >= base, lane < base + 8)
        s = {(j, k): row(own[k], j) for j in range(8) for k in range(j, 8)}
        c = {}
        for i in range(t + 1, blocks):
            for j in range(8):
                c[i, j] = column(rows[i], base + j)
        last = t + 1 == blocks
        if not last:
            own = [column(rows[t + 1], base + 8 + k) for k in range(8)]
        for i in range(t + 1, blocks):
            rows[i] = jnp.where(here, 0.0, rows[i])
        b = [jnp.where(here, jnp.where(lane == base + j, 1.0, 0.0), row(rows[t], j)) for j in range(8)]
        d = [] if last else [c[t + 1, j] for j in range(8)]
        m = {}
        z = []
        x = jnp.zeros(full, F32)
        for j in range(8):
            r0 = pl.reciprocal(s[j, j], approx=True)
            e = 2.0 - s[j, j] * r0
            r = r0 * e
            for k in range(j + 1, 8):
                m[j, k] = s[j, k] * r
            for k in range(j + 1, 8):
                for l in range(k, 8):
                    if k == j + 1 and l == k:
                        s[k, l] = s[k, l] - ((s[j, k] * s[j, k]) * r0) * e
                    else:
                        s[k, l] = s[k, l] - m[j, k] * s[j, l]
                b[k] = b[k] - m[j, k] * b[j]
            z.append(r * b[j])
            if not last:
                for k in range(j + 1, 8):
                    d[k] = d[k] - m[j, k] * d[j]
                w = d[j] * r
                own = [own[k] - w * row(d[j], k) for k in range(8)]
                rows[t + 1] = rows[t + 1] - d[j] * z[j]
            x = jnp.where(sub == j, lax.rsqrt(s[j, j]) * b[j], x)
        out.append(jnp.where(lane < base + 8, x, 0.0))
        if t + 2 < blocks:
            y = list(z)
            for k in range(7, 0, -1):
                for j in range(k):
                    y[j] = y[j] - m[j, k] * y[k]
            for i in range(t + 2, blocks):
                for j in range(8):
                    rows[i] = rows[i] - c[i, j] * y[j]
    return jnp.concatenate(out, axis=0)


def split(x):
    high = x.astype(BF16)
    return high, (x - high.astype(F32)).astype(BF16)


def scale_row(ref, tile, n):
    tail = ref[n:, :].astype(F32)
    return tail[3 * tile : 3 * tile + 1] + tail[3 * tile + 1 : 3 * tile + 2] + tail[3 * tile + 2 : 3 * tile + 3]


def first_half(tile, inv_ref, low_ref, rest_ref):
    x = inverse_factor(tile[:HALF, :HALF])
    factor = dot_nt(tile[HALF:, :HALF], x, HIGHEST)
    inv_ref[...] = x
    low_ref[...] = factor
    rest_ref[...] = tile[HALF:, HALF:] - dot_nt(factor, factor, HIGHEST)


def second_half(inv_ref, low_ref, rest_ref, out_ref):
    x22 = inverse_factor(rest_ref[...])
    x11 = inv_ref[...]
    x21 = -dot_nn(x22, dot_nn(low_ref[...], x11, HIGHEST), HIGHEST)
    for k, x in enumerate((x11, x21, x22)):
        out_ref[k], out_ref[k + 3] = split(x)


def scale_tail(scales, n):
    row = lax.broadcasted_iota(jnp.int32, (EXTRA, n), 0)
    total = jnp.zeros((EXTRA, n), F32)
    for t in range(scales.shape[0]):
        rest = jnp.full((EXTRA, n), scales[t, 0], F32)
        for k in range(3):
            part = rest.astype(BF16).astype(F32)
            total = jnp.where(row == 3 * t + k, part, total)
            rest = rest - part
    return total.astype(BF16)


def pack_kernel(scales, packed, message, pivot, sem):
    n = pivot.shape[1]
    tall = message.shape[0] - EXTRA
    tile_copy = pltpu.make_async_copy(packed.at[0:n, 0:n], pivot.at[0:n], sem.at[0])
    block_copy = pltpu.make_async_copy(packed.at[:, 0:n], message.at[0:tall], sem.at[1])
    tile_copy.start()
    block_copy.start()
    tail = scale_tail(scales, n)
    pivot[n:, :] = tail
    message[tall:, :] = tail
    tile_copy.wait()
    block_copy.wait()


def take(tiles, mask, target):
    for k, tile in enumerate(tiles):

        @pl.when(mask == 2 * k)
        def _(tile=tile):
            n = target.shape[0]
            target[...] = tile[:n, :].astype(F32) * scale_row(tile, 0, n)


def factor_kernel(*refs):
    tiles, out_ref, left, tile, inv, low, rest = refs[:-6], *refs[-6:]
    n = 2 * HALF
    r = lax.axis_index("prow")
    place = r - r % 2

    @pl.when(r % 2 != lax.axis_index("pcol") % 2)
    def _():
        take(tiles, place, tile)
        take(tiles, place ^ 2, left)
        first_half(tile, inv, low, rest)
        second_half(inv, low, rest, out_ref.at[0:6])
        take(tiles, place ^ 4, tile)
        high, part = split(left[...])
        cat = join(out_ref, 0)
        both = jnp.concatenate([cat[:, :n], cat[:, :n], cat[:, n:]], axis=1)
        panel = dot_nt(jnp.concatenate([high, part, high], axis=1), both).astype(BF16)
        for k in range(4):
            i, j = divmod(k, 2)
            out_ref[12 + k] = panel[i * HALF : (i + 1) * HALF, j * HALF : (j + 1) * HALF]
        tile[...] = tile[...] - dot_nt(panel, panel)
        first_half(tile, inv, low, rest)
        second_half(inv, low, rest, out_ref.at[6:12])


def join(x, base):
    zero = jnp.zeros((HALF, HALF), BF16)
    upper = jnp.concatenate([x[base], zero, x[base + 3], zero], axis=1)
    lower = jnp.concatenate([x[base + 1], x[base + 2], x[base + 4], x[base + 5]], axis=1)
    return jnp.concatenate([upper, lower], axis=0)


VMEM = pl.BlockSpec(memory_space=pltpu.VMEM)
SMEM = pl.BlockSpec(memory_space=pltpu.SMEM)
HBM = pl.BlockSpec(memory_space=pltpu.HBM)
BLOCK = jax.ShapeDtypeStruct((HALF, HALF), F32)
PARTS = jax.ShapeDtypeStruct((6, HALF, HALF), BF16)
FACTORS = jax.ShapeDtypeStruct((16, HALF, HALF), BF16)


def factor_call(kernel, name, outs, args, specs=None, scratch=(), work=1):
    return pl.pallas_call(
        kernel,
        out_shape=outs,
        in_specs=specs or [VMEM] * len(args),
        out_specs=(VMEM,) * len(outs),
        scratch_shapes=scratch,
        compiler_params=pltpu.CompilerParams(vmem_limit_bytes=24 << 20),
        cost_estimate=pl.CostEstimate(flops=work * 5_000_000_000, bytes_accessed=0, transcendentals=0),
        name=name,
    )(*args)


def update_kernel(geometry, table, scales, packed, factors, factors_other, *rest):
    ratio, nr, nc, tpr, tpc, n, count = geometry
    here, there, blocks = rest[0:2], rest[2:4], rest[4 : 4 + count]
    out, stored, result, block, rowp, colp, rowl, xs, sem = rest[4 + count :]
    r = lax.axis_index("prow")
    c = lax.axis_index("pcol")
    tall = tpr * n

    reads = [pltpu.make_async_copy(packed.at[t * n : (t + 1) * n], stored.at[t], sem.at[0, t]) for t in range(tpr)]
    writes = [pltpu.make_async_copy(result.at[t], out.at[t * n : (t + 1) * n], sem.at[1, t]) for t in range(tpr)]
    for copy in reads:
        copy.start()

    def when(condition, target, value):
        @pl.when(condition)
        def _():
            target[...] = value[...]

    same = (r % 2) == (c % 2)
    when(jnp.logical_not(same), xs, factors)
    when(same, xs, factors_other)
    cat0 = join(xs, 0).T
    cat1 = join(xs, 6).T
    cat1 = jnp.concatenate([cat1[:n], cat1[:n], cat1[n:]], axis=0)
    panel = jnp.concatenate(
        [jnp.concatenate([xs[12], xs[13]], axis=1), jnp.concatenate([xs[14], xs[15]], axis=1)], axis=0
    ).T

    def solve(each):
        for t in range(tpr):
            rows = slice(t * n, (t + 1) * n)
            a0 = block[0, rows, :]
            raw0 = dot_nn(jnp.concatenate([a0, a0], axis=1), cat0)
            p0 = (raw0 * scale_row(block[0], t, tall)).astype(BF16)
            s1 = scale_row(block[1], t, tall)
            left = block[1, rows, :].astype(F32) * s1 - dot_nn(p0, panel)
            high, low = split(left)
            f1 = dot_nn(jnp.concatenate([high, low, high], axis=1), cat1)
            each(t, raw0, f1, s1, p0, f1.astype(BF16))

    early = jnp.where(c == 2, 1, 0) if nc == 4 else jnp.where(c < 2, 0, 1)
    for g in range(ratio):
        for half, panel_index in enumerate((early, 1 - early)):
            when(same, block.at[panel_index], here[g].at[half])
            when(jnp.logical_not(same), block.at[panel_index], there[g].at[half])

        def keep_column(t, raw0, f1, s1, p0, p1, g=g):
            colp[t * ratio + g, :n, :] = p0.T
            colp[t * ratio + g, n:, :] = p1.T

        solve(keep_column)

    for panel_index in range(2):
        index = table[2 * (r * nc + c) + panel_index]
        for k in range(3):
            when(index == k, block.at[panel_index], blocks[k])
        if count > 3:
            when(index > 2, block.at[panel_index], blocks[3].at[panel_index])

    def keep_row(t, raw0, f1, s1, p0, p1):
        rowp[t, :, :n] = p0
        rowp[t, :, n:] = p1

        @pl.when(c == 0)
        def _():
            rowl[t] = raw0

        @pl.when(c == 1)
        def _():
            rowl[t] = f1 / s1

    solve(keep_row)

    for t in range(tpr):
        reads[t].wait()
        true_row = t * nr + r
        for q in range(tpc):
            true_col = q * nc + c
            cols = slice(q * n, (q + 1) * n)

            @pl.when(true_row < true_col)
            def _():
                result[t, :, cols] = stored[t, :, cols]

            @pl.when(jnp.logical_and(true_row >= true_col, true_col >= 2))
            def _():
                change = dot_nn(rowp[t], colp[q])
                inverse = 1.0 / jnp.full((1, n), scales[t, q], F32)
                result[t, :, cols] = (stored[t, :, cols].astype(F32) - change * inverse).astype(BF16)

            if q * nc < 2:

                @pl.when(jnp.logical_and(true_row >= true_col, true_col < 2))
                def _():
                    row = lax.broadcasted_iota(jnp.int32, (n, n), 0)
                    col = lax.broadcasted_iota(jnp.int32, (n, n), 1)
                    keep = jnp.logical_or(row >= col, true_row != true_col)
                    result[t, :, cols] = jnp.where(keep, rowl[t], 0.0).astype(BF16)

        writes[t].start()
    for copy in writes:
        copy.wait()


def update(table, scales, packed, arrays, blocks, nr, nc, tpr, tpc, n):
    geometry = (nr // nc, nr, nc, tpr, tpc, n, len(blocks))
    tall = blocks[0].shape[0]
    return pl.pallas_call(
        functools.partial(update_kernel, geometry),
        out_shape=jax.ShapeDtypeStruct(packed.shape, BF16),
        in_specs=[SMEM, SMEM, HBM] + [VMEM] * (len(arrays) + len(blocks)),
        out_specs=HBM,
        scratch_shapes=[
            pltpu.VMEM((tpr, n, tpc * n), BF16),
            pltpu.VMEM((tpr, n, tpc * n), BF16),
            pltpu.VMEM((2, tall, n), BF16),
            pltpu.VMEM((tpr, n, 2 * n), BF16),
            pltpu.VMEM((tpc, 2 * n, n), BF16),
            pltpu.VMEM((tpr, n, n), F32),
            pltpu.VMEM(FACTORS.shape, BF16),
            pltpu.SemaphoreType.DMA((2, tpr)),
        ],
        compiler_params=pltpu.CompilerParams(vmem_limit_bytes=40 << 20),
        cost_estimate=pl.CostEstimate(flops=4_000_000_000, bytes_accessed=8 << 20, transcendentals=0),
        name="update_tiles",
    )(table, scales, packed, *arrays, *blocks)


def on_device(nr, nc, packed, tile_scales):
    tpr, tpc = tile_scales.shape
    n = packed.shape[0] // tpr
    r = lax.axis_index("prow")
    c = lax.axis_index("pcol")
    def choose(options, index):
        value = options[0]
        for k in range(1, len(options)):
            value = jnp.where(index == k, options[k], value)
        return value

    def send(x, pairs):
        table = [(a * nc + b, d * nc + e) for (a, b), (d, e) in pairs]
        return lax.ppermute(x, ("prow", "pcol"), table)

    message, pivot = pl.pallas_call(
        pack_kernel,
        out_shape=(jax.ShapeDtypeStruct((tpr * n + EXTRA, n), BF16), jax.ShapeDtypeStruct((n + EXTRA, n), BF16)),
        in_specs=[SMEM, HBM],
        out_specs=(VMEM,) * 2,
        scratch_shapes=[pltpu.SemaphoreType.DMA((2,))],
        compiler_params=pltpu.CompilerParams(vmem_limit_bytes=48 << 20),
        name="pack_panel",
    )(tile_scales, pltpu.with_memory_space_constraint(packed, pltpu.HBM))

    other = [(k + 1) % 2 for k in range(nc)]
    came = []
    for k in range(nc):
        came.append(send(pivot, [((0, 0), (other[k], k)), ((1, 0), (2 + other[k], k)), ((1, 1), (4 + other[k], k))]))
    tile = choose(came, c)
    tiles = [tile]
    for mask in range(2, nr, 2):
        tiles.append(send(tile, [((a + other[e], e), ((a + other[e]) ^ mask, e)) for a in (0, 2, 4) for e in range(nc)]))
    scratch = [pltpu.VMEM((n, n), F32)] * 2 + [pltpu.VMEM((HALF, HALF), F32)] * 3
    (factors,) = factor_call(factor_kernel, "factor_pivots", (FACTORS,), tuple(tiles), None, scratch, 0)

    u = r % nc
    blocks = [message]
    holds = {(a, p, p): 0 for a in range(nr) for p in range(2)}

    def send_round(operand, moves):
        for a, b, d, k in moves:
            holds[a, d, next(p for p in range(2) if holds.get((a, b, p)) == k)] = len(blocks)
        blocks.append(send(operand, [((a, b), (a, d)) for a, b, d, _ in moves]))

    if nc == 4:
        first = {0: [(1, 0), (0, 2)], 1: [(0, 1), (1, 3)], 2: [(1, 2), (0, 1)], 3: [(0, 3), (1, 0)]}
        second = {0: [(1, 2), (0, 1)], 1: [(0, 3), (1, 0)], 2: [(0, 2), (1, 0)], 3: [(1, 3), (0, 1)]}
        for turn, row_zero in ((first, [(1, 2)]), (second, [(0, 2), (1, 0)])):
            send_round(message, [(a, *move, 0) for a in range(nr) for move in (turn[a % 4] if a else row_zero)])
    else:
        kept = [[], []]
        for k in range(nc):
            for panel in range(2):
                if k != panel:
                    kept[panel if k == 0 else 1 - panel if k > 1 else 0].append((k, panel))
        for slot in range(2):
            value = jnp.zeros_like(message)
            for k, panel in kept[slot]:
                came = send(message, [((a, panel), (a, k)) for a in range(nr)])
                value = jnp.where(c == k, came, value)
                for a in range(nr):
                    holds[a, k, panel] = slot + 1
            blocks.append(value)
    factors, blocks[0], blocks[1] = lax.optimization_barrier((factors, *blocks[:2]))

    ratio = nr // nc

    parity = [(a, e) for a in range(nr) for e in range(nc) if a % 2 == e % 2]

    def star(x):
        near = [x]
        for mask in range(2, nr, 2):
            pairs = [((e + nc * g, e), ((e + nc * g) ^ mask, e)) for e in range(nc) for g in range(ratio)]
            near.append(send(x, pairs))
        return near

    def ends(near):
        return [choose(near, (r ^ (c + nc * g)) // 2) for g in range(ratio)]

    early = star(jnp.where(c == 0, blocks[0], blocks[1]))
    blocks[2], _ = lax.optimization_barrier((blocks[2], early[1]))
    first_late = jnp.where(r == 0, blocks[2], blocks[1]) if nc == 4 else blocks[1]
    late = star(jnp.where(c == 0, first_late, jnp.where(c == 1, blocks[0], blocks[2])))
    early, late = ends(early), ends(late)

    if nc == 4:
        swap = (u == 0) | (u == 3)
        m0 = jnp.where(c == 0, message, jnp.where(swap & (r > 0), blocks[1], blocks[2]))
        m1 = jnp.where(swap & (r > 0), blocks[2], blocks[1])
        beside = [((a, 3), (a - 1, 2)) if a % 2 else ((a, 2), (a + 1, 3)) for a in range(nr)]
        relayed = send(jnp.stack([m0, m1]), beside + [((0, 0), (1, 1))])
        for a in range(nr):
            for p in range(2):
                holds[a, 2 if a % 2 else 3, p] = 3 + p
        holds[0, 1, 0] = 3

    cols = [jnp.stack([early[g], late[g]]) for g in range(ratio)]
    cols_other = [send(x, [((a, e), (a ^ 1, e)) for a, e in parity]) for x in cols]
    factors_other = send(factors, [((a ^ 1, e), (a, e)) for a, e in parity])
    if nc == 4:
        last = send(relayed, [((a, e), (a ^ 1, e)) for a, e in parity if e > 1 or (a, e) == (1, 1)])
        blocks += [last]
    packed = pltpu.with_memory_space_constraint(packed, pltpu.HBM)
    table = np.array([holds[a, b, p] for a in range(nr) for b in range(nc) for p in range(2)], np.int32)
    return update(table, tile_scales, packed, (factors, factors_other, *cols, *cols_other), blocks, nr, nc, tpr, tpc, n)


def solution(mesh):
    nr = mesh.shape["prow"]
    nc = mesh.shape["pcol"]
    return jax.shard_map(
        functools.partial(on_device, nr, nc),
        mesh=mesh,
        in_specs=(P("prow", "pcol"), P("prow", "pcol")),
        out_specs=P("prow", "pcol"),
        check_vma=False,
    )
```

```python
import functools

import jax
import jax.numpy as jnp
import numpy as np
from jax import lax
from jax.experimental import pallas as pl
from jax.experimental.pallas import tpu as pltpu
from jax.sharding import PartitionSpec as P

F32 = jnp.float32
BF16 = jnp.bfloat16
HALF = 128
EXTRA = 16


def dot_nt(a, b, precision=None):
    dims = (((1,), (1,)), ((), ()))
    return lax.dot_general(a, b, dims, precision=precision, preferred_element_type=F32)


def dot_nn(a, b, precision=None):
    dims = (((1,), (0,)), ((), ()))
    return lax.dot_general(a, b, dims, precision=precision, preferred_element_type=F32)


HIGHEST = lax.Precision.HIGHEST


def inverse_factor(a):
    n = a.shape[0]
    blocks = n // 8
    full = (8, n)
    rows = [a[8 * i : 8 * i + 8, :] for i in range(blocks)]
    lane = lax.broadcasted_iota(jnp.int32, full, 1)
    sub = lax.broadcasted_iota(jnp.int32, full, 0)

    def column(x, k):
        return jnp.broadcast_to(x[:, k : k + 1], full)

    def row(x, k):
        return jnp.broadcast_to(x[k : k + 1, :], full)

    out = []
    own = [column(rows[0], k) for k in range(8)]
    for t in range(blocks):
        base = 8 * t
        here = jnp.logical_and(lane >= base, lane < base + 8)
        s = {(j, k): row(own[k], j) for j in range(8) for k in range(j, 8)}
        c = {}
        for i in range(t + 1, blocks):
            for j in range(8):
                c[i, j] = column(rows[i], base + j)
        last = t + 1 == blocks
        if not last:
            own = [column(rows[t + 1], base + 8 + k) for k in range(8)]
        for i in range(t + 1, blocks):
            rows[i] = jnp.where(here, 0.0, rows[i])
        b = [jnp.where(here, jnp.where(lane == base + j, 1.0, 0.0), row(rows[t], j)) for j in range(8)]
        d = [] if last else [c[t + 1, j] for j in range(8)]
        m = {}
        z = []
        x = jnp.zeros(full, F32)
        for j in range(8):
            r0 = pl.reciprocal(s[j, j], approx=True)
            e = 2.0 - s[j, j] * r0
            r = r0 * e
            for k in range(j + 1, 8):
                m[j, k] = s[j, k] * r
            for k in range(j + 1, 8):
                for l in range(k, 8):
                    if k == j + 1 and l == k:
                        s[k, l] = s[k, l] - ((s[j, k] * s[j, k]) * r0) * e
                    else:
                        s[k, l] = s[k, l] - m[j, k] * s[j, l]
                b[k] = b[k] - m[j, k] * b[j]
            z.append(r * b[j])
            if not last:
                for k in range(j + 1, 8):
                    d[k] = d[k] - m[j, k] * d[j]
                w = d[j] * r
                own = [own[k] - w * row(d[j], k) for k in range(8)]
                rows[t + 1] = rows[t + 1] - d[j] * z[j]
            x = jnp.where(sub == j, lax.rsqrt(s[j, j]) * b[j], x)
        out.append(jnp.where(lane < base + 8, x, 0.0))
        if t + 2 < blocks:
            y = list(z)
            for k in range(7, 0, -1):
                for j in range(k):
                    y[j] = y[j] - m[j, k] * y[k]
            for i in range(t + 2, blocks):
                for j in range(8):
                    rows[i] = rows[i] - c[i, j] * y[j]
    return jnp.concatenate(out, axis=0)


def split(x):
    high = x.astype(BF16)
    return high, (x - high.astype(F32)).astype(BF16)


def scale_row(ref, tile, n):
    tail = ref[n:, :].astype(F32)
    return tail[3 * tile : 3 * tile + 1] + tail[3 * tile + 1 : 3 * tile + 2] + tail[3 * tile + 2 : 3 * tile + 3]


def first_half(tile, inv_ref, low_ref, rest_ref):
    x = inverse_factor(tile[:HALF, :HALF])
    factor = dot_nt(tile[HALF:, :HALF], x, HIGHEST)
    inv_ref[...] = x
    low_ref[...] = factor
    rest_ref[...] = tile[HALF:, HALF:] - dot_nt(factor, factor, HIGHEST)


def second_half(inv_ref, low_ref, rest_ref, out_ref):
    x22 = inverse_factor(rest_ref[...])
    x11 = inv_ref[...]
    x21 = -dot_nn(x22, dot_nn(low_ref[...], x11, HIGHEST), HIGHEST)
    for k, x in enumerate((x11, x21, x22)):
        out_ref[k], out_ref[k + 3] = split(x)


def scale_tail(scales, n):
    row = lax.broadcasted_iota(jnp.int32, (EXTRA, n), 0)
    total = jnp.zeros((EXTRA, n), F32)
    for t in range(scales.shape[0]):
        rest = jnp.full((EXTRA, n), scales[t, 0], F32)
        for k in range(3):
            part = rest.astype(BF16).astype(F32)
            total = jnp.where(row == 3 * t + k, part, total)
            rest = rest - part
    return total.astype(BF16)


def pack_kernel(scales, packed, message, pivot, sem):
    n = pivot.shape[1]
    tall = message.shape[0] - EXTRA
    tile_copy = pltpu.make_async_copy(packed.at[0:n, 0:n], pivot.at[0:n], sem.at[0])
    block_copy = pltpu.make_async_copy(packed.at[:, 0:n], message.at[0:tall], sem.at[1])
    tile_copy.start()
    block_copy.start()
    tail = scale_tail(scales, n)
    pivot[n:, :] = tail
    message[tall:, :] = tail
    tile_copy.wait()
    block_copy.wait()


def take(tiles, mask, target):
    for k, tile in enumerate(tiles):

        @pl.when(mask == 2 * k)
        def _(tile=tile):
            n = target.shape[0]
            target[...] = tile[:n, :].astype(F32) * scale_row(tile, 0, n)


def factor_kernel(*refs):
    tiles, out_ref, left, tile, inv, low, rest = refs[:-6], *refs[-6:]
    n = 2 * HALF
    r = lax.axis_index("prow")

    @pl.when(r % 2 == 0)
    def _():
        take(tiles, r, tile)
        take(tiles, r ^ 2, left)
        first_half(tile, inv, low, rest)
        second_half(inv, low, rest, out_ref.at[0:6])
        take(tiles, r ^ 4, tile)
        high, part = split(left[...])
        cat = join(out_ref, 0)
        both = jnp.concatenate([cat[:, :n], cat[:, :n], cat[:, n:]], axis=1)
        panel = dot_nt(jnp.concatenate([high, part, high], axis=1), both).astype(BF16)
        for k in range(4):
            i, j = divmod(k, 2)
            out_ref[12 + k] = panel[i * HALF : (i + 1) * HALF, j * HALF : (j + 1) * HALF]
        tile[...] = tile[...] - dot_nt(panel, panel)
        first_half(tile, inv, low, rest)
        second_half(inv, low, rest, out_ref.at[6:12])


def join(x, base):
    zero = jnp.zeros((HALF, HALF), BF16)
    upper = jnp.concatenate([x[base], zero, x[base + 3], zero], axis=1)
    lower = jnp.concatenate([x[base + 1], x[base + 2], x[base + 4], x[base + 5]], axis=1)
    return jnp.concatenate([upper, lower], axis=0)


VMEM = pl.BlockSpec(memory_space=pltpu.VMEM)
SMEM = pl.BlockSpec(memory_space=pltpu.SMEM)
HBM = pl.BlockSpec(memory_space=pltpu.HBM)
BLOCK = jax.ShapeDtypeStruct((HALF, HALF), F32)
PARTS = jax.ShapeDtypeStruct((6, HALF, HALF), BF16)
FACTORS = jax.ShapeDtypeStruct((16, HALF, HALF), BF16)


def factor_call(kernel, name, outs, args, specs=None, scratch=(), work=1):
    return pl.pallas_call(
        kernel,
        out_shape=outs,
        in_specs=specs or [VMEM] * len(args),
        out_specs=(VMEM,) * len(outs),
        scratch_shapes=scratch,
        compiler_params=pltpu.CompilerParams(vmem_limit_bytes=24 << 20),
        cost_estimate=pl.CostEstimate(flops=work * 5_000_000_000, bytes_accessed=1 << 20, transcendentals=0),
        name=name,
    )(*args)


def update_kernel(geometry, scales, packed, factors, factors_other, *rest):
    ratio, nr, nc, tpr, tpc, n = geometry
    here, there, mine, relayed = rest[0:2], rest[2:4], rest[4], rest[5]
    out, stored, result, block, rowp, colp, rowl, xs, sem = rest[6:]
    r = lax.axis_index("prow")
    c = lax.axis_index("pcol")
    tall = tpr * n

    reads = [pltpu.make_async_copy(packed.at[t * n : (t + 1) * n], stored.at[t], sem.at[0, t]) for t in range(tpr)]
    writes = [pltpu.make_async_copy(result.at[t], out.at[t * n : (t + 1) * n], sem.at[1, t]) for t in range(tpr)]
    for copy in reads:
        copy.start()

    def when(condition, target, value):
        @pl.when(condition)
        def _():
            target[...] = value[...]

    when(r % 2 == 0, xs, factors)
    when(r % 2 == 1, xs, factors_other)
    cat0 = join(xs, 0).T
    cat1 = join(xs, 6).T
    cat1 = jnp.concatenate([cat1[:n], cat1[:n], cat1[n:]], axis=0)
    panel = jnp.concatenate(
        [jnp.concatenate([xs[12], xs[13]], axis=1), jnp.concatenate([xs[14], xs[15]], axis=1)], axis=0
    ).T

    def solve(each):
        for t in range(tpr):
            rows = slice(t * n, (t + 1) * n)
            a0 = block[0, rows, :]
            raw0 = dot_nn(jnp.concatenate([a0, a0], axis=1), cat0)
            p0 = (raw0 * scale_row(block[0], t, tall)).astype(BF16)
            s1 = scale_row(block[1], t, tall)
            left = block[1, rows, :].astype(F32) * s1 - dot_nn(p0, panel)
            high, low = split(left)
            f1 = dot_nn(jnp.concatenate([high, low, high], axis=1), cat1)
            each(t, raw0, f1, s1, p0, f1.astype(BF16))

    same = (r % 2) == (c % 2)
    for g in range(ratio):
        when(same, block, here[g])
        when(jnp.logical_not(same), block, there[g])

        def keep_column(t, raw0, f1, s1, p0, p1, g=g):
            colp[t * ratio + g, :n, :] = p0.T
            colp[t * ratio + g, n:, :] = p1.T

        solve(keep_column)

    late = jnp.logical_and(nc == 4, jnp.where(r % 4 == 3, c == 2, c == 3))
    when(late, block, relayed)
    when(jnp.logical_not(late), block, mine)
    when(jnp.logical_and(nc == 4, jnp.logical_and(r == 0, c == 1)), block.at[0], relayed.at[0])

    def keep_row(t, raw0, f1, s1, p0, p1):
        rowp[t, :, :n] = p0
        rowp[t, :, n:] = p1

        @pl.when(c == 0)
        def _():
            rowl[t] = raw0

        @pl.when(c == 1)
        def _():
            rowl[t] = f1 / s1

    solve(keep_row)

    for t in range(tpr):
        reads[t].wait()
        true_row = t * nr + r
        for q in range(tpc):
            true_col = q * nc + c
            cols = slice(q * n, (q + 1) * n)

            @pl.when(true_row < true_col)
            def _():
                result[t, :, cols] = stored[t, :, cols]

            @pl.when(jnp.logical_and(true_row >= true_col, true_col >= 2))
            def _():
                change = dot_nn(rowp[t], colp[q])
                inverse = 1.0 / jnp.full((1, n), scales[t, q], F32)
                result[t, :, cols] = (stored[t, :, cols].astype(F32) - change * inverse).astype(BF16)

            if q * nc < 2:

                @pl.when(jnp.logical_and(true_row >= true_col, true_col < 2))
                def _():
                    row = lax.broadcasted_iota(jnp.int32, (n, n), 0)
                    col = lax.broadcasted_iota(jnp.int32, (n, n), 1)
                    keep = jnp.logical_or(row >= col, true_row != true_col)
                    result[t, :, cols] = jnp.where(keep, rowl[t], 0.0).astype(BF16)

        writes[t].start()
    for copy in writes:
        copy.wait()


def update(scales, packed, arrays, nr, nc, tpr, tpc, n):
    geometry = (nr // nc, nr, nc, tpr, tpc, n)
    tall = arrays[-1].shape[1]
    return pl.pallas_call(
        functools.partial(update_kernel, geometry),
        out_shape=jax.ShapeDtypeStruct(packed.shape, BF16),
        in_specs=[SMEM, HBM] + [VMEM] * len(arrays),
        out_specs=HBM,
        scratch_shapes=[
            pltpu.VMEM((tpr, n, tpc * n), BF16),
            pltpu.VMEM((tpr, n, tpc * n), BF16),
            pltpu.VMEM((2, tall, n), BF16),
            pltpu.VMEM((tpr, n, 2 * n), BF16),
            pltpu.VMEM((tpc, 2 * n, n), BF16),
            pltpu.VMEM((tpr, n, n), F32),
            pltpu.VMEM(FACTORS.shape, BF16),
            pltpu.SemaphoreType.DMA((2, tpr)),
        ],
        compiler_params=pltpu.CompilerParams(vmem_limit_bytes=40 << 20),
        cost_estimate=pl.CostEstimate(flops=4_000_000_000, bytes_accessed=8 << 20, transcendentals=0),
        name="update_tiles",
    )(scales, packed, *arrays)


def on_device(nr, nc, packed, tile_scales):
    tpr, tpc = tile_scales.shape
    n = packed.shape[0] // tpr
    r = lax.axis_index("prow")
    c = lax.axis_index("pcol")
    def send(x, pairs):
        table = [(a * nc + b, d * nc + e) for (a, b), (d, e) in pairs]
        return lax.ppermute(x, ("prow", "pcol"), table)

    message, pivot = pl.pallas_call(
        pack_kernel,
        out_shape=(jax.ShapeDtypeStruct((tpr * n + EXTRA, n), BF16), jax.ShapeDtypeStruct((n + EXTRA, n), BF16)),
        in_specs=[SMEM, HBM],
        out_specs=(VMEM,) * 2,
        scratch_shapes=[pltpu.SemaphoreType.DMA((2,))],
        compiler_params=pltpu.CompilerParams(vmem_limit_bytes=48 << 20),
        name="pack_panel",
    )(tile_scales, pltpu.with_memory_space_constraint(packed, pltpu.HBM))

    came = []
    for k in range(nc):
        pairs = [((1, 0), (2, k)), ((1, 1), (4, (k + 1) % nc))]
        came.append(send(pivot, pairs + [((0, 0), (0, k))] * (k > 0)))
    index = jnp.where(r == 4, (c + nc - 1) % nc, c)
    tile = jnp.where((r == 0) & (c == 0), pivot, came[0])
    for k in range(1, nc):
        tile = jnp.where(index == k, came[k], tile)
    tiles = [tile]
    for mask in range(2, nr, 2):
        tiles.append(send(tile, [((a, e), (a ^ mask, e)) for a in (0, 2, 4) for e in range(nc)]))
    u = r % nc
    if nc == 4:
        first = {0: [(1, 0), (0, 2)], 1: [(0, 1), (1, 2)], 2: [(1, 2), (0, 1)], 3: [(1, 3), (0, 1)]}
        second = {0: [(1, 2), (0, 1)], 1: [(0, 2), (1, 0)], 2: [(0, 2), (1, 0)], 3: [(0, 3), (1, 0)]}
        turns = [[((a, x), (a, y)) for a in range(nr) for x, y in t[a % 4]] for t in (first, second)]
        turns[1].remove(((0, 0), (0, 1)))
        got = [send(message, turn) for turn in turns]
        *tiles, got[0], got[1] = lax.optimization_barrier((*tiles, *got))
        swap = (u == 0) == (c >= 2)
        m0 = jnp.where(c == 0, message, jnp.where(swap, got[0], got[1]))
        m0 = jnp.where(c == 1, jnp.where(u == 0, got[1], got[0]), m0)
        m1 = jnp.where(c == 1, message, jnp.where(swap, got[1], got[0]))
        m1 = jnp.where(c == 0, jnp.where(u == 0, got[0], got[1]), m1)
        mine = jnp.stack([m0, m1])
        relays = [((a, 3), (a, 2)) if a % 4 == 3 else ((a, 2), (a, 3)) for a in range(nr)]
        relayed = send(mine, relays + [((0, 0), (0, 1))])
    else:
        m0 = message
        m1 = jnp.where(c == 1, message, 0)
        for k in range(1, nc):
            m0 = jnp.where(c == k, send(message, [((a, 0), (a, k)) for a in range(nr)]), m0)
        for k in range(nc):
            if k != 1:
                m1 = jnp.where(c == k, send(message, [((a, 1), (a, k)) for a in range(nr)]), m1)
        mine = jnp.stack([m0, m1])
        relayed = mine

    ratio = nr // nc
    near = []
    for mask in range(2, nr, 2):
        pairs = [((e + nc * g, e), ((e + nc * g) ^ mask, e)) for e in range(nc) for g in range(ratio)]
        near.append(send(mine, pairs))
    scratch = [pltpu.VMEM((n, n), F32)] * 2 + [pltpu.VMEM((HALF, HALF), F32)] * 3
    (factors,) = factor_call(factor_kernel, "factor_pivots", (FACTORS,), tuple(tiles), None, scratch, 4)
    factors_other = send(factors, [((a, e), (a + 1, e)) for a in range(0, nr, 2) for e in range(nc)])
    *near, _ = lax.optimization_barrier((*near, factors))
    cols = [mine] * ratio
    for k, got in enumerate(near):
        cols = [jnp.where((r ^ (c + nc * g)) // 2 == k + 1, got, cols[g]) for g in range(ratio)]
    pairs = [((a, e), (a ^ 1, e)) for a in range(nr) for e in range(nc) if a % 2 == e % 2]
    cols_other = [send(x, pairs) for x in cols]
    packed = pltpu.with_memory_space_constraint(packed, pltpu.HBM)
    arrays = (factors, factors_other, *cols, *cols_other, mine, relayed)
    return update(tile_scales, packed, arrays, nr, nc, tpr, tpc, n)


def solution(mesh):
    nr = mesh.shape["prow"]
    nc = mesh.shape["pcol"]
    return jax.shard_map(
        functools.partial(on_device, nr, nc),
        mesh=mesh,
        in_specs=(P("prow", "pcol"), P("prow", "pcol")),
        out_specs=P("prow", "pcol"),
        check_vma=False,
    )
```

```python
import functools

import jax
import jax.numpy as jnp
import numpy as np
from jax import lax
from jax.experimental import pallas as pl
from jax.experimental.pallas import tpu as pltpu
from jax.sharding import PartitionSpec as P

F32 = jnp.float32
BF16 = jnp.bfloat16
HALF = 128
EXTRA = 16


def dot_nt(a, b, precision=None):
    dims = (((1,), (1,)), ((), ()))
    return lax.dot_general(a, b, dims, precision=precision, preferred_element_type=F32)


def dot_nn(a, b, precision=None):
    dims = (((1,), (0,)), ((), ()))
    return lax.dot_general(a, b, dims, precision=precision, preferred_element_type=F32)


HIGHEST = lax.Precision.HIGHEST


def inverse_factor(a):
    n = a.shape[0]
    blocks = n // 8
    full = (8, n)
    rows = [a[8 * i : 8 * i + 8, :] for i in range(blocks)]
    lane = lax.broadcasted_iota(jnp.int32, full, 1)
    sub = lax.broadcasted_iota(jnp.int32, full, 0)

    def column(x, k):
        return jnp.broadcast_to(x[:, k : k + 1], full)

    def row(x, k):
        return jnp.broadcast_to(x[k : k + 1, :], full)

    out = []
    own = [column(rows[0], k) for k in range(8)]
    for t in range(blocks):
        base = 8 * t
        here = jnp.logical_and(lane >= base, lane < base + 8)
        s = {(j, k): row(own[k], j) for j in range(8) for k in range(j, 8)}
        c = {}
        for i in range(t + 1, blocks):
            for j in range(8):
                c[i, j] = column(rows[i], base + j)
        last = t + 1 == blocks
        if not last:
            own = [column(rows[t + 1], base + 8 + k) for k in range(8)]
        for i in range(t + 1, blocks):
            rows[i] = jnp.where(here, 0.0, rows[i])
        b = [jnp.where(here, jnp.where(lane == base + j, 1.0, 0.0), row(rows[t], j)) for j in range(8)]
        d = [] if last else [c[t + 1, j] for j in range(8)]
        m = {}
        z = []
        x = jnp.zeros(full, F32)
        for j in range(8):
            r0 = pl.reciprocal(s[j, j], approx=True)
            e = 2.0 - s[j, j] * r0
            r = r0 * e
            for k in range(j + 1, 8):
                m[j, k] = s[j, k] * r
            for k in range(j + 1, 8):
                for l in range(k, 8):
                    if k == j + 1 and l == k:
                        s[k, l] = s[k, l] - ((s[j, k] * s[j, k]) * r0) * e
                    else:
                        s[k, l] = s[k, l] - m[j, k] * s[j, l]
                b[k] = b[k] - m[j, k] * b[j]
            z.append(r * b[j])
            if not last:
                for k in range(j + 1, 8):
                    d[k] = d[k] - m[j, k] * d[j]
                w = d[j] * r
                own = [own[k] - w * row(d[j], k) for k in range(8)]
                rows[t + 1] = rows[t + 1] - d[j] * z[j]
            x = jnp.where(sub == j, lax.rsqrt(s[j, j]) * b[j], x)
        out.append(jnp.where(lane < base + 8, x, 0.0))
        if t + 2 < blocks:
            y = list(z)
            for k in range(7, 0, -1):
                for j in range(k):
                    y[j] = y[j] - m[j, k] * y[k]
            for i in range(t + 2, blocks):
                for j in range(8):
                    rows[i] = rows[i] - c[i, j] * y[j]
    return jnp.concatenate(out, axis=0)


def split(x):
    high = x.astype(BF16)
    return high, (x - high.astype(F32)).astype(BF16)


def scale_row(ref, tile, n):
    tail = ref[n:, :].astype(F32)
    return tail[3 * tile : 3 * tile + 1] + tail[3 * tile + 1 : 3 * tile + 2] + tail[3 * tile + 2 : 3 * tile + 3]


def first_half(tile, inv_ref, low_ref, rest_ref):
    x = inverse_factor(tile[:HALF, :HALF])
    factor = dot_nt(tile[HALF:, :HALF], x, HIGHEST)
    inv_ref[...] = x
    low_ref[...] = factor
    rest_ref[...] = tile[HALF:, HALF:] - dot_nt(factor, factor, HIGHEST)


def dot_parts(a, b):
    ah, al = split(a)
    bh, bl = split(b)
    return dot_nn(jnp.concatenate([ah, al, ah], axis=1), jnp.concatenate([bh, bh, bl], axis=0))


def second_half(inv_ref, low_ref, rest_ref, out_ref):
    x22 = inverse_factor(rest_ref[...])
    x11 = inv_ref[...]
    x21 = -dot_parts(x22, dot_parts(low_ref[...], x11))
    for k, x in enumerate((x11, x21, x22)):
        out_ref[k], out_ref[k + 3] = split(x)


def scale_tail(scales, n):
    row = lax.broadcasted_iota(jnp.int32, (EXTRA, n), 0)
    total = jnp.zeros((EXTRA, n), F32)
    for t in range(scales.shape[0]):
        rest = jnp.full((EXTRA, n), scales[t, 0], F32)
        for k in range(3):
            part = rest.astype(BF16).astype(F32)
            total = jnp.where(row == 3 * t + k, part, total)
            rest = rest - part
    return total.astype(BF16)


def pack_kernel(scales, packed, message, pivot, sem):
    n = pivot.shape[1]
    tall = message.shape[0] - EXTRA
    tile_copy = pltpu.make_async_copy(packed.at[0:n, 0:n], pivot.at[0:n], sem.at[0])
    block_copy = pltpu.make_async_copy(packed.at[:, 0:n], message.at[0:tall], sem.at[1])
    tile_copy.start()
    block_copy.start()
    tail = scale_tail(scales, n)
    pivot[n:, :] = tail
    message[tall:, :] = tail
    tile_copy.wait()
    block_copy.wait()


def take(tiles, mask, target):
    for k, tile in enumerate(tiles):

        @pl.when(mask == 2 * k)
        def _(tile=tile):
            n = target.shape[0]
            target[...] = tile[:n, :].astype(F32) * scale_row(tile, 0, n)


def factor_kernel(*refs):
    tiles, out_ref, left, tile, inv, low, rest = refs[:-6], *refs[-6:]
    n = 2 * HALF
    r = lax.axis_index("prow")

    @pl.when(r % 2 == 0)
    def _():
        take(tiles, r, tile)
        take(tiles, r ^ 2, left)
        first_half(tile, inv, low, rest)
        second_half(inv, low, rest, out_ref.at[0:6])
        take(tiles, r ^ 4, tile)
        high, part = split(left[...])
        cat = join(out_ref, 0)
        both = jnp.concatenate([cat[:, :n], cat[:, :n], cat[:, n:]], axis=1)
        panel = dot_nt(jnp.concatenate([high, part, high], axis=1), both).astype(BF16)
        for k in range(4):
            i, j = divmod(k, 2)
            out_ref[12 + k] = panel[i * HALF : (i + 1) * HALF, j * HALF : (j + 1) * HALF]
        tile[...] = tile[...] - dot_nt(panel, panel)
        first_half(tile, inv, low, rest)
        second_half(inv, low, rest, out_ref.at[6:12])


def join(x, base):
    zero = jnp.zeros((HALF, HALF), BF16)
    upper = jnp.concatenate([x[base], zero, x[base + 3], zero], axis=1)
    lower = jnp.concatenate([x[base + 1], x[base + 2], x[base + 4], x[base + 5]], axis=1)
    return jnp.concatenate([upper, lower], axis=0)


VMEM = pl.BlockSpec(memory_space=pltpu.VMEM)
SMEM = pl.BlockSpec(memory_space=pltpu.SMEM)
HBM = pl.BlockSpec(memory_space=pltpu.HBM)
BLOCK = jax.ShapeDtypeStruct((HALF, HALF), F32)
PARTS = jax.ShapeDtypeStruct((6, HALF, HALF), BF16)
FACTORS = jax.ShapeDtypeStruct((16, HALF, HALF), BF16)


def factor_call(kernel, name, outs, args, specs=None, scratch=(), work=1):
    return pl.pallas_call(
        kernel,
        out_shape=outs,
        in_specs=specs or [VMEM] * len(args),
        out_specs=(VMEM,) * len(outs),
        scratch_shapes=scratch,
        compiler_params=pltpu.CompilerParams(vmem_limit_bytes=24 << 20),
        cost_estimate=pl.CostEstimate(flops=work * 5_000_000_000, bytes_accessed=1 << 20, transcendentals=0),
        name=name,
    )(*args)


def update_kernel(geometry, scales, packed, factors, factors_other, *rest):
    ratio, nr, nc, tpr, tpc, n = geometry
    here, there, mine, relayed = rest[0:2], rest[2:4], rest[4], rest[5]
    out, stored, result, block, rowp, colp, rowl, xs, sem = rest[6:]
    r = lax.axis_index("prow")
    c = lax.axis_index("pcol")
    tall = tpr * n

    reads = [pltpu.make_async_copy(packed.at[t * n : (t + 1) * n], stored.at[t], sem.at[0, t]) for t in range(tpr)]
    writes = [pltpu.make_async_copy(result.at[t], out.at[t * n : (t + 1) * n], sem.at[1, t]) for t in range(tpr)]
    for copy in reads:
        copy.start()

    def when(condition, target, value):
        @pl.when(condition)
        def _():
            target[...] = value[...]

    when(r % 2 == 0, xs, factors)
    when(r % 2 == 1, xs, factors_other)
    cat0 = join(xs, 0).T
    cat1 = join(xs, 6).T
    cat1 = jnp.concatenate([cat1[:n], cat1[:n], cat1[n:]], axis=0)
    panel = jnp.concatenate(
        [jnp.concatenate([xs[12], xs[13]], axis=1), jnp.concatenate([xs[14], xs[15]], axis=1)], axis=0
    ).T

    def solve(each):
        for t in range(tpr):
            rows = slice(t * n, (t + 1) * n)
            a0 = block[0, rows, :]
            raw0 = dot_nn(jnp.concatenate([a0, a0], axis=1), cat0)
            p0 = (raw0 * scale_row(block[0], t, tall)).astype(BF16)
            s1 = scale_row(block[1], t, tall)
            left = block[1, rows, :].astype(F32) * s1 - dot_nn(p0, panel)
            high, low = split(left)
            f1 = dot_nn(jnp.concatenate([high, low, high], axis=1), cat1)
            each(t, raw0, f1, s1, p0, f1.astype(BF16))

    same = (r % 2) == (c % 2)
    for g in range(ratio):
        when(same, block, here[g])
        when(jnp.logical_not(same), block, there[g])

        def keep_column(t, raw0, f1, s1, p0, p1, g=g):
            colp[t * ratio + g, :n, :] = p0.T
            colp[t * ratio + g, n:, :] = p1.T

        solve(keep_column)

    late = jnp.logical_and(nc == 4, jnp.where(r % 4 == 3, c == 2, c == 3))
    when(late, block, relayed)
    when(jnp.logical_not(late), block, mine)

    def keep_row(t, raw0, f1, s1, p0, p1):
        rowp[t, :, :n] = p0
        rowp[t, :, n:] = p1

        @pl.when(c == 0)
        def _():
            rowl[t] = raw0

        @pl.when(c == 1)
        def _():
            rowl[t] = f1 / s1

    solve(keep_row)

    for t in range(tpr):
        reads[t].wait()
        true_row = t * nr + r
        for q in range(tpc):
            true_col = q * nc + c
            cols = slice(q * n, (q + 1) * n)

            @pl.when(true_row < true_col)
            def _():
                result[t, :, cols] = stored[t, :, cols]

            @pl.when(jnp.logical_and(true_row >= true_col, true_col >= 2))
            def _():
                change = dot_nn(rowp[t], colp[q])
                inverse = 1.0 / jnp.full((1, n), scales[t, q], F32)
                result[t, :, cols] = (stored[t, :, cols].astype(F32) - change * inverse).astype(BF16)

            if q * nc < 2:

                @pl.when(jnp.logical_and(true_row >= true_col, true_col < 2))
                def _():
                    row = lax.broadcasted_iota(jnp.int32, (n, n), 0)
                    col = lax.broadcasted_iota(jnp.int32, (n, n), 1)
                    keep = jnp.logical_or(row >= col, true_row != true_col)
                    result[t, :, cols] = jnp.where(keep, rowl[t], 0.0).astype(BF16)

        writes[t].start()
    for copy in writes:
        copy.wait()


def update(scales, packed, arrays, nr, nc, tpr, tpc, n):
    geometry = (nr // nc, nr, nc, tpr, tpc, n)
    tall = arrays[-1].shape[1]
    return pl.pallas_call(
        functools.partial(update_kernel, geometry),
        out_shape=jax.ShapeDtypeStruct(packed.shape, BF16),
        in_specs=[SMEM, HBM] + [VMEM] * len(arrays),
        out_specs=HBM,
        scratch_shapes=[
            pltpu.VMEM((tpr, n, tpc * n), BF16),
            pltpu.VMEM((tpr, n, tpc * n), BF16),
            pltpu.VMEM((2, tall, n), BF16),
            pltpu.VMEM((tpr, n, 2 * n), BF16),
            pltpu.VMEM((tpc, 2 * n, n), BF16),
            pltpu.VMEM((tpr, n, n), F32),
            pltpu.VMEM(FACTORS.shape, BF16),
            pltpu.SemaphoreType.DMA((2, tpr)),
        ],
        compiler_params=pltpu.CompilerParams(vmem_limit_bytes=40 << 20),
        cost_estimate=pl.CostEstimate(flops=4_000_000_000, bytes_accessed=8 << 20, transcendentals=0),
        name="update_tiles",
    )(scales, packed, *arrays)


def on_device(nr, nc, packed, tile_scales):
    tpr, tpc = tile_scales.shape
    n = packed.shape[0] // tpr
    r = lax.axis_index("prow")
    c = lax.axis_index("pcol")
    def send(x, pairs):
        table = [(a * nc + b, d * nc + e) for (a, b), (d, e) in pairs]
        return lax.ppermute(x, ("prow", "pcol"), table)

    message, pivot = pl.pallas_call(
        pack_kernel,
        out_shape=(jax.ShapeDtypeStruct((tpr * n + EXTRA, n), BF16), jax.ShapeDtypeStruct((n + EXTRA, n), BF16)),
        in_specs=[SMEM, HBM],
        out_specs=(VMEM,) * 2,
        scratch_shapes=[pltpu.SemaphoreType.DMA((2,))],
        compiler_params=pltpu.CompilerParams(vmem_limit_bytes=48 << 20),
        name="pack_panel",
    )(pltpu.with_memory_space_constraint(tile_scales, pltpu.HBM), pltpu.with_memory_space_constraint(packed, pltpu.HBM))

    came = []
    for k in range(nc):
        pairs = [((1, 0), (2, k)), ((1, 1), (4, (k + 1) % nc))]
        came.append(send(pivot, pairs + [((0, 0), (0, k))] * (k > 0)))
    index = jnp.where(r == 4, (c + nc - 1) % nc, c)
    tile = jnp.where((r == 0) & (c == 0), pivot, came[0])
    for k in range(1, nc):
        tile = jnp.where(index == k, came[k], tile)
    tiles = [tile]
    for mask in range(2, nr, 2):
        tiles.append(send(tile, [((a, e), (a ^ mask, e)) for a in (0, 2, 4) for e in range(nc)]))
    u = r % nc
    if nc == 4:
        first = {0: [(1, 0), (0, 2)], 1: [(0, 1), (1, 2)], 2: [(1, 2), (0, 1)], 3: [(1, 3), (0, 1)]}
        second = {0: [(1, 2), (0, 1)], 1: [(0, 2), (1, 0)], 2: [(0, 2), (1, 0)], 3: [(0, 3), (1, 0)]}
        turns = [[((a, x), (a, y)) for a in range(nr) for x, y in t[a % 4]] for t in (first, second)]
        got = [send(message, turn) for turn in turns]
        *tiles, got[0], got[1] = lax.optimization_barrier((*tiles, *got))
        swap = (u == 0) == (c >= 2)
        m0 = jnp.where(c == 0, message, jnp.where(swap, got[0], got[1]))
        m0 = jnp.where(c == 1, jnp.where(u == 0, got[1], got[0]), m0)
        m1 = jnp.where(c == 1, message, jnp.where(swap, got[1], got[0]))
        m1 = jnp.where(c == 0, jnp.where(u == 0, got[0], got[1]), m1)
        mine = jnp.stack([m0, m1])
        relayed = send(mine, [((a, 3), (a, 2)) if a % 4 == 3 else ((a, 2), (a, 3)) for a in range(nr)])
    else:
        m0 = message
        m1 = jnp.where(c == 1, message, 0)
        for k in range(1, nc):
            m0 = jnp.where(c == k, send(message, [((a, 0), (a, k)) for a in range(nr)]), m0)
        for k in range(nc):
            if k != 1:
                m1 = jnp.where(c == k, send(message, [((a, 1), (a, k)) for a in range(nr)]), m1)
        mine = jnp.stack([m0, m1])
        relayed = mine

    ratio = nr // nc
    near = []
    for mask in range(2, nr, 2):
        pairs = [((e + nc * g, e), ((e + nc * g) ^ mask, e)) for e in range(nc) for g in range(ratio)]
        near.append(send(mine, pairs))
    scratch = [pltpu.VMEM((n, n), F32)] * 2 + [pltpu.VMEM((HALF, HALF), F32)] * 3
    (factors,) = factor_call(factor_kernel, "factor_pivots", (FACTORS,), tuple(tiles), None, scratch, 4)
    factors_other = send(factors, [((a, e), (a + 1, e)) for a in range(0, nr, 2) for e in range(nc)])
    *near, _ = lax.optimization_barrier((*near, factors))
    cols = [mine] * ratio
    for k, got in enumerate(near):
        cols = [jnp.where((r ^ (c + nc * g)) // 2 == k + 1, got, cols[g]) for g in range(ratio)]
    pairs = [((a, e), (a ^ 1, e)) for a in range(nr) for e in range(nc) if a % 2 == e % 2]
    cols_other = [send(x, pairs) for x in cols]
    packed = pltpu.with_memory_space_constraint(packed, pltpu.HBM)
    arrays = (factors, factors_other, *cols, *cols_other, mine, relayed)
    return update(tile_scales, packed, arrays, nr, nc, tpr, tpc, n)


def solution(mesh):
    nr = mesh.shape["prow"]
    nc = mesh.shape["pcol"]
    return jax.shard_map(
        functools.partial(on_device, nr, nc),
        mesh=mesh,
        in_specs=(P("prow", "pcol"), P("prow", "pcol")),
        out_specs=P("prow", "pcol"),
        check_vma=False,
    )
```
